128 devices in a mesh: segment: 8 (over x_lo, z), dp: 16 (over x_hi, y, core).
Axes of the slice: x: 4 (x_hi: 2, x_lo: 2; x = x_hi * 2 + x_lo), y: 4, z: 4, core: 2. Of those that a mesh axis runs over, the one named last changes fastest.
Arguments:
- control_in: bfloat16 [4096, 1536], P('dp'), may hold values from -10 to 10
- base_in: bfloat16 [4096, 2560], P('dp'), may hold values from -6 to 6
- base_update: bfloat16 [8, 4096, 2560], P('segment', 'dp'), may hold values from -4 to 4
- out_gain: float32 [2560], replicated, may hold values from 0.25 to 1.75
- cotangent: bfloat16 [4096, 2560], P('dp'), may hold values from -6 to 6
- w_qkv: bfloat16 [8, 1536, 2304], P('segment', 'dp'), may hold values from -1 to 1
- w_out: bfloat16 [8, 768, 1536], P('segment', 'dp'), may hold values from -0.21875 to 0.21875
- w_hint: bfloat16 [8, 1536, 2560], P('segment', 'dp'), may hold values from -0.15625 to 0.15625
- window_offset: int32 [8, 4], P('segment'), may hold values from -1 to 1
- tile_mask: int32 [8, 4, 4], P('segment'), may hold values 0 or 1
- token_layout: int32 [16, 256], P('dp'), may hold values from 0 to 255, each once within a row
Outputs:
- features: float32 [4096, 2560], P('dp')
- grad_qkv: float32 [8, 1536, 2304], P('segment', 'dp')
- grad_out: float32 [8, 768, 1536], P('segment', 'dp')
- grad_hint: float32 [8, 1536, 2560], P('segment', 'dp')
The draws below stay inside these ranges and needn't reach their ends.
All inputs are finite; a program needn't handle non-finite values. No bound on the sum of `tile_mask` on one device may be relied on, other than what follows from the above.
Results may differ from the reference program's by a relative error of at most 0.03.
Values may be sent and summed in bfloat16 or wider, within the bound.
A program may use at most 192 MiB of HBM per device.

```python
import jax
import jax.numpy as jnp
from jax import lax

D_CTRL = 1536
HEADS = 6
HEAD = 128
XW = 2560
TILE = 64
TILES = 4
CLIPS_DEV = 1
CLIP_ROWS = 256
CLIPS = 16
TOKENS = 4096
SECTIONS = 8
HD = 768
N_DP = 16


def draw_control_in(key, part):
    key = jax.random.fold_in(key, 11)
    noise_key = jax.random.fold_in(key, 0)
    noise = jnp.clip(jax.random.normal(noise_key, (TOKENS, D_CTRL), jnp.float32), -6.0, 6.0)
    return noise.astype(jnp.bfloat16)


def draw_w_qkv(key, part):
    key = jax.random.fold_in(key, 23)
    base_key = jax.random.fold_in(key, 0)
    weights = jnp.clip(jax.random.normal(base_key, (SECTIONS, D_CTRL, 3, HEADS, HEAD), jnp.float32), -4.0, 4.0) * D_CTRL ** (-0.5)
    return weights.reshape(SECTIONS, D_CTRL, 3 * HEADS * HEAD).astype(jnp.bfloat16)


def set_ends(values, own_key, smallest, top_value):
    place = [jax.random.randint(jax.random.fold_in(own_key, axis), (), 0, length) for axis, length in enumerate(values.shape)]
    widest = values.shape.index(max(values.shape))
    neighbour = place[:widest] + [(place[widest] + 1) % values.shape[widest]] + place[widest + 1:]
    return values.at[tuple(place)].set(smallest).at[tuple(neighbour)].set(top_value)


def level_of(own_key, dims, cuts, low, high):
    level = 1.0
    for dim, shards_of in cuts:
        draws = jax.random.uniform(jax.random.fold_in(jax.random.fold_in(own_key, 6), dim), (shards_of,), jnp.float32, low / len(cuts), high / len(cuts))
        level = level * jnp.repeat(jnp.exp(draws), dims[dim] // shards_of).reshape((-1,) + (1,) * (len(dims) - 1 - dim))
    return level


def scatter_about(key, extent, scale, bound, cuts=(), kind=jnp.bfloat16):
    factor_of = level_of(key, extent, cuts, -0.22, 0.18) if cuts else 1.0
    result = jax.random.normal(key, extent, jnp.float32) * scale * factor_of
    return jnp.minimum(jnp.maximum(result, -bound), bound).astype(kind)


def setup_inputs(seed: int = 0) -> dict:
    streams_of = jax.random.split(jax.random.key(seed), 12)
    control_in = draw_control_in(jax.random.fold_in(streams_of[11], 71), 0)
    base_in = scatter_about(streams_of[1], (TOKENS, XW), 1.0, 6.0, ((0, 16),))
    base_update = scatter_about(streams_of[2], (SECTIONS, TOKENS, XW), 0.5, 4.0, ((0, 8), (1, 16)))
    out_gain = jnp.clip(1.0 + 0.15 * jax.random.normal(streams_of[3], (XW,), jnp.float32), 0.25, 1.75)
    cotangent = scatter_about(streams_of[4], (TOKENS, XW), 1.0, 6.0, ((0, 16),))
    w_qkv = draw_w_qkv(jax.random.fold_in(streams_of[11], 71), 0)
    w_out = scatter_about(streams_of[6], (SECTIONS, HD, D_CTRL), HD ** -0.5, 0.21875, ((0, 8), (1, 16)))
    w_hint = scatter_about(streams_of[7], (SECTIONS, D_CTRL, XW), D_CTRL ** -0.5, 0.15625, ((0, 8), (1, 16)))
    window_offset = set_ends(jax.random.randint(streams_of[8], (SECTIONS, TILES), -1, 2), jax.random.fold_in(streams_of[8], 1), -1, 1).astype(jnp.int32)
    tile_mask = set_ends((jax.random.randint(streams_of[9], (SECTIONS, TILES, TILES), 0, 4) < 3).astype(jnp.int32), jax.random.fold_in(streams_of[9], 1), 0, 1)
    token_layout = jax.vmap(lambda own: jax.random.permutation(own, CLIP_ROWS))(jax.random.split(streams_of[10], CLIPS)).reshape((CLIPS, CLIP_ROWS)).astype(jnp.int32)
    return {"control_in": control_in, "base_in": base_in, "base_update": base_update, "out_gain": out_gain, "cotangent": cotangent, "w_qkv": w_qkv, "w_out": w_out, "w_hint": w_hint, "window_offset": window_offset, "tile_mask": tile_mask, "token_layout": token_layout}


def token_mask(offset, mask):
    count = mask.shape[0]
    row_tile = jnp.arange(count)[:, None]
    col_tile = jnp.arange(count)[None, :]
    near_window = jnp.abs(col_tile - row_tile - offset[:, None]) <= 1
    permitted = (row_tile == col_tile) | near_window & (mask == 1)
    return jnp.repeat(jnp.repeat(permitted, TILE, 0), TILE, 1)

def flat_positions(layout):
    count, length = layout.shape
    return (layout + (jnp.arange(count) * length)[:, None].astype(jnp.int32)).reshape(-1).astype(jnp.int32)

def forward_block(control, positions, permitted, weight_qkv, weight_out, weight_hint):
    total_rows = control.shape[0]
    length = permitted.shape[0]
    count = total_rows // length
    widened = control.astype(jnp.float32)
    inverse = lax.rsqrt(lax.optimization_barrier(jnp.mean(widened * widened, -1, keepdims=True)) + 1e-06)
    normed = (widened * inverse).astype(jnp.bfloat16)
    projected = jnp.dot(normed, weight_qkv, preferred_element_type=jnp.float32).astype(jnp.bfloat16)
    tiled_proj = projected[positions].reshape(count, length, 3, HEADS, HEAD)
    query_rows = tiled_proj[:, :, 0].astype(jnp.float32)
    key_rows = tiled_proj[:, :, 1].astype(jnp.float32)
    value_rows = tiled_proj[:, :, 2].astype(jnp.float32)
    scores = jnp.einsum('cqhe,ckhe->chqk', query_rows, key_rows) * HEAD ** (-0.5)
    scores = jnp.where(permitted, scores, -1e+30)
    row_max = lax.optimization_barrier(jnp.max(scores, -1, keepdims=True))
    shifted = jnp.exp(scores - row_max)
    softmax_out = shifted / lax.optimization_barrier(jnp.sum(shifted, -1, keepdims=True))
    soft_half = softmax_out.astype(jnp.bfloat16)
    attended = jnp.einsum('chqk,ckhe->cqhe', soft_half.astype(jnp.float32), value_rows).astype(jnp.bfloat16)
    attended = attended.reshape(total_rows, HEADS * HEAD)
    merged = jnp.zeros_like(attended).at[positions].set(attended)
    control_out = (widened + jnp.dot(merged, weight_out, preferred_element_type=jnp.float32)).astype(jnp.bfloat16)
    hint_term = jnp.dot(control_out, weight_hint, preferred_element_type=jnp.float32)
    return (control_out, hint_term, (control, normed, tiled_proj, softmax_out, merged))

def backward_block(saved, control_out, grad_next, grad_summed, positions, weight_qkv, weight_out, weight_hint):
    control, normed, tiled_proj, softmax_out, merged = saved
    total_rows = control.shape[0]
    count, length = (tiled_proj.shape[0], tiled_proj.shape[1])
    grad_after = (grad_next.astype(jnp.float32) + jnp.dot(grad_summed, weight_hint.T, preferred_element_type=jnp.float32)).astype(jnp.bfloat16)
    grad_hint = jnp.dot(control_out.T, grad_summed, preferred_element_type=jnp.float32)
    grad_out = jnp.dot(merged.T, grad_after, preferred_element_type=jnp.float32)
    grad_merged = jnp.dot(grad_after, weight_out.T, preferred_element_type=jnp.float32).astype(jnp.bfloat16)
    grad_tiled = grad_merged[positions].reshape(count, length, HEADS, HEAD).astype(jnp.float32)
    query_rows = tiled_proj[:, :, 0].astype(jnp.float32)
    key_rows = tiled_proj[:, :, 1].astype(jnp.float32)
    value_rows = tiled_proj[:, :, 2].astype(jnp.float32)
    soft_half = softmax_out.astype(jnp.bfloat16).astype(jnp.float32)
    grad_values = jnp.einsum('chqk,cqhe->ckhe', soft_half, grad_tiled).astype(jnp.bfloat16)
    grad_probs = jnp.einsum('cqhe,ckhe->chqk', grad_tiled, value_rows)
    grad_scores = softmax_out * (grad_probs - lax.optimization_barrier(jnp.sum(grad_probs * softmax_out, -1, keepdims=True))) * HEAD ** (-0.5)
    grad_scores = grad_scores.astype(jnp.bfloat16).astype(jnp.float32)
    grad_queries = jnp.einsum('chqk,ckhe->cqhe', grad_scores, key_rows).astype(jnp.bfloat16)
    grad_keys = jnp.einsum('chqk,cqhe->ckhe', grad_scores, query_rows).astype(jnp.bfloat16)
    grad_stack = jnp.stack((grad_queries, grad_keys, grad_values), 2).reshape(total_rows, 3 * HEADS * HEAD)
    grad_proj = jnp.zeros_like(grad_stack).at[positions].set(grad_stack)
    grad_qkv = jnp.dot(normed.T, grad_proj, preferred_element_type=jnp.float32)
    grad_normed = jnp.dot(grad_proj, weight_qkv.T, preferred_element_type=jnp.float32)
    widened = control.astype(jnp.float32)
    inverse = lax.rsqrt(lax.optimization_barrier(jnp.mean(widened * widened, -1, keepdims=True)) + 1e-06)
    through = inverse * grad_normed - widened * inverse ** 3 * lax.optimization_barrier(jnp.mean(grad_normed * widened, -1, keepdims=True))
    grad_control = (grad_after.astype(jnp.float32) + through).astype(jnp.bfloat16)
    return (grad_control, (grad_qkv, grad_out, grad_hint))

def norm_grad(summed, gain, cotangent):
    inverse = lax.rsqrt(lax.optimization_barrier(jnp.mean(summed * summed, -1, keepdims=True)) + 1e-06)
    features = summed * inverse * gain
    grad_normed = cotangent.astype(jnp.float32) * gain
    grad_summed = inverse * grad_normed - summed * inverse ** 3 * lax.optimization_barrier(jnp.mean(grad_normed * summed, -1, keepdims=True))
    return (features, grad_summed.astype(jnp.bfloat16))

def reference(control_in, base_in, base_update, out_gain, cotangent, w_qkv, w_out, w_hint, window_offset, tile_mask, token_layout):
    rows_group = CLIPS_DEV * TILES * TILE
    masks = [token_mask(window_offset[section], tile_mask[section]) for section in range(SECTIONS)]
    control_all = control_in.reshape(N_DP, rows_group, D_CTRL)
    base_all = base_in.reshape(N_DP, rows_group, XW)
    update_all = base_update.reshape(SECTIONS, N_DP, rows_group, XW).transpose(1, 0, 2, 3)
    cot_all = cotangent.reshape(N_DP, rows_group, XW)
    layout_all = token_layout.reshape(N_DP, CLIPS_DEV, TILES * TILE)

    def one_group(carry, pieces):
        control, base_rows, updates, cot_rows, layout = pieces
        positions = flat_positions(layout)
        running = jnp.zeros((rows_group, XW), jnp.float32)
        stored = []
        for section in range(SECTIONS):
            control_out, hint_term, saved = forward_block(control, positions, masks[section], w_qkv[section], w_out[section], w_hint[section])
            term = updates[section].astype(jnp.float32) + hint_term
            running = running + term
            stored.append((saved, control_out))
            control = control_out
        summed = base_rows.astype(jnp.float32) + running
        features, grad_summed = norm_grad(summed, out_gain, cot_rows)
        grad_next = jnp.zeros((rows_group, D_CTRL), jnp.bfloat16)
        parts = [None] * SECTIONS
        for section in reversed(range(SECTIONS)):
            saved, control_out = stored[section]
            grad_next, parts[section] = backward_block(saved, control_out, grad_next, grad_summed, positions, w_qkv[section], w_out[section], w_hint[section])
        added = tuple((carry[idx] + jnp.stack([parts[section][idx] for section in range(SECTIONS)]).astype(jnp.bfloat16).astype(jnp.float32) for idx in range(3)))
        return (added, features)
    start = (jnp.zeros(w_qkv.shape, jnp.float32), jnp.zeros(w_out.shape, jnp.float32), jnp.zeros(w_hint.shape, jnp.float32))
    totals, features = lax.scan(one_group, start, (control_all, base_all, update_all, cot_all, layout_all))
    factor = float(TOKENS) ** (-0.5)
    return (features.reshape(N_DP * rows_group, XW), totals[0] * factor, totals[1] * factor, totals[2] * factor)
```

```python
import functools

import jax
import jax.numpy as jnp
from jax import lax
from jax.experimental import pallas as pl
from jax.experimental.pallas import tpu as pltpu
from jax.sharding import PartitionSpec as P

HEADS = 6
HEAD = 128
TILE = 64
ROWS = 256
WIDTH = 1536
HD = HEADS * HEAD
QKV = 3 * HD
CW = 256
CH = WIDTH // CW
SCALE = HEAD ** (-0.5)
MESH = pl.DeviceIdType.MESH
VMEM_LIMIT = 56 * 1024 * 1024
F32 = jnp.float32
BF16 = jnp.bfloat16


def dot(a, b, dims=((1,), (0,))):
    return lax.dot_general(a, b, (dims, ((), ())), preferred_element_type=F32)


def chain_place():
    z = lax.axis_index("z")
    core = lax.axis_index("core")
    section = z + 4 * core
    later = lax.rem(section + 1, 8)
    earlier = lax.rem(section + 7, 8)
    return (
        section,
        {"z": lax.rem(later, 4), "core": later // 4},
        {"z": lax.rem(earlier, 4), "core": earlier // 4},
    )


def greet(*others):
    barrier = pltpu.get_barrier_semaphore()
    for other in others:
        pl.semaphore_signal(barrier, inc=1, device_id=other, device_id_type=MESH)
    pl.semaphore_wait(barrier, len(others))


def head_probs(proj, bias, head):
    lo = head * HEAD
    queries = proj[:, lo : lo + HEAD]
    keys = proj[:, HD + lo : HD + lo + HEAD]
    scores = dot(queries, keys, ((1,), (1,))) * SCALE + bias
    shifted = jnp.exp(scores - jnp.max(scores, -1, keepdims=True))
    return shifted / jnp.sum(shifted, -1, keepdims=True)


def forward_chain(
    start_ref, bias_ref, wqkv_ref, wout_ref,
    control_ref, after_ref, proj_ref, att_ref,
    landed, leaving, acc, send_sem, recv_sem,
):
    section, later, earlier = chain_place()
    greet(later, earlier)

    @pl.when(section == 0)
    def _():
        for k in range(CH):
            landed[k] = start_ref[k]

    def hop(k):
        return pltpu.make_async_remote_copy(
            src_ref=leaving.at[k],
            dst_ref=landed.at[k],
            send_sem=send_sem.at[k],
            recv_sem=recv_sem.at[k],
            device_id=later,
            device_id_type=MESH,
        )

    squares = jnp.zeros((ROWS, 1), F32)
    for k in range(CH):
        @pl.when(section > 0)
        def _():
            hop(k).wait_recv()

        x = landed[k]
        wide = x.astype(F32)
        squares += jnp.sum(wide * wide, -1, keepdims=True)
        for n in range(3):
            cols = slice(n * HD, (n + 1) * HD)
            part = dot(x, wqkv_ref[k * CW : (k + 1) * CW, cols])
            if k == 0:
                acc[:, cols] = part
            elif k < CH - 1:
                acc[:, cols] += part
            else:
                inverse = lax.rsqrt(squares * (1.0 / WIDTH) + 1e-06)
                proj_ref[:, cols] = ((acc[:, cols] + part) * inverse).astype(BF16)
    bias = bias_ref[...]
    for h in range(HEADS):
        probs = head_probs(proj_ref, bias, h).astype(BF16)
        lo = 2 * HD + h * HEAD
        att_ref[:, h * HEAD : (h + 1) * HEAD] = dot(probs, proj_ref[:, lo : lo + HEAD]).astype(BF16)
    att = att_ref[...]
    for k in range(CH):
        out = landed[k].astype(F32) + dot(att, wout_ref[:, k * CW : (k + 1) * CW])
        leaving[k] = out.astype(BF16)

        @pl.when(section < 7)
        def _():
            hop(k).start()

    control_ref[...] = landed[...]
    after_ref[...] = leaving[...]

    @pl.when(section < 7)
    def _():
        for k in range(CH):
            hop(k).wait_send()


def backward_chain(
    hint_ref, control_ref, proj_ref, bias_ref, wqkv_ref, wout_ref,
    after_ref, gproj_ref,
    landed, leaving, probs_ref, acc, send_sem, recv_sem,
):
    section, later, earlier = chain_place()
    greet(later, earlier)
    bias = bias_ref[...]
    for h in range(HEADS):
        probs_ref[h] = head_probs(proj_ref, bias, h)
    squares = jnp.zeros((ROWS, 1), F32)
    for k in range(CH):
        wide = control_ref[k].astype(F32)
        squares += jnp.sum(wide * wide, -1, keepdims=True)
    inverse = lax.rsqrt(squares * (1.0 / WIDTH) + 1e-06)

    def hop(k):
        return pltpu.make_async_remote_copy(
            src_ref=leaving.at[k],
            dst_ref=landed.at[k],
            send_sem=send_sem.at[k],
            recv_sem=recv_sem.at[k],
            device_id=earlier,
            device_id_type=MESH,
        )

    @pl.when(section == 7)
    def _():
        for k in range(CH):
            landed[k] = jnp.zeros((ROWS, CW), BF16)

    for k in range(CH):
        @pl.when(section < 7)
        def _():
            hop(k).wait_recv()

        grad = (landed[k].astype(F32) + hint_ref[k]).astype(BF16)
        after_ref[k] = grad
        part = dot(grad, wout_ref[:, k * CW : (k + 1) * CW], ((1,), (1,)))
        if k == 0:
            acc[...] = part
        else:
            acc[...] += part
    through = jnp.zeros((ROWS, 1), F32)
    for h in range(HEADS):
        lo = h * HEAD
        grad_att = acc[:, lo : lo + HEAD].astype(BF16)
        queries = proj_ref[:, lo : lo + HEAD]
        keys = proj_ref[:, HD + lo : HD + lo + HEAD]
        values = proj_ref[:, 2 * HD + lo : 2 * HD + lo + HEAD]
        probs = probs_ref[h]
        grad_probs = dot(grad_att, values, ((1,), (1,)))
        grad_values = dot(probs.astype(BF16), grad_att, ((0,), (0,))).astype(BF16)
        total = jnp.sum(grad_probs * probs, -1, keepdims=True)
        grad_scores = (probs * (grad_probs - total) * SCALE).astype(BF16)
        grad_queries = dot(grad_scores, keys).astype(BF16)
        grad_keys = dot(grad_scores, queries, ((0,), (0,))).astype(BF16)
        for n, (grad, value) in enumerate(
            ((grad_queries, queries), (grad_keys, keys), (grad_values, values))
        ):
            gproj_ref[:, n * HD + lo : n * HD + lo + HEAD] = grad
            through += jnp.sum(grad.astype(F32) * value.astype(F32), -1, keepdims=True)
    slope = inverse * inverse * through * (1.0 / WIDTH)
    grad_proj = gproj_ref[...]
    for k in range(CH):
        grad_normed = dot(grad_proj, wqkv_ref[k * CW : (k + 1) * CW, :], ((1,), (1,)))
        out = after_ref[k].astype(F32) + inverse * grad_normed - control_ref[k].astype(F32) * slope
        leaving[k] = out.astype(BF16)

        @pl.when(section > 0)
        def _():
            hop(k).start()

    @pl.when(section > 0)
    def _():
        for k in range(CH):
            hop(k).wait_send()


def vmem_call(kernel, out_shape, scratch, collective_id, flops):
    spec = pl.BlockSpec(memory_space=pltpu.VMEM)
    return lambda *args: pl.pallas_call(
        kernel,
        out_shape=out_shape,
        in_specs=[spec] * len(args),
        out_specs=[spec] * len(out_shape),
        scratch_shapes=scratch,
        compiler_params=pltpu.CompilerParams(
            collective_id=collective_id, has_side_effects=True, vmem_limit_bytes=VMEM_LIMIT
        ),
        cost_estimate=pl.CostEstimate(flops=flops, bytes_accessed=12_000_000, transcendentals=0),
    )(*args)


def chunked(value):
    return value.reshape(ROWS, CH, CW).transpose(1, 0, 2)


def flat(value):
    return value.transpose(1, 0, 2).reshape(ROWS, WIDTH)


def swap_roles(value):
    return lax.ppermute(value, ("xlo", "core"), [(0, 0), (1, 2), (2, 1), (3, 3)])


def of_clip(value):
    other = lax.ppermute(value, "core", [(0, 1), (1, 0)])
    return jnp.where(lax.axis_index("core") == lax.axis_index("xlo"), value, other)


def mask_bias(offset, mask, layout):
    row_tile = jnp.arange(4)[:, None]
    col_tile = jnp.arange(4)[None, :]
    near_window = jnp.abs(col_tile - row_tile - offset[:, None]) <= 1
    permitted = (row_tile == col_tile) | near_window & (mask == 1)
    holds = layout[None, :] == jnp.arange(ROWS)[:, None]
    tile_of = jnp.sum(jnp.where(holds, jnp.arange(ROWS)[None, :] // TILE, 0), 1)
    member = (tile_of[:, None] == jnp.arange(4)[None, :]).astype(BF16)
    allowed = dot(dot(member, permitted.astype(BF16)).astype(BF16), member, ((1,), (1,)))
    return jnp.where(allowed > 0.5, 0.0, -1e30)


def shards(
    control_in, base_in, base_update, out_gain, cotangent,
    w_qkv, w_out, w_hint, window_offset, tile_mask, token_layout,
):
    plane = ("xhi", "y", "xlo")
    small = jnp.concatenate([window_offset.reshape(-1), tile_mask.reshape(-1)])
    small = swap_roles(small)
    layout = of_clip(token_layout[0])
    bias = mask_bias(small[:4], small[4:].reshape(4, 4), layout)
    control = of_clip(control_in)
    base = of_clip(base_in)
    cot = of_clip(cotangent)
    update = swap_roles(base_update[0])
    weight_qkv = lax.all_gather(swap_roles(w_qkv[0]), plane, axis=0, tiled=True)
    weight_out = lax.all_gather(swap_roles(w_out[0]), plane, axis=0, tiled=True)
    weight_hint = lax.all_gather(swap_roles(w_hint[0]), plane, axis=0, tiled=True)

    chunk_shape = jax.ShapeDtypeStruct((CH, ROWS, CW), BF16)
    control_s, control_next, proj, att = vmem_call(
        forward_chain,
        [
            chunk_shape,
            chunk_shape,
            jax.ShapeDtypeStruct((ROWS, QKV), BF16),
            jax.ShapeDtypeStruct((ROWS, HD), BF16),
        ],
        [
            pltpu.VMEM((CH, ROWS, CW), BF16),
            pltpu.VMEM((CH, ROWS, CW), BF16),
            pltpu.VMEM((ROWS, QKV), F32),
            pltpu.SemaphoreType.DMA((CH,)),
            pltpu.SemaphoreType.DMA((CH,)),
        ],
        1,
        40_000_000_000,
    )(chunked(control), bias, weight_qkv, weight_out)

    after = flat(control_next)
    term = dot(after, weight_hint) + update.astype(F32)
    summed = base.astype(F32) + lax.psum(term.astype(BF16), ("z", "core")).astype(F32)

    inverse = lax.rsqrt(jnp.mean(summed * summed, -1, keepdims=True) + 1e-06)
    grad_normed = cot.astype(F32) * out_gain
    grad_summed = (
        inverse * grad_normed
        - summed * inverse**3 * jnp.mean(grad_normed * summed, -1, keepdims=True)
    ).astype(BF16)

    mine = swap_roles(summed.astype(BF16)).astype(F32)
    features = mine * lax.rsqrt(jnp.mean(mine * mine, -1, keepdims=True) + 1e-06) * out_gain

    hint_grad = dot(grad_summed, weight_hint, ((1,), (1,)))
    grad_hint = dot(after, grad_summed, ((0,), (0,))).astype(BF16)
    sum_hint = lax.psum_scatter(grad_hint, plane, scatter_dimension=0, tiled=True)

    grad_after, grad_proj = vmem_call(
        backward_chain,
        [chunk_shape, jax.ShapeDtypeStruct((ROWS, QKV), BF16)],
        [
            pltpu.VMEM((CH, ROWS, CW), BF16),
            pltpu.VMEM((CH, ROWS, CW), BF16),
            pltpu.VMEM((HEADS, ROWS, ROWS), F32),
            pltpu.VMEM((ROWS, HD), F32),
            pltpu.SemaphoreType.DMA((CH,)),
            pltpu.SemaphoreType.DMA((CH,)),
        ],
        2,
        40_000_000_000,
    )(chunked(hint_grad), control_s, proj, bias, weight_qkv, weight_out)

    wide = flat(control_s).astype(F32)
    normed = (wide * lax.rsqrt(jnp.mean(wide * wide, -1, keepdims=True) + 1e-06)).astype(BF16)
    grad_qkv = dot(normed, grad_proj, ((0,), (0,))).astype(BF16)
    grad_out = dot(att, flat(grad_after), ((0,), (0,))).astype(BF16)
    sum_qkv = lax.psum_scatter(grad_qkv, plane, scatter_dimension=0, tiled=True)
    sum_out = lax.psum_scatter(grad_out, plane, scatter_dimension=0, tiled=True)
    factor = 4096.0 ** (-0.5)
    return (
        features,
        (swap_roles(sum_qkv).astype(F32) * factor)[None],
        (swap_roles(sum_out).astype(F32) * factor)[None],
        (swap_roles(sum_hint).astype(F32) * factor)[None],
    )


def solution(mesh):
    parts = jax.sharding.Mesh(
        mesh.devices.reshape(2, 4, 2, 4, 2), ("xlo", "z", "xhi", "y", "core")
    )
    segment = ("xlo", "z")
    dp = ("xhi", "y", "core")
    by_rows = P(dp, None)
    by_both = P(segment, dp, None)
    placed = (
        by_rows, by_rows, by_both, P(), by_rows, by_both, by_both, by_both,
        P(segment, None), P(segment, None, None), by_rows,
    )
    return jax.shard_map(
        shards,
        mesh=parts,
        in_specs=placed,
        out_specs=(by_rows, by_both, by_both, by_both),
        check_vma=False,
    )
```

```python
import functools

import jax
import jax.numpy as jnp
from jax import lax
from jax.experimental import pallas as pl
from jax.experimental.pallas import tpu as pltpu
from jax.sharding import PartitionSpec as P

HEADS = 6
HEAD = 128
TILE = 64
ROWS = 256
WIDTH = 1536
FEAT = 2560
HD = HEADS * HEAD
QKV = 3 * HD
CW = 256
CH = WIDTH // CW
SCALE = HEAD ** (-0.5)
MESH = pl.DeviceIdType.MESH
VMEM_LIMIT = 60 * 1024 * 1024
F32 = jnp.float32
BF16 = jnp.bfloat16
QKV_CUT = (96, ((0, 640, 1152), (1152, 1792, 2304)))
OUT_CUT = (48, ((0, 384, 768), (768, 1152, 1536)))
HINT_CUT = (96, ((0, 640, 1280), (1280, 1920, 2560)))


def dot(a, b, dims=((1,), (0,))):
    return lax.dot_general(a, b, (dims, ((), ())), preferred_element_type=F32)


class Place:
    def __init__(self):
        self.xlo, self.z, self.xhi, self.y, self.core = (
            lax.axis_index(name) for name in ("xlo", "z", "xhi", "y", "core")
        )
        self.x = 2 * self.xhi + self.xlo
        self.section = self.z + 4 * self.core
        later = lax.rem(self.section + 1, 8)
        earlier = lax.rem(self.section + 7, 8)
        self.later = {"z": lax.rem(later, 4), "core": later // 4}
        self.earlier = {"z": lax.rem(earlier, 4), "core": earlier // 4}
        self.sibling = {"core": 1 - self.core}
        self.partner = {"xlo": 1 - self.xlo, "core": 1 - self.core}
        self.moved = self.xlo != self.core

    def along_x(self, by):
        x = lax.rem(self.x + by, 4)
        return {"xhi": x // 2, "xlo": lax.rem(x, 2)}

    def along_y(self, by):
        return {"y": lax.rem(self.y + by, 4)}

    def neighbour(self, half, ring, by):
        return self.along_y(by) if half == ring else self.along_x(by)

    def block(self, half, first, second):
        dx, dy = (second, first) if half == 0 else (first, second)
        x = lax.rem(self.x + dx, 4)
        y = lax.rem(self.y + dy, 4)
        return (x // 2) * 8 + y * 2 + lax.rem(x, 2)

    def greet(self):
        others = (
            self.later, self.earlier, self.sibling, self.partner,
            self.along_x(1), self.along_x(3), self.along_y(1), self.along_y(3),
        )
        barrier = pltpu.get_barrier_semaphore()
        for other in others:
            pl.semaphore_signal(barrier, inc=1, device_id=other, device_id_type=MESH)
        pl.semaphore_wait(barrier, len(others))


def remote(src, dst, send_sem, recv_sem, to):
    return pltpu.make_async_remote_copy(
        src_ref=src, dst_ref=dst, send_sem=send_sem, recv_sem=recv_sem,
        device_id=to, device_id_type=MESH,
    )


def rows_of(index, rows):
    return pl.ds(pl.multiple_of(index * rows, rows), rows)


class Gather:
    def __init__(self, place, shard, full, cut, send_sem, recv_sem, own_sem):
        self.place, self.shard, self.full = place, shard, full
        self.rows, self.cuts = cut
        self.send_sem, self.recv_sem, self.own_sem = send_sem, recv_sem, own_sem

    def region(self, half, first, second, part):
        lo, mid, hi = self.cuts[half]
        lo, hi = ((lo, hi), (lo, mid), (mid, hi))[part]
        index = self.place.block(half, first, second)
        return self.full.at[rows_of(index, self.rows), lo:hi]

    def copy(self, half, slot, first, second, part, ring=0, by=1):
        ref = self.region(half, first, second, part)
        return remote(
            ref, ref, self.send_sem.at[half, slot], self.recv_sem.at[half, slot],
            self.place.neighbour(half, ring, by),
        )

    def own(self, half):
        lo, _, hi = self.cuts[half]
        return self.shard.at[:, lo:hi], self.region(half, 0, 0, 0)

    def moved_own(self, half, index=None):
        src, dst = self.own(half)
        if index is not None:
            lo, _, hi = self.cuts[half]
            dst = self.full.at[rows_of(index, self.rows), lo:hi]
        return remote(
            src, dst, self.send_sem.at[half, 20], self.recv_sem.at[half, 20], self.place.partner
        )

    def kept_own(self, half):
        src, dst = self.own(half)
        return pltpu.make_async_copy(src, dst, self.own_sem.at[half])

    def sends(self, half):
        yield 0, (0, 0), 0, 0, 1
        yield 1, (0, 0), 0, 0, 3
        yield 2, (3, 0), 1, 0, 1
        yield 3, (1, 0), 2, 0, 3
        for j, first in enumerate((0, 3, 1, 2)):
            yield 4 + 4 * j, (first, 0), 0, 1, 1
            yield 5 + 4 * j, (first, 0), 0, 1, 3
            yield 6 + 4 * j, (first, 3), 1, 1, 1
            yield 7 + 4 * j, (first, 1), 2, 1, 3

    def send(self, half, *slots):
        plan = {entry[0]: entry for entry in self.sends(half)}
        for slot in slots:
            _, block, part, ring, by = plan[slot]
            self.copy(half, slot, *block, part, ring, by).start()

    def wait(self, half, *slots):
        plan = {0: (3, 0, 0), 1: (1, 0, 0), 2: (2, 0, 1), 3: (2, 0, 2)}
        for j, first in enumerate((0, 3, 1, 2)):
            plan |= {
                4 + 4 * j: (first, 3, 0), 5 + 4 * j: (first, 1, 0),
                6 + 4 * j: (first, 2, 1), 7 + 4 * j: (first, 2, 2),
            }
        for slot in slots:
            self.copy(half, slot, *plan[slot]).wait_recv()

    def start_own(self, half):
        place = self.place

        @pl.when(place.moved)
        def _():
            self.moved_own(half, place.xhi * 8 + place.y * 2 + 1 - place.xlo).start()

        @pl.when(jnp.logical_not(place.moved))
        def _():
            self.kept_own(half).start()

    def wait_own(self, half):
        @pl.when(self.place.moved)
        def _():
            self.moved_own(half).wait_recv()

        @pl.when(jnp.logical_not(self.place.moved))
        def _():
            self.kept_own(half).wait()

    def wait_sent(self):
        for half in range(2):
            for slot, block, part, ring, by in self.sends(half):
                self.copy(half, slot, *block, part, ring, by).wait_send()

            @pl.when(self.place.moved)
            def _():
                self.moved_own(half).wait_send()


def start_own(parts):
    for part in parts:
        for half in range(2):
            part.start_own(half)


def gather(parts):
    pairs = [(part, half) for part in parts for half in range(2)]
    for part, half in pairs:
        part.wait_own(half)
        part.send(half, 0, 1, 4, 5)
    for part, half in pairs:
        part.wait(half, 0)
        part.send(half, 2, 8, 9)
        part.wait(half, 1)
        part.send(half, 3, 12, 13)
    for part, half in pairs:
        part.wait(half, 4)
        part.send(half, 6)
        part.wait(half, 5)
        part.send(half, 7)
    for part, half in pairs:
        part.wait(half, 2, 3)
        part.send(half, 16, 17)
    for j in (1, 2, 3):
        for part, half in pairs:
            part.wait(half, 4 + 4 * j)
            part.send(half, 6 + 4 * j)
            part.wait(half, 5 + 4 * j)
            part.send(half, 7 + 4 * j)
    for part, half in pairs:
        for j in range(4):
            part.wait(half, 6 + 4 * j, 7 + 4 * j)


class Reduce:
    def __init__(self, place, grad, landing, total, result, cut, send_sem, recv_sem):
        self.place, self.grad, self.landing = place, grad, landing
        self.total, self.result = total, result
        self.rows, self.cuts = cut
        self.send_sem, self.recv_sem = send_sem, recv_sem

    def columns(self, half, part):
        lo, mid, hi = self.cuts[half]
        return ((lo, hi), (lo, mid), (mid, hi))[part]

    def region(self, half, first, second, part):
        lo, hi = self.columns(half, part)
        return self.grad.at[rows_of(self.place.block(half, first, second), self.rows), lo:hi]

    def slot_ref(self, half, slot, part):
        base = self.cuts[half][0]
        lo, hi = self.columns(half, part)
        return self.landing.at[half, slot, :, lo - base : hi - base]

    def copy(self, half, sem, first, second, part, slot, ring=0, by=1):
        return remote(
            self.region(half, first, second, part), self.slot_ref(half, slot, part),
            self.send_sem.at[half, sem], self.recv_sem.at[half, sem],
            self.place.neighbour(half, ring, by),
        )

    def plan(self):
        found = {}
        for i, second in enumerate((2, 3, 1, 0)):
            found[4 * i] = ((2, second), 1, i, 0, 1)
            found[4 * i + 1] = ((2, second), 2, i, 0, 3)
            found[4 * i + 2] = ((1, second), 0, 4 + i, 0, 1)
            found[4 * i + 3] = ((3, second), 0, 8 + i, 0, 3)
        found[16] = ((0, 2), 1, 12, 1, 1)
        found[17] = ((0, 2), 2, 12, 1, 3)
        found[18] = ((0, 1), 0, 13, 1, 1)
        found[19] = ((0, 3), 0, 14, 1, 3)
        return found

    def send(self, half, *sems):
        for sem in sems:
            block, part, slot, ring, by = self.plan()[sem]
            self.copy(half, sem, *block, part, slot, ring, by).start()

    def wait(self, half, *sems):
        for sem in sems:
            block, part, slot, ring, by = self.plan()[sem]
            self.copy(half, sem, *block, part, slot, ring, by).wait_recv()

    def wait_sent(self):
        for half in range(2):
            for sem, (block, part, slot, ring, by) in self.plan().items():
                self.copy(half, sem, *block, part, slot, ring, by).wait_send()

    def add(self, half, first, second, part, *slots):
        ref = self.region(half, first, second, part)
        value = ref[...].astype(F32)
        for slot in slots:
            value += self.slot_ref(half, slot, part)[...].astype(F32)
        ref[...] = value.astype(BF16)

    def finish(self, half):
        lo, hi = self.columns(half, 0)
        value = self.region(half, 0, 0, 0)[...].astype(F32)
        for slot in (13, 14):
            value += self.slot_ref(half, slot, 0)[...].astype(F32)
        self.total[:, lo:hi] = value.astype(BF16)

        @pl.when(self.place.moved)
        def _():
            self.moved(half).start()

    def moved(self, half):
        lo, hi = self.columns(half, 0)
        return remote(
            self.total.at[:, lo:hi], self.result.at[:, lo:hi],
            self.send_sem.at[half, 20], self.recv_sem.at[half, 20], self.place.partner,
        )

    def put(self, out_ref):
        @pl.when(self.place.moved)
        def _():
            for half in range(2):
                self.moved(half).wait()
            out_ref[...] = self.result[...]

        @pl.when(jnp.logical_not(self.place.moved))
        def _():
            out_ref[...] = self.total[...]


def reduce(parts):
    pairs = [(part, half) for part in parts for half in range(2)]
    for i in range(4):
        for part, half in pairs:
            part.send(half, 4 * i, 4 * i + 1)
    for i, second in enumerate((2, 3, 1, 0)):
        for part, half in pairs:
            part.wait(half, 4 * i)
            part.add(half, 1, second, 1, i)
            part.send(half, 4 * i + 2)
            part.wait(half, 4 * i + 1)
            part.add(half, 3, second, 2, i)
            part.send(half, 4 * i + 3)
    for i, second in enumerate((2, 3, 1, 0)):
        for part, half in pairs:
            part.wait(half, 4 * i + 2, 4 * i + 3)
            part.add(half, 0, second, 0, 4 + i, 8 + i)
            if i == 0:
                part.send(half, 16, 17)
            elif i == 1:
                part.wait(half, 17)
                part.add(half, 0, 3, 2, 12)
                part.send(half, 19)
            elif i == 2:
                part.wait(half, 16)
                part.add(half, 0, 1, 1, 12)
                part.send(half, 18)
    for part, half in pairs:
        part.wait(half, 18, 19)
        part.finish(half)


def head_probs(proj, bias, head):
    lo = head * HEAD
    queries = proj[:, lo : lo + HEAD]
    keys = proj[:, HD + lo : HD + lo + HEAD]
    scores = dot(queries, keys, ((1,), (1,))) * SCALE + bias
    shifted = jnp.exp(scores - jnp.max(scores, -1, keepdims=True))
    return shifted / jnp.sum(shifted, -1, keepdims=True)


def forward_kernel(
    start_ref, member_ref, permitted_ref, qkv_shard, out_shard, hint_shard,
    control_ref, after_ref, proj_ref, att_ref, bias_ref, term_ref, qkv_ref, out_ref, hint_ref,
    landed, leaving, acc, member, permitted, qkv, out, hint,
    hop_send, hop_recv, small_send, small_recv, start_sem, copy_sem,
    qkv_send, qkv_recv, qkv_own, out_send, out_recv, out_own, hint_send, hint_recv, hint_own,
    go_sem,
):
    place = Place()
    section, core = place.section, place.core
    kept = jnp.logical_not(place.moved)
    place.greet()

    def member_copy():
        return remote(member_ref, member, small_send.at[0], small_recv.at[0], place.sibling)

    def permitted_copy():
        return remote(permitted_ref, permitted, small_send.at[1], small_recv.at[1], place.partner)

    def start_copy(k):
        return pltpu.make_async_copy(
            start_ref.at[:, k * CW : (k + 1) * CW], landed.at[k], start_sem.at[k]
        )

    def start_across(k):
        return remote(
            start_ref.at[:, k * CW : (k + 1) * CW], landed.at[k],
            hop_send.at[k], hop_recv.at[k], place.sibling,
        )

    def hop(k):
        return remote(leaving.at[k], landed.at[k], hop_send.at[k], hop_recv.at[k], place.later)

    @pl.when(kept)
    def _():
        member_copy().start()
        member[...] = member_ref[...]
        permitted[...] = permitted_ref[...]

    @pl.when(place.moved)
    def _():
        permitted_copy().start()

    first_here = (section == 0) & kept
    first_given = (section == 4) & kept & (place.xlo == 1)

    @pl.when(first_here)
    def _():
        for k in range(CH):
            start_copy(k).start()

    @pl.when((place.z == 0) & (place.xlo == 1) & (core == 1))
    def _():
        for k in range(CH):
            start_across(k).start()

    qkv_gather = Gather(place, qkv_shard, qkv, QKV_CUT, qkv_send, qkv_recv, qkv_own)
    out_gather = Gather(place, out_shard, out, OUT_CUT, out_send, out_recv, out_own)
    hint_gather = Gather(place, hint_shard, hint, HINT_CUT, hint_send, hint_recv, hint_own)

    start_own([qkv_gather, out_gather])

    @pl.when(core == 1)
    def _():
        pl.semaphore_wait(go_sem, 1)

    gather([qkv_gather, out_gather])

    @pl.when(core == 0)
    def _():
        pl.semaphore_signal(go_sem, inc=1, device_id=place.sibling, device_id_type=MESH)

    start_own([hint_gather])
    keep_qkv = pltpu.make_async_copy(qkv, qkv_ref, copy_sem.at[0])
    keep_out = pltpu.make_async_copy(out, out_ref, copy_sem.at[1])
    keep_hint = pltpu.make_async_copy(hint, hint_ref, copy_sem.at[2])
    keep_qkv.start()
    keep_out.start()

    @pl.when(place.moved)
    def _():
        member_copy().wait_recv()
        permitted_copy().wait_recv()

    pairs = dot(dot(member[...], permitted[...]).astype(BF16), member[...], ((1,), (1,)))
    bias_ref[...] = jnp.where(pairs > 0.5, 0.0, -1e30)

    @pl.when(core == 1)
    def _():
        gather([hint_gather])

    squares = jnp.zeros((ROWS, 1), F32)
    for k in range(CH):
        @pl.when(first_here)
        def _():
            start_copy(k).wait()

        @pl.when(jnp.logical_not(first_here))
        def _():
            hop(k).wait_recv()

        x = landed[k]
        wide = x.astype(F32)
        squares += jnp.sum(wide * wide, -1, keepdims=True)
        for n in range(3):
            cols = slice(n * HD, (n + 1) * HD)
            part = dot(x, qkv[k * CW : (k + 1) * CW, cols])
            if k == 0:
                acc[:, cols] = part
            elif k < CH - 1:
                acc[:, cols] += part
            else:
                inverse = lax.rsqrt(squares * (1.0 / WIDTH) + 1e-06)
                proj_ref[:, cols] = ((acc[:, cols] + part) * inverse).astype(BF16)
    bias = bias_ref[...]
    for h in range(HEADS):
        probs = head_probs(proj_ref, bias, h).astype(BF16)
        lo = 2 * HD + h * HEAD
        att_ref[:, h * HEAD : (h + 1) * HEAD] = dot(probs, proj_ref[:, lo : lo + HEAD]).astype(BF16)
    att = att_ref[...]

    @pl.when(first_given)
    def _():
        for k in range(CH):
            start_across(k).wait_send()

    for k in range(CH):
        value = landed[k].astype(F32) + dot(att, out[:, k * CW : (k + 1) * CW])
        leaving[k] = value.astype(BF16)

        @pl.when(section < 7)
        def _():
            hop(k).start()

    control_ref[...] = landed[...]
    after_ref[...] = leaving[...]

    @pl.when(core == 0)
    def _():
        gather([hint_gather])

    keep_hint.start()
    for n in range(FEAT // 512):
        cols = slice(n * 512, (n + 1) * 512)
        value = dot(leaving[0], hint[0:CW, cols])
        for k in range(1, CH):
            value += dot(leaving[k], hint[k * CW : (k + 1) * CW, cols])
        term_ref[:, cols] = value

    @pl.when(kept)
    def _():
        member_copy().wait_send()

    @pl.when(place.moved)
    def _():
        permitted_copy().wait_send()

    @pl.when(section < 7)
    def _():
        for k in range(CH):
            hop(k).wait_send()

    qkv_gather.wait_sent()
    out_gather.wait_sent()
    hint_gather.wait_sent()
    keep_qkv.wait()
    keep_out.wait()
    keep_hint.wait()


def backward_kernel(
    hint_ref, control_ref, proj_ref, bias_ref, wqkv_ref, wout_ref, att_ref, next_ref, summed_ref,
    sum_qkv, sum_out, sum_hint,
    landed, leaving, probs_ref, acc, after, gproj,
    normed_t, att_t, next_t,
    grad_qkv, grad_out, grad_hint, land_qkv, land_out, land_hint,
    tot_qkv, tot_out, tot_hint, res_qkv, res_out, res_hint,
    hop_send, hop_recv,
    qkv_send, qkv_recv, out_send, out_recv, hint_send, hint_recv,
):
    place = Place()
    section, core = place.section, place.core
    place.greet()
    red_qkv = Reduce(place, grad_qkv, land_qkv, tot_qkv, res_qkv, QKV_CUT, qkv_send, qkv_recv)
    red_out = Reduce(place, grad_out, land_out, tot_out, res_out, OUT_CUT, out_send, out_recv)
    red_hint = Reduce(place, grad_hint, land_hint, tot_hint, res_hint, HINT_CUT, hint_send, hint_recv)

    bias = bias_ref[...]
    for h in range(HEADS):
        probs_ref[h] = head_probs(proj_ref, bias, h)
    squares = jnp.zeros((ROWS, 1), F32)
    for k in range(CH):
        wide = control_ref[k].astype(F32)
        squares += jnp.sum(wide * wide, -1, keepdims=True)
    inverse = lax.rsqrt(squares * (1.0 / WIDTH) + 1e-06)

    def hint_part():
        for k in range(CH):
            next_t[k * CW : (k + 1) * CW, :] = next_ref[k].T
        for m in range(CH):
            for n in range(FEAT // 512):
                cols = slice(n * 512, (n + 1) * 512)
                rows = slice(m * CW, (m + 1) * CW)
                grad_hint[rows, cols] = dot(next_t[rows, :], summed_ref[:, cols]).astype(BF16)
        reduce([red_hint])

    @pl.when(core == 0)
    def _():
        hint_part()

    for k in range(CH):
        normed = (control_ref[k].astype(F32) * inverse).astype(BF16)
        normed_t[k * CW : (k + 1) * CW, :] = normed.T
    for k in range(HD // CW):
        att_t[k * CW : (k + 1) * CW, :] = att_ref[:, k * CW : (k + 1) * CW].T

    def hop(k):
        return remote(leaving.at[k], landed.at[k], hop_send.at[k], hop_recv.at[k], place.earlier)

    @pl.when(section == 7)
    def _():
        for k in range(CH):
            landed[k] = jnp.zeros((ROWS, CW), BF16)

    for k in range(CH):
        @pl.when(section < 7)
        def _():
            hop(k).wait_recv()

        grad = (landed[k].astype(F32) + hint_ref[k]).astype(BF16)
        after[k] = grad
        part = dot(grad, wout_ref[:, k * CW : (k + 1) * CW], ((1,), (1,)))
        if k == 0:
            acc[...] = part
        else:
            acc[...] += part
    through = jnp.zeros((ROWS, 1), F32)
    for h in range(HEADS):
        lo = h * HEAD
        grad_att = acc[:, lo : lo + HEAD].astype(BF16)
        queries = proj_ref[:, lo : lo + HEAD]
        keys = proj_ref[:, HD + lo : HD + lo + HEAD]
        values = proj_ref[:, 2 * HD + lo : 2 * HD + lo + HEAD]
        probs = probs_ref[h]
        grad_probs = dot(grad_att, values, ((1,), (1,)))
        grad_values = dot(probs.astype(BF16), grad_att, ((0,), (0,))).astype(BF16)
        total = jnp.sum(grad_probs * probs, -1, keepdims=True)
        grad_scores = (probs * (grad_probs - total) * SCALE).astype(BF16)
        grad_queries = dot(grad_scores, keys).astype(BF16)
        grad_keys = dot(grad_scores, queries, ((0,), (0,))).astype(BF16)
        for n, (grad, value) in enumerate(
            ((grad_queries, queries), (grad_keys, keys), (grad_values, values))
        ):
            gproj[:, n * HD + lo : n * HD + lo + HEAD] = grad
            through += jnp.sum(grad.astype(F32) * value.astype(F32), -1, keepdims=True)
    slope = inverse * inverse * through * (1.0 / WIDTH)

    @pl.when(section > 0)
    def _():
        grad_proj = gproj[...]
        for k in range(CH):
            grad_normed = dot(grad_proj, wqkv_ref[k * CW : (k + 1) * CW, :], ((1,), (1,)))
            value = after[k].astype(F32) + inverse * grad_normed - control_ref[k].astype(F32) * slope
            leaving[k] = value.astype(BF16)
            hop(k).start()

    for m in range(CH):
        rows = slice(m * CW, (m + 1) * CW)
        for n in range(3):
            cols = slice(n * HD, (n + 1) * HD)
            grad_qkv[rows, cols] = dot(normed_t[rows, :], gproj[:, cols]).astype(BF16)
    for m in range(HD // CW):
        rows = slice(m * CW, (m + 1) * CW)
        for n in range(CH):
            grad_out[rows, n * CW : (n + 1) * CW] = dot(att_t[rows, :], after[n]).astype(BF16)
    reduce([red_qkv, red_out])

    @pl.when(core == 1)
    def _():
        hint_part()

    red_qkv.put(sum_qkv)
    red_out.put(sum_out)
    red_hint.put(sum_hint)

    @pl.when(section > 0)
    def _():
        for k in range(CH):
            hop(k).wait_send()

    red_qkv.wait_sent()
    red_out.wait_sent()
    red_hint.wait_sent()


def dma_sems(*shape):
    return pltpu.SemaphoreType.DMA(shape)


def kernel_call(kernel, ins, outs, scratch, collective_id, flops):
    spaces = {"v": pltpu.VMEM, "a": pl.ANY}
    return pl.pallas_call(
        kernel,
        out_shape=[shape for shape, _ in outs],
        in_specs=[pl.BlockSpec(memory_space=spaces[kind]) for kind in ins],
        out_specs=[pl.BlockSpec(memory_space=spaces[kind]) for _, kind in outs],
        scratch_shapes=scratch,
        compiler_params=pltpu.CompilerParams(
            collective_id=collective_id, has_side_effects=True, vmem_limit_bytes=VMEM_LIMIT
        ),
        cost_estimate=pl.CostEstimate(flops=flops, bytes_accessed=12_000_000, transcendentals=0),
    )


def chunked(value):
    return value.reshape(ROWS, CH, CW).transpose(1, 0, 2)


def flat(value):
    return value.transpose(1, 0, 2).reshape(ROWS, WIDTH)


def swap_roles(value):
    return lax.ppermute(value, ("xlo", "core"), [(0, 0), (1, 2), (2, 1), (3, 3)])


def of_clip(value):
    other = lax.ppermute(value, "core", [(0, 1), (1, 0)])
    return jnp.where(lax.axis_index("core") == lax.axis_index("xlo"), value, other)


def tile_members(layout):
    holds = layout[None, :] == jnp.arange(ROWS)[:, None]
    tile_of = jnp.sum(jnp.where(holds, jnp.arange(ROWS)[None, :] // TILE, 0), 1)
    return (tile_of[:, None] == jnp.arange(128)[None, :]).astype(BF16)


def permitted_tiles(offset, mask):
    row_tile = jnp.arange(4)[:, None]
    col_tile = jnp.arange(4)[None, :]
    near_window = jnp.abs(col_tile - row_tile - offset[:, None]) <= 1
    permitted = (row_tile == col_tile) | near_window & (mask == 1)
    return jnp.pad(permitted.astype(BF16), ((0, 124), (0, 124)))


def shape_of(*dims, dtype=BF16):
    return jax.ShapeDtypeStruct(dims, dtype)


def shards(
    control_in, base_in, base_update, out_gain, cotangent,
    w_qkv, w_out, w_hint, window_offset, tile_mask, token_layout,
):
    member = tile_members(token_layout[0])
    permitted = permitted_tiles(window_offset[0], tile_mask[0])
    chunks = (CH, ROWS, CW)

    control_s, control_next, proj, att, bias, term, weight_qkv, weight_out, weight_hint = kernel_call(
        forward_kernel,
        "avvaaa",
        [
            (shape_of(*chunks), "v"),
            (shape_of(*chunks), "v"),
            (shape_of(ROWS, QKV), "v"),
            (shape_of(ROWS, HD), "v"),
            (shape_of(ROWS, ROWS, dtype=F32), "v"),
            (shape_of(ROWS, FEAT, dtype=F32), "v"),
            (shape_of(WIDTH, QKV), "a"),
            (shape_of(HD, WIDTH), "a"),
            (shape_of(WIDTH, FEAT), "a"),
        ],
        [
            pltpu.VMEM(chunks, BF16),
            pltpu.VMEM(chunks, BF16),
            pltpu.VMEM((ROWS, QKV), F32),
            pltpu.VMEM((ROWS, 128), BF16),
            pltpu.VMEM((128, 128), BF16),
            pltpu.VMEM((WIDTH, QKV), BF16),
            pltpu.VMEM((HD, WIDTH), BF16),
            pltpu.VMEM((WIDTH, FEAT), BF16),
            dma_sems(CH), dma_sems(CH), dma_sems(2), dma_sems(2), dma_sems(CH), dma_sems(3),
            dma_sems(2, 21), dma_sems(2, 21), dma_sems(2),
            dma_sems(2, 21), dma_sems(2, 21), dma_sems(2),
            dma_sems(2, 21), dma_sems(2, 21), dma_sems(2),
            pltpu.SemaphoreType.REGULAR,
        ],
        1,
        100_000_000_000,
    )(control_in, member, permitted, w_qkv[0], w_out[0], w_hint[0])

    base = of_clip(base_in)
    cot = of_clip(cotangent)
    update = swap_roles(base_update[0])
    term = term + update.astype(F32)
    summed = base.astype(F32) + lax.psum(term.astype(BF16), ("z", "core")).astype(F32)

    inverse = lax.rsqrt(jnp.mean(summed * summed, -1, keepdims=True) + 1e-06)
    grad_normed = cot.astype(F32) * out_gain
    grad_summed = (
        inverse * grad_normed
        - summed * inverse**3 * jnp.mean(grad_normed * summed, -1, keepdims=True)
    ).astype(BF16)

    mine = swap_roles(summed.astype(BF16)).astype(F32)
    features = mine * lax.rsqrt(jnp.mean(mine * mine, -1, keepdims=True) + 1e-06) * out_gain

    hint_grad = dot(grad_summed, weight_hint, ((1,), (1,)))

    sum_qkv, sum_out, sum_hint = kernel_call(
        backward_kernel,
        "vvvvvvvvv",
        [
            (shape_of(96, QKV), "v"),
            (shape_of(48, WIDTH), "v"),
            (shape_of(96, FEAT), "v"),
        ],
        [
            pltpu.VMEM(chunks, BF16),
            pltpu.VMEM(chunks, BF16),
            pltpu.VMEM((HEADS, ROWS, ROWS), F32),
            pltpu.VMEM((ROWS, HD), F32),
            pltpu.VMEM(chunks, BF16),
            pltpu.VMEM((ROWS, QKV), BF16),
            pltpu.VMEM((WIDTH, ROWS), BF16),
            pltpu.VMEM((HD, ROWS), BF16),
            pltpu.VMEM((WIDTH, ROWS), BF16),
            pltpu.VMEM((WIDTH, QKV), BF16),
            pltpu.VMEM((HD, WIDTH), BF16),
            pltpu.VMEM((WIDTH, FEAT), BF16),
            pltpu.VMEM((2, 15, 96, QKV // 2), BF16),
            pltpu.VMEM((2, 15, 48, WIDTH // 2), BF16),
            pltpu.VMEM((2, 15, 96, FEAT // 2), BF16),
            pltpu.VMEM((96, QKV), BF16),
            pltpu.VMEM((48, WIDTH), BF16),
            pltpu.VMEM((96, FEAT), BF16),
            pltpu.VMEM((96, QKV), BF16),
            pltpu.VMEM((48, WIDTH), BF16),
            pltpu.VMEM((96, FEAT), BF16),
            dma_sems(CH), dma_sems(CH),
            dma_sems(2, 21), dma_sems(2, 21),
            dma_sems(2, 21), dma_sems(2, 21),
            dma_sems(2, 21), dma_sems(2, 21),
        ],
        2,
        100_000_000_000,
    )(
        chunked(hint_grad), control_s, proj, bias, weight_qkv, weight_out, att, control_next,
        grad_summed,
    )
    factor = 4096.0 ** (-0.5)
    return (
        features,
        (sum_qkv.astype(F32) * factor)[None],
        (sum_out.astype(F32) * factor)[None],
        (sum_hint.astype(F32) * factor)[None],
    )


def solution(mesh):
    parts = jax.sharding.Mesh(
        mesh.devices.reshape(2, 4, 2, 4, 2), ("xlo", "z", "xhi", "y", "core")
    )
    segment = ("xlo", "z")
    dp = ("xhi", "y", "core")
    by_rows = P(dp, None)
    by_both = P(segment, dp, None)
    placed = (
        by_rows, by_rows, by_both, P(), by_rows, by_both, by_both, by_both,
        P(segment, None), P(segment, None, None), by_rows,
    )
    return jax.shard_map(
        shards,
        mesh=parts,
        in_specs=placed,
        out_specs=(by_rows, by_both, by_both, by_both),
        check_vma=False,
    )
```

```python
import functools

import jax
import jax.numpy as jnp
from jax import lax
from jax.experimental import pallas as pl
from jax.experimental.pallas import tpu as pltpu
from jax.sharding import PartitionSpec as P

HEADS = 6
HEAD = 128
TILE = 64
ROWS = 256
WIDTH = 1536
FEAT = 2560
HD = HEADS * HEAD
QKV = 3 * HD
CW = 256
CH = WIDTH // CW
SCALE = HEAD ** (-0.5)
MESH = pl.DeviceIdType.MESH
VMEM_LIMIT = 60 * 1024 * 1024
F32 = jnp.float32
BF16 = jnp.bfloat16
QKV_CUT = (96, ((0, 640, 1152), (1152, 1792, 2304)))
OUT_CUT = (48, ((0, 384, 768), (768, 1152, 1536)))
HINT_CUT = (96, ((0, 640, 1280), (1280, 1920, 2560)))


def dot(a, b, dims=((1,), (0,))):
    return lax.dot_general(a, b, (dims, ((), ())), preferred_element_type=F32)


class Place:
    def __init__(self):
        self.xlo, self.z, self.xhi, self.y, self.core = (
            lax.axis_index(name) for name in ("xlo", "z", "xhi", "y", "core")
        )
        self.x = 2 * self.xhi + self.xlo
        self.section = self.z + 4 * self.core
        later = lax.rem(self.section + 1, 8)
        earlier = lax.rem(self.section + 7, 8)
        self.later = {"z": lax.rem(later, 4), "core": later // 4}
        self.earlier = {"z": lax.rem(earlier, 4), "core": earlier // 4}
        self.sibling = {"core": 1 - self.core}
        self.partner = {"xlo": 1 - self.xlo, "core": 1 - self.core}
        self.moved = self.xlo != self.core

    def along_x(self, by):
        x = lax.rem(self.x + by, 4)
        return {"xhi": x // 2, "xlo": lax.rem(x, 2)}

    def along_y(self, by):
        return {"y": lax.rem(self.y + by, 4)}

    def neighbour(self, half, ring, by):
        return self.along_y(by) if half == ring else self.along_x(by)

    def block(self, half, first, second):
        dx, dy = (second, first) if half == 0 else (first, second)
        x = lax.rem(self.x + dx, 4)
        y = lax.rem(self.y + dy, 4)
        return (x // 2) * 8 + y * 2 + lax.rem(x, 2)

    def greet(self):
        others = [self.partner, self.along_x(1), self.along_x(3), self.along_y(1), self.along_y(3)]
        for by in range(1, 8):
            other = lax.rem(self.section + by, 8)
            others.append({"z": lax.rem(other, 4), "core": other // 4})
        barrier = pltpu.get_barrier_semaphore()
        for other in others:
            pl.semaphore_signal(barrier, inc=1, device_id=other, device_id_type=MESH)
        pl.semaphore_wait(barrier, len(others))


def remote(src, dst, send_sem, recv_sem, to):
    return pltpu.make_async_remote_copy(
        src_ref=src, dst_ref=dst, send_sem=send_sem, recv_sem=recv_sem,
        device_id=to, device_id_type=MESH,
    )


def rows_of(index, rows):
    return pl.ds(pl.multiple_of(index * rows, rows), rows)


class Gather:
    def __init__(self, place, shard, full, cut, send_sem, recv_sem, own_sem):
        self.place, self.shard, self.full = place, shard, full
        self.rows, self.cuts = cut
        self.send_sem, self.recv_sem, self.own_sem = send_sem, recv_sem, own_sem

    def region(self, half, first, second, part):
        lo, mid, hi = self.cuts[half]
        lo, hi = ((lo, hi), (lo, mid), (mid, hi))[part]
        index = self.place.block(half, first, second)
        return self.full.at[rows_of(index, self.rows), lo:hi]

    def copy(self, half, slot, first, second, part, ring=0, by=1):
        ref = self.region(half, first, second, part)
        return remote(
            ref, ref, self.send_sem.at[half, slot], self.recv_sem.at[half, slot],
            self.place.neighbour(half, ring, by),
        )

    def own(self, half):
        lo, _, hi = self.cuts[half]
        return self.shard.at[:, lo:hi], self.region(half, 0, 0, 0)

    def moved_own(self, half, index=None):
        src, dst = self.own(half)
        if index is not None:
            lo, _, hi = self.cuts[half]
            dst = self.full.at[rows_of(index, self.rows), lo:hi]
        return remote(
            src, dst, self.send_sem.at[half, 20], self.recv_sem.at[half, 20], self.place.partner
        )

    def kept_own(self, half):
        src, dst = self.own(half)
        return pltpu.make_async_copy(src, dst, self.own_sem.at[half])

    def sends(self, half):
        yield 0, (0, 0), 0, 0, 1
        yield 1, (0, 0), 0, 0, 3
        yield 2, (3, 0), 1, 0, 1
        yield 3, (1, 0), 2, 0, 3
        for j, first in enumerate((0, 3, 1, 2)):
            yield 4 + 4 * j, (first, 0), 0, 1, 1
            yield 5 + 4 * j, (first, 0), 0, 1, 3
            yield 6 + 4 * j, (first, 3), 1, 1, 1
            yield 7 + 4 * j, (first, 1), 2, 1, 3

    def send(self, half, *slots):
        plan = {entry[0]: entry for entry in self.sends(half)}
        for slot in slots:
            _, block, part, ring, by = plan[slot]
            self.copy(half, slot, *block, part, ring, by).start()

    def wait(self, half, *slots):
        plan = {0: (3, 0, 0), 1: (1, 0, 0), 2: (2, 0, 1), 3: (2, 0, 2)}
        for j, first in enumerate((0, 3, 1, 2)):
            plan |= {
                4 + 4 * j: (first, 3, 0), 5 + 4 * j: (first, 1, 0),
                6 + 4 * j: (first, 2, 1), 7 + 4 * j: (first, 2, 2),
            }
        for slot in slots:
            self.copy(half, slot, *plan[slot]).wait_recv()

    def start_own(self, half):
        place = self.place

        @pl.when(place.moved)
        def _():
            self.moved_own(half, place.xhi * 8 + place.y * 2 + 1 - place.xlo).start()

        @pl.when(jnp.logical_not(place.moved))
        def _():
            self.kept_own(half).start()

    def wait_own(self, half):
        @pl.when(self.place.moved)
        def _():
            self.moved_own(half).wait_recv()

        @pl.when(jnp.logical_not(self.place.moved))
        def _():
            self.kept_own(half).wait()

    def wait_sent(self):
        for half in range(2):
            for slot, block, part, ring, by in self.sends(half):
                self.copy(half, slot, *block, part, ring, by).wait_send()

            @pl.when(self.place.moved)
            def _():
                self.moved_own(half).wait_send()


def start_own(parts):
    for part in parts:
        for half in range(2):
            part.start_own(half)


def gather(parts):
    pairs = [(part, half) for part in parts for half in range(2)]
    for part, half in pairs:
        part.wait_own(half)
        part.send(half, 0, 1, 4, 5)
    for part, half in pairs:
        part.wait(half, 0)
        part.send(half, 2, 8, 9)
        part.wait(half, 1)
        part.send(half, 3, 12, 13)
    for part, half in pairs:
        part.wait(half, 4)
        part.send(half, 6)
        part.wait(half, 5)
        part.send(half, 7)
    for part, half in pairs:
        part.wait(half, 2, 3)
        part.send(half, 16, 17)
    for j in (1, 2, 3):
        for part, half in pairs:
            part.wait(half, 4 + 4 * j)
            part.send(half, 6 + 4 * j)
            part.wait(half, 5 + 4 * j)
            part.send(half, 7 + 4 * j)
    for part, half in pairs:
        for j in range(4):
            part.wait(half, 6 + 4 * j, 7 + 4 * j)


class Reduce:
    def __init__(self, place, grad, landing, result, cut, send_sem, recv_sem):
        self.place, self.grad, self.landing, self.result = place, grad, landing, result
        self.rows, self.cuts = cut
        self.send_sem, self.recv_sem = send_sem, recv_sem

    def columns(self, half, part):
        lo, mid, hi = self.cuts[half]
        return ((lo, hi), (lo, mid), (mid, hi))[part]

    def region(self, half, first, second, part):
        lo, hi = self.columns(half, part)
        return self.grad.at[rows_of(self.place.block(half, first, second), self.rows), lo:hi]

    def slot_ref(self, half, slot, part):
        base = self.cuts[half][0]
        lo, hi = self.columns(half, part)
        return self.landing.at[half, slot, :, lo - base : hi - base]

    def copy(self, half, sem, first, second, part, slot, ring=0, by=1):
        return remote(
            self.region(half, first, second, part), self.slot_ref(half, slot, part),
            self.send_sem.at[half, sem], self.recv_sem.at[half, sem],
            self.place.neighbour(half, ring, by),
        )

    def plan(self):
        found = {}
        for i, second in enumerate((2, 3, 1, 0)):
            found[4 * i] = ((2, second), 1, i, 0, 1)
            found[4 * i + 1] = ((2, second), 2, i, 0, 3)
            found[4 * i + 2] = ((1, second), 0, 4 + i, 0, 1)
            found[4 * i + 3] = ((3, second), 0, 8 + i, 0, 3)
        found[16] = ((0, 2), 1, 12, 1, 1)
        found[17] = ((0, 2), 2, 12, 1, 3)
        found[18] = ((0, 1), 0, 13, 1, 1)
        found[19] = ((0, 3), 0, 14, 1, 3)
        return found

    def send(self, half, *sems):
        for sem in sems:
            block, part, slot, ring, by = self.plan()[sem]
            self.copy(half, sem, *block, part, slot, ring, by).start()

    def wait(self, half, *sems):
        for sem in sems:
            block, part, slot, ring, by = self.plan()[sem]
            self.copy(half, sem, *block, part, slot, ring, by).wait_recv()

    def wait_sent(self):
        for half in range(2):
            for sem, (block, part, slot, ring, by) in self.plan().items():
                self.copy(half, sem, *block, part, slot, ring, by).wait_send()

    def add(self, half, first, second, part, *slots):
        ref = self.region(half, first, second, part)
        value = ref[...].astype(F32)
        for slot in slots:
            value += self.slot_ref(half, slot, part)[...].astype(F32)
        ref[...] = value.astype(BF16)

    def finish(self, half):
        self.add(half, 0, 0, 0, 13, 14)

        @pl.when(self.place.moved)
        def _():
            self.moved(half).start()

    def moved(self, half):
        lo, hi = self.columns(half, 0)
        return remote(
            self.region(half, 0, 0, 0), self.result.at[:, lo:hi],
            self.send_sem.at[half, 20], self.recv_sem.at[half, 20], self.place.partner,
        )

    def put(self, out_ref, sem):
        here = pltpu.make_async_copy(self.region_rows(), out_ref, sem)
        across = pltpu.make_async_copy(self.result, out_ref, sem)

        @pl.when(self.place.moved)
        def _():
            for half in range(2):
                self.moved(half).wait()
            across.start()

        @pl.when(jnp.logical_not(self.place.moved))
        def _():
            here.start()

        def wait():
            @pl.when(self.place.moved)
            def _():
                across.wait()

            @pl.when(jnp.logical_not(self.place.moved))
            def _():
                here.wait()

        return wait

    def region_rows(self):
        return self.grad.at[rows_of(self.place.block(0, 0, 0), self.rows), :]


def reduce(parts):
    pairs = [(part, half) for part in parts for half in range(2)]
    for i in range(4):
        for part, half in pairs:
            part.send(half, 4 * i, 4 * i + 1)
    for i, second in enumerate((2, 3, 1, 0)):
        for part, half in pairs:
            part.wait(half, 4 * i)
            part.add(half, 1, second, 1, i)
            part.send(half, 4 * i + 2)
            part.wait(half, 4 * i + 1)
            part.add(half, 3, second, 2, i)
            part.send(half, 4 * i + 3)
    for i, second in enumerate((2, 3, 1, 0)):
        for part, half in pairs:
            part.wait(half, 4 * i + 2, 4 * i + 3)
            part.add(half, 0, second, 0, 4 + i, 8 + i)
            if i == 0:
                part.send(half, 16, 17)
            elif i == 1:
                part.wait(half, 17)
                part.add(half, 0, 3, 2, 12)
                part.send(half, 19)
            elif i == 2:
                part.wait(half, 16)
                part.add(half, 0, 1, 1, 12)
                part.send(half, 18)
    for part, half in pairs:
        part.wait(half, 18, 19)
        part.finish(half)


def head_probs(proj, bias, head):
    lo = head * HEAD
    queries = proj[:, lo : lo + HEAD]
    keys = proj[:, HD + lo : HD + lo + HEAD]
    scores = dot(queries, keys, ((1,), (1,))) * SCALE + bias
    shifted = jnp.exp(scores - jnp.max(scores, -1, keepdims=True))
    return shifted / jnp.sum(shifted, -1, keepdims=True)


def section_kernel(
    start_ref, member_ref, permitted_ref, qkv_shard, out_shard, hint_shard,
    base_ref, cot_ref, update_ref, gain_ref,
    mine_out, sum_qkv, sum_out, sum_hint,
    landed, leaving, back_landed, back_leaving, after, acc, proj, att, gproj, probs, bias_ref,
    member, permitted, qkv, out, hint, normed_t, att_t,
    update, slots, gs, mine, mine_rows, base_rows, cot_rows,
    land_qkv, land_out, land_hint, res_qkv, res_out, res_hint,
    hop_send, hop_recv, back_send, back_recv, small_send, small_recv, start_sem, local_sem, out_sem,
    qkv_send, qkv_recv, qkv_own, out_send, out_recv, out_own, hint_send, hint_recv, hint_own,
    rqkv_send, rqkv_recv, rout_send, rout_recv, rhint_send, rhint_recv,
    term_send, term_recv, gs_send, gs_recv, mine_send, mine_recv,
    go_sem,
):
    place = Place()
    section, core = place.section, place.core
    kept = jnp.logical_not(place.moved)
    place.greet()

    def member_copy():
        return remote(member_ref, member, small_send.at[0], small_recv.at[0], place.sibling)

    def permitted_copy():
        return remote(permitted_ref, permitted, small_send.at[1], small_recv.at[1], place.partner)

    def row_copies(to_sibling):
        owner = place.z + 4 * (1 - core) if to_sibling else section
        for i, (src, dst) in enumerate(((base_ref, base_rows), (cot_ref, cot_rows))):
            src = src.at[rows_of(owner, 32), :]
            if to_sibling:
                yield remote(src, dst, small_send.at[2 + i], small_recv.at[2 + i], place.sibling)
            else:
                yield pltpu.make_async_copy(src, dst, local_sem.at[i])

    def update_across():
        return remote(update_ref, update, small_send.at[4], small_recv.at[4], place.partner)

    def update_here():
        return pltpu.make_async_copy(update_ref, update, local_sem.at[2])

    def start_copy(k):
        return pltpu.make_async_copy(
            start_ref.at[:, k * CW : (k + 1) * CW], landed.at[k], start_sem.at[k]
        )

    def start_across(k):
        return remote(
            start_ref.at[:, k * CW : (k + 1) * CW], landed.at[k],
            hop_send.at[k], hop_recv.at[k], place.sibling,
        )

    def hop(k):
        return remote(leaving.at[k], landed.at[k], hop_send.at[k], hop_recv.at[k], place.later)

    first_here = (section == 0) & kept
    first_given = (section == 4) & kept

    qkv_gather = Gather(place, qkv_shard, qkv, QKV_CUT, qkv_send, qkv_recv, qkv_own)
    out_gather = Gather(place, out_shard, out, OUT_CUT, out_send, out_recv, out_own)
    hint_gather = Gather(place, hint_shard, hint, HINT_CUT, hint_send, hint_recv, hint_own)
    start_own([qkv_gather, out_gather])

    @pl.when(kept)
    def _():
        member_copy().start()
        for copy in row_copies(True):
            copy.start()
        for copy in row_copies(False):
            copy.start()
        update_here().start()
        member[...] = member_ref[...]
        permitted[...] = permitted_ref[...]

    @pl.when(place.moved)
    def _():
        permitted_copy().start()

    @pl.when(first_here)
    def _():
        for k in range(CH):
            start_copy(k).start()

    @pl.when(first_given)
    def _():
        for k in range(CH):
            start_across(k).start()

    @pl.when(core == 1)
    def _():
        pl.semaphore_wait(go_sem, 1)

    gather([qkv_gather, out_gather])

    @pl.when(core == 0)
    def _():
        pl.semaphore_signal(go_sem, inc=1, device_id=place.sibling, device_id_type=MESH)

    start_own([hint_gather])

    @pl.when(place.moved)
    def _():
        member_copy().wait_recv()
        permitted_copy().wait_recv()

    pairs = dot(dot(member[...], permitted[...]).astype(BF16), member[...], ((1,), (1,)))
    bias_ref[...] = jnp.where(pairs > 0.5, 0.0, -1e30)

    @pl.when(place.moved & (core == 1))
    def _():
        update_across().start()

    @pl.when(section >= 6)
    def _():
        gather([hint_gather])

    squares = jnp.zeros((ROWS, 1), F32)
    for k in range(CH):
        @pl.when(first_here)
        def _():
            start_copy(k).wait()

        @pl.when(jnp.logical_not(first_here))
        def _():
            hop(k).wait_recv()

        x = landed[k]
        wide = x.astype(F32)
        squares += jnp.sum(wide * wide, -1, keepdims=True)
        for n in range(3):
            cols = slice(n * HD, (n + 1) * HD)
            part = dot(x, qkv[k * CW : (k + 1) * CW, cols])
            if k == 0:
                acc[:, cols] = part
            elif k < CH - 1:
                acc[:, cols] += part
            else:
                inverse = lax.rsqrt(squares * (1.0 / WIDTH) + 1e-06)
                proj[:, cols] = ((acc[:, cols] + part) * inverse).astype(BF16)
    bias = bias_ref[...]
    for h in range(HEADS):
        soft = head_probs(proj, bias, h)
        probs[h] = soft
        lo = 2 * HD + h * HEAD
        value = dot(soft.astype(BF16), proj[:, lo : lo + HEAD])
        att[:, h * HEAD : (h + 1) * HEAD] = value.astype(BF16)

    @pl.when(first_given)
    def _():
        for k in range(CH):
            start_across(k).wait_send()

    attended = att[...]
    for k in range(CH):
        value = landed[k].astype(F32) + dot(attended, out[:, k * CW : (k + 1) * CW])
        leaving[k] = value.astype(BF16)

        @pl.when(section < 7)
        def _():
            hop(k).start()

    @pl.when(place.moved & (core == 0))
    def _():
        update_across().start()

    @pl.when(section < 6)
    def _():
        gather([hint_gather])

    @pl.when(place.moved)
    def _():
        update_across().wait_recv()

    @pl.when(kept)
    def _():
        update_here().wait()

    def along_column(by):
        other = lax.rem(section + by, 8)
        return other, {"z": lax.rem(other, 4), "core": other // 4}

    def term_copy(by, half):
        other, to = along_column(by)
        cols = slice(half * 1280, (half + 1) * 1280)
        return remote(
            update.at[rows_of(other, 32), cols], slots.at[by, :, cols],
            term_send.at[by, half], term_recv.at[by, half], to,
        )

    def gs_copy(by, owner):
        rows = gs.at[rows_of(owner, 32), :]
        return remote(rows, rows, gs_send.at[by], gs_recv.at[by], along_column(by)[1])

    far_first = (4, 3, 5, 2, 6, 1, 7)
    for half in range(2):
        for n in range(2):
            cols = slice(half * 1280 + n * 640, half * 1280 + (n + 1) * 640)
            value = update[:, cols].astype(F32)
            for k in range(CH):
                value += dot(leaving[k], hint[k * CW : (k + 1) * CW, cols])
            update[:, cols] = value.astype(BF16)
        for by in far_first:
            term_copy(by, half).start()

    @pl.when(kept)
    def _():
        for copy in row_copies(False):
            copy.wait()

    @pl.when(place.moved)
    def _():
        for copy in row_copies(True):
            copy.wait_recv()

    own_rows = rows_of(section, 32)
    summed = base_rows[...].astype(F32) + update[own_rows, :].astype(F32)
    for by in (1, 7, 2, 6, 3, 5, 4):
        for half in range(2):
            term_copy(by, half).wait_recv()
        summed += slots[by].astype(F32)
    inverse = lax.rsqrt(jnp.mean(summed * summed, -1, keepdims=True) + 1e-06)
    grad_normed = cot_rows[...].astype(F32) * gain_ref[...]
    slope = inverse * inverse * inverse * jnp.mean(grad_normed * summed, -1, keepdims=True)
    gs[own_rows, :] = (inverse * grad_normed - summed * slope).astype(BF16)
    for by in far_first:
        gs_copy(by, section).start()
    mine_rows[...] = summed.astype(BF16)

    def mine_copy(by, kind, owner):
        rows = mine.at[rows_of(owner, 32), :]
        to = {"z": lax.rem(place.z + by, 4), "core": place.xlo}
        return remote(mine_rows, rows, mine_send.at[by], mine_recv.at[by, kind], to)

    def mine_across():
        to = {"xlo": 1 - place.xlo}
        return remote(mine, mine, mine_send.at[4], mine_recv.at[4, 0], to)

    @pl.when(kept)
    def _():
        mine[own_rows, :] = summed.astype(BF16)
        for by in (2, 1, 3):
            mine_copy(by, 0, section).start()

    @pl.when(place.moved)
    def _():
        for by in (2, 1, 3, 0):
            mine_copy(by, 1, section).start()

    hint_gather.wait_sent()
    for by in (1, 7, 2, 6, 3, 5, 4):
        gs_copy(by, lax.rem(section + 8 - by, 8)).wait_recv()

    grad_sum = gs[...]
    for k in range(CH):
        acc[:, k * CW : (k + 1) * CW] = dot(grad_sum, hint[k * CW : (k + 1) * CW, :], ((1,), (1,)))

    red_qkv = Reduce(place, qkv, land_qkv, res_qkv, QKV_CUT, rqkv_send, rqkv_recv)
    red_out = Reduce(place, out, land_out, res_out, OUT_CUT, rout_send, rout_recv)
    red_hint = Reduce(place, hint, land_hint, res_hint, HINT_CUT, rhint_send, rhint_recv)

    mine_keep = pltpu.make_async_copy(mine, mine_out, out_sem.at[3])

    def hint_part():
        @pl.when(kept)
        def _():
            for by in range(4):
                for kind in range(2):
                    if (by, kind) != (0, 0):
                        owner = lax.rem(place.z + 4 - by, 4) + 4 * (core if kind == 0 else 1 - core)
                        mine_copy(by, kind, owner).wait_recv()
            mine_across().start()

        for m in range(CH):
            for n in range(FEAT // 512):
                cols = slice(n * 512, (n + 1) * 512)
                rows = slice(m * CW, (m + 1) * CW)
                hint[rows, cols] = dot(leaving[m], gs[:, cols], ((0,), (0,))).astype(BF16)
        reduce([red_hint])

        @pl.when(place.moved)
        def _():
            for by in (2, 1, 3, 0):
                mine_copy(by, 1, section).wait_send()
            mine_across().wait_recv()

        mine_keep.start()

    def transposes():
        squares = jnp.zeros((ROWS, 1), F32)
        for k in range(CH):
            wide = landed[k].astype(F32)
            squares += jnp.sum(wide * wide, -1, keepdims=True)
        inverse = lax.rsqrt(squares * (1.0 / WIDTH) + 1e-06)
        for k in range(CH):
            normed = (landed[k].astype(F32) * inverse).astype(BF16)
            normed_t[k * CW : (k + 1) * CW, :] = normed.T
        for k in range(HD // CW):
            att_t[k * CW : (k + 1) * CW, :] = att[:, k * CW : (k + 1) * CW].T

    @pl.when(core == 0)
    def _():
        hint_part()
        transposes()

    squares = jnp.zeros((ROWS, 1), F32)
    for k in range(CH):
        wide = landed[k].astype(F32)
        squares += jnp.sum(wide * wide, -1, keepdims=True)
    inverse = lax.rsqrt(squares * (1.0 / WIDTH) + 1e-06)

    def back(k):
        return remote(
            back_leaving.at[k], back_landed.at[k], back_send.at[k], back_recv.at[k], place.earlier
        )

    @pl.when(section == 7)
    def _():
        for k in range(CH):
            back_landed[k] = jnp.zeros((ROWS, CW), BF16)

    grad_att_cols = slice(WIDTH, WIDTH + HD)
    for k in range(CH):
        @pl.when(section < 7)
        def _():
            back(k).wait_recv()

        grad = (back_landed[k].astype(F32) + acc[:, k * CW : (k + 1) * CW]).astype(BF16)
        after[k] = grad
        part = dot(grad, out[:, k * CW : (k + 1) * CW], ((1,), (1,)))
        if k == 0:
            acc[:, grad_att_cols] = part
        else:
            acc[:, grad_att_cols] += part
    through = jnp.zeros((ROWS, 1), F32)
    for h in range(HEADS):
        lo = h * HEAD
        grad_att = acc[:, WIDTH + lo : WIDTH + lo + HEAD].astype(BF16)
        queries = proj[:, lo : lo + HEAD]
        keys = proj[:, HD + lo : HD + lo + HEAD]
        values = proj[:, 2 * HD + lo : 2 * HD + lo + HEAD]
        soft = probs[h]
        grad_probs = dot(grad_att, values, ((1,), (1,)))
        grad_values = dot(soft.astype(BF16), grad_att, ((0,), (0,))).astype(BF16)
        total = jnp.sum(grad_probs * soft, -1, keepdims=True)
        grad_scores = (soft * (grad_probs - total) * SCALE).astype(BF16)
        grad_queries = dot(grad_scores, keys).astype(BF16)
        grad_keys = dot(grad_scores, queries, ((0,), (0,))).astype(BF16)
        for n, (grad, value) in enumerate(
            ((grad_queries, queries), (grad_keys, keys), (grad_values, values))
        ):
            gproj[:, n * HD + lo : n * HD + lo + HEAD] = grad
            through += jnp.sum(grad.astype(F32) * value.astype(F32), -1, keepdims=True)
    slope = inverse * inverse * through * (1.0 / WIDTH)

    @pl.when(section > 0)
    def _():
        grad_proj = gproj[...]
        for k in range(CH):
            grad_normed = dot(grad_proj, qkv[k * CW : (k + 1) * CW, :], ((1,), (1,)))
            value = after[k].astype(F32) + inverse * grad_normed - landed[k].astype(F32) * slope
            back_leaving[k] = value.astype(BF16)
            back(k).start()

    @pl.when(core == 1)
    def _():
        transposes()

    qkv_gather.wait_sent()
    out_gather.wait_sent()
    for m in range(CH):
        rows = slice(m * CW, (m + 1) * CW)
        for n in range(3):
            cols = slice(n * HD, (n + 1) * HD)
            qkv[rows, cols] = dot(normed_t[rows, :], gproj[:, cols]).astype(BF16)
    for m in range(HD // CW):
        rows = slice(m * CW, (m + 1) * CW)
        for n in range(CH):
            out[rows, n * CW : (n + 1) * CW] = dot(att_t[rows, :], after[n]).astype(BF16)
    reduce([red_qkv, red_out])

    @pl.when(core == 1)
    def _():
        hint_part()

    keeps = [
        red.put(ref, out_sem.at[i])
        for i, (red, ref) in enumerate(((red_qkv, sum_qkv), (red_out, sum_out), (red_hint, sum_hint)))
    ]

    @pl.when(kept)
    def _():
        member_copy().wait_send()
        for copy in row_copies(True):
            copy.wait_send()
        for by in (2, 1, 3):
            mine_copy(by, 0, section).wait_send()
        mine_across().wait_send()

    @pl.when(place.moved)
    def _():
        permitted_copy().wait_send()
        update_across().wait_send()

    @pl.when(section < 7)
    def _():
        for k in range(CH):
            hop(k).wait_send()

    @pl.when(section > 0)
    def _():
        for k in range(CH):
            back(k).wait_send()

    for by in far_first:
        for half in range(2):
            term_copy(by, half).wait_send()
        gs_copy(by, section).wait_send()
    for red in (red_qkv, red_out, red_hint):
        red.wait_sent()
    mine_keep.wait()
    for keep in keeps:
        keep()


def scale_kernel(mine_ref, gain_ref, qkv_ref, out_ref, hint_ref, features, qkv, out, hint):
    mine = mine_ref[...].astype(F32)
    inverse = lax.rsqrt(jnp.mean(mine * mine, -1, keepdims=True) + 1e-06)
    features[...] = mine * inverse * gain_ref[...]
    for src, dst in ((qkv_ref, qkv), (out_ref, out), (hint_ref, hint)):
        dst[...] = src[...].astype(F32) * 4096.0 ** (-0.5)


def dma_sems(*shape):
    return pltpu.SemaphoreType.DMA(shape)


def kernel_call(kernel, ins, outs, scratch, collective_id, flops):
    spaces = {"v": pltpu.VMEM, "a": pl.ANY}
    return pl.pallas_call(
        kernel,
        out_shape=[shape for shape, _ in outs],
        in_specs=[pl.BlockSpec(memory_space=spaces[kind]) for kind in ins],
        out_specs=[pl.BlockSpec(memory_space=spaces[kind]) for _, kind in outs],
        scratch_shapes=scratch,
        compiler_params=pltpu.CompilerParams(
            collective_id=collective_id, has_side_effects=True, vmem_limit_bytes=VMEM_LIMIT
        ),
        cost_estimate=pl.CostEstimate(flops=flops, bytes_accessed=12_000_000, transcendentals=0),
    )


def tile_members(layout):
    holds = layout[None, :] == jnp.arange(ROWS)[:, None]
    tile_of = jnp.sum(jnp.where(holds, jnp.arange(ROWS)[None, :] // TILE, 0), 1)
    return (tile_of[:, None] == jnp.arange(128)[None, :]).astype(BF16)


def permitted_tiles(offset, mask):
    row_tile = jnp.arange(4)[:, None]
    col_tile = jnp.arange(4)[None, :]
    near_window = jnp.abs(col_tile - row_tile - offset[:, None]) <= 1
    permitted = (row_tile == col_tile) | near_window & (mask == 1)
    return jnp.pad(permitted.astype(BF16), ((0, 124), (0, 124)))


def shape_of(*dims, dtype=BF16):
    return jax.ShapeDtypeStruct(dims, dtype)


def shards(
    control_in, base_in, base_update, out_gain, cotangent,
    w_qkv, w_out, w_hint, window_offset, tile_mask, token_layout,
):
    member = tile_members(token_layout[0])
    permitted = permitted_tiles(window_offset[0], tile_mask[0])
    chunks = (CH, ROWS, CW)
    gain = out_gain[None]
    mine, sum_qkv, sum_out, sum_hint = kernel_call(
        section_kernel,
        "avvaaaaaav",
        [
            (shape_of(ROWS, FEAT), "a"),
            (shape_of(96, QKV), "a"),
            (shape_of(48, WIDTH), "a"),
            (shape_of(96, FEAT), "a"),
        ],
        [
            *[pltpu.VMEM(chunks, BF16)] * 5,
            pltpu.VMEM((ROWS, QKV), F32),
            pltpu.VMEM((ROWS, QKV), BF16),
            pltpu.VMEM((ROWS, HD), BF16),
            pltpu.VMEM((ROWS, QKV), BF16),
            pltpu.VMEM((HEADS, ROWS, ROWS), F32),
            pltpu.VMEM((ROWS, ROWS), F32),
            pltpu.VMEM((ROWS, 128), BF16),
            pltpu.VMEM((128, 128), BF16),
            pltpu.VMEM((WIDTH, QKV), BF16),
            pltpu.VMEM((HD, WIDTH), BF16),
            pltpu.VMEM((WIDTH, FEAT), BF16),
            pltpu.VMEM((WIDTH, ROWS), BF16),
            pltpu.VMEM((HD, ROWS), BF16),
            pltpu.VMEM((ROWS, FEAT), BF16),
            pltpu.VMEM((8, 32, FEAT), BF16),
            pltpu.VMEM((ROWS, FEAT), BF16),
            pltpu.VMEM((ROWS, FEAT), BF16),
            *[pltpu.VMEM((32, FEAT), BF16)] * 3,
            pltpu.VMEM((2, 15, 96, QKV // 2), BF16),
            pltpu.VMEM((2, 15, 48, WIDTH // 2), BF16),
            pltpu.VMEM((2, 15, 96, FEAT // 2), BF16),
            pltpu.VMEM((96, QKV), BF16),
            pltpu.VMEM((48, WIDTH), BF16),
            pltpu.VMEM((96, FEAT), BF16),
            *[dma_sems(CH)] * 4,
            dma_sems(5), dma_sems(5), dma_sems(CH), dma_sems(3), dma_sems(4),
            *[dma_sems(2, 21), dma_sems(2, 21), dma_sems(2)] * 3,
            *[dma_sems(2, 21)] * 6,
            dma_sems(8, 2), dma_sems(8, 2), dma_sems(8), dma_sems(8), dma_sems(5), dma_sems(5, 2),
            pltpu.SemaphoreType.REGULAR,
        ],
        1,
        100_000_000_000,
    )(
        control_in, member, permitted, w_qkv[0], w_out[0], w_hint[0],
        base_in, cotangent, base_update[0], gain,
    )
    features, grad_qkv, grad_out, grad_hint = pl.pallas_call(
        scale_kernel,
        out_shape=[
            shape_of(ROWS, FEAT, dtype=F32),
            shape_of(96, QKV, dtype=F32),
            shape_of(48, WIDTH, dtype=F32),
            shape_of(96, FEAT, dtype=F32),
        ],
        in_specs=[pl.BlockSpec(memory_space=pltpu.VMEM)] * 5,
        out_specs=[pl.BlockSpec(memory_space=pltpu.VMEM)] * 4,
        compiler_params=pltpu.CompilerParams(vmem_limit_bytes=VMEM_LIMIT // 2),
    )(mine, gain, sum_qkv, sum_out, sum_hint)
    return features, grad_qkv[None], grad_out[None], grad_hint[None]


def solution(mesh):
    parts = jax.sharding.Mesh(
        mesh.devices.reshape(2, 4, 2, 4, 2), ("xlo", "z", "xhi", "y", "core")
    )
    segment = ("xlo", "z")
    dp = ("xhi", "y", "core")
    by_rows = P(dp, None)
    by_both = P(segment, dp, None)
    placed = (
        by_rows, by_rows, by_both, P(), by_rows, by_both, by_both, by_both,
        P(segment, None), P(segment, None, None), by_rows,
    )
    return jax.shard_map(
        shards,
        mesh=parts,
        in_specs=placed,
        out_specs=(by_rows, by_both, by_both, by_both),
        check_vma=False,
    )
```

```python
import functools

import jax
import jax.numpy as jnp
from jax import lax
from jax.experimental import pallas as pl
from jax.experimental.pallas import tpu as pltpu
from jax.sharding import PartitionSpec as P

HEADS = 6
HEAD = 128
TILE = 64
ROWS = 256
WIDTH = 1536
FEAT = 2560
HD = HEADS * HEAD
QKV = 3 * HD
CW = 256
CH = WIDTH // CW
SCALE = HEAD ** (-0.5)
MESH = pl.DeviceIdType.MESH
VMEM_LIMIT = 60 * 1024 * 1024
F32 = jnp.float32
BF16 = jnp.bfloat16
QKV_CUT = (96, ((0, 640, 1152), (1152, 1792, 2304)))
OUT_CUT = (48, ((0, 384, 768), (768, 1152, 1536)))
HINT_CUT = (96, ((0, 640, 1280), (1280, 1920, 2560)))


def dot(a, b, dims=((1,), (0,))):
    return lax.dot_general(a, b, (dims, ((), ())), preferred_element_type=F32)


class Place:
    def __init__(self):
        self.xlo, self.z, self.xhi, self.y, self.core = (
            lax.axis_index(name) for name in ("xlo", "z", "xhi", "y", "core")
        )
        self.x = 2 * self.xhi + self.xlo
        self.section = self.z + 4 * self.core
        later = lax.rem(self.section + 1, 8)
        earlier = lax.rem(self.section + 7, 8)
        self.later = {"z": lax.rem(later, 4), "core": later // 4}
        self.earlier = {"z": lax.rem(earlier, 4), "core": earlier // 4}
        self.sibling = {"core": 1 - self.core}
        self.partner = {"xlo": 1 - self.xlo, "core": 1 - self.core}
        self.moved = self.xlo != self.core

    def along_x(self, by):
        x = lax.rem(self.x + by, 4)
        return {"xhi": x // 2, "xlo": lax.rem(x, 2)}

    def along_y(self, by):
        return {"y": lax.rem(self.y + by, 4)}

    def neighbour(self, half, ring, by):
        return self.along_y(by) if half == ring else self.along_x(by)

    def block(self, half, first, second):
        dx, dy = (second, first) if half == 0 else (first, second)
        x = lax.rem(self.x + dx, 4)
        y = lax.rem(self.y + dy, 4)
        return (x // 2) * 8 + y * 2 + lax.rem(x, 2)

    def greet(self):
        others = [self.partner, self.along_x(1), self.along_x(3), self.along_y(1), self.along_y(3)]
        for by in range(1, 8):
            other = lax.rem(self.section + by, 8)
            others.append({"z": lax.rem(other, 4), "core": other // 4})
        barrier = pltpu.get_barrier_semaphore()
        for other in others:
            pl.semaphore_signal(barrier, inc=1, device_id=other, device_id_type=MESH)
        pl.semaphore_wait(barrier, len(others))


def remote(src, dst, send_sem, recv_sem, to):
    return pltpu.make_async_remote_copy(
        src_ref=src, dst_ref=dst, send_sem=send_sem, recv_sem=recv_sem,
        device_id=to, device_id_type=MESH,
    )


def rows_of(index, rows):
    return pl.ds(pl.multiple_of(index * rows, rows), rows)


class Gather:
    def __init__(self, place, shard, full, cut, send_sem, recv_sem, own_sem):
        self.place, self.shard, self.full = place, shard, full
        self.rows, self.cuts = cut
        self.send_sem, self.recv_sem, self.own_sem = send_sem, recv_sem, own_sem

    def region(self, half, first, second, part):
        lo, mid, hi = self.cuts[half]
        lo, hi = ((lo, hi), (lo, mid), (mid, hi))[part]
        index = self.place.block(half, first, second)
        return self.full.at[rows_of(index, self.rows), lo:hi]

    def copy(self, half, slot, first, second, part, ring=0, by=1):
        ref = self.region(half, first, second, part)
        return remote(
            ref, ref, self.send_sem.at[half, slot], self.recv_sem.at[half, slot],
            self.place.neighbour(half, ring, by),
        )

    def own(self, half):
        lo, _, hi = self.cuts[half]
        return self.shard.at[:, lo:hi], self.region(half, 0, 0, 0)

    def moved_own(self, half, index=None):
        src, dst = self.own(half)
        if index is not None:
            lo, _, hi = self.cuts[half]
            dst = self.full.at[rows_of(index, self.rows), lo:hi]
        return remote(
            src, dst, self.send_sem.at[half, 20], self.recv_sem.at[half, 20], self.place.partner
        )

    def kept_own(self, half):
        src, dst = self.own(half)
        return pltpu.make_async_copy(src, dst, self.own_sem.at[half])

    def sends(self, half):
        yield 0, (0, 0), 0, 0, 1
        yield 1, (0, 0), 0, 0, 3
        yield 2, (3, 0), 1, 0, 1
        yield 3, (1, 0), 2, 0, 3
        for j, first in enumerate((0, 3, 1, 2)):
            yield 4 + 4 * j, (first, 0), 0, 1, 1
            yield 5 + 4 * j, (first, 0), 0, 1, 3
            yield 6 + 4 * j, (first, 3), 1, 1, 1
            yield 7 + 4 * j, (first, 1), 2, 1, 3

    def send(self, half, *slots):
        plan = {entry[0]: entry for entry in self.sends(half)}
        for slot in slots:
            _, block, part, ring, by = plan[slot]
            self.copy(half, slot, *block, part, ring, by).start()

    def wait(self, half, *slots):
        plan = {0: (3, 0, 0), 1: (1, 0, 0), 2: (2, 0, 1), 3: (2, 0, 2)}
        for j, first in enumerate((0, 3, 1, 2)):
            plan |= {
                4 + 4 * j: (first, 3, 0), 5 + 4 * j: (first, 1, 0),
                6 + 4 * j: (first, 2, 1), 7 + 4 * j: (first, 2, 2),
            }
        for slot in slots:
            self.copy(half, slot, *plan[slot]).wait_recv()

    def start_own(self, half):
        place = self.place

        @pl.when(place.moved)
        def _():
            self.moved_own(half, place.xhi * 8 + place.y * 2 + 1 - place.xlo).start()

        @pl.when(jnp.logical_not(place.moved))
        def _():
            self.kept_own(half).start()

    def wait_own(self, half):
        @pl.when(self.place.moved)
        def _():
            self.moved_own(half).wait_recv()

        @pl.when(jnp.logical_not(self.place.moved))
        def _():
            self.kept_own(half).wait()

    def wait_sent(self):
        for half in range(2):
            for slot, block, part, ring, by in self.sends(half):
                self.copy(half, slot, *block, part, ring, by).wait_send()

            @pl.when(self.place.moved)
            def _():
                self.moved_own(half).wait_send()


def start_own(parts):
    for part in parts:
        for half in range(2):
            part.start_own(half)


def gather(parts):
    pairs = [(part, half) for part in parts for half in range(2)]
    for part, half in pairs:
        part.wait_own(half)
        part.send(half, 0, 1, 4, 5)
    for part, half in pairs:
        part.wait(half, 0)
        part.send(half, 2, 8, 9)
        part.wait(half, 1)
        part.send(half, 3, 12, 13)
    for part, half in pairs:
        part.wait(half, 4)
        part.send(half, 6)
        part.wait(half, 5)
        part.send(half, 7)
    for part, half in pairs:
        part.wait(half, 2, 3)
        part.send(half, 16, 17)
    for j in (1, 2, 3):
        for part, half in pairs:
            part.wait(half, 4 + 4 * j)
            part.send(half, 6 + 4 * j)
            part.wait(half, 5 + 4 * j)
            part.send(half, 7 + 4 * j)
    for part, half in pairs:
        for j in range(4):
            part.wait(half, 6 + 4 * j, 7 + 4 * j)


class Reduce:
    def __init__(self, place, grad, landing, result, cut, send_sem, recv_sem):
        self.place, self.grad, self.landing, self.result = place, grad, landing, result
        self.rows, self.cuts = cut
        self.send_sem, self.recv_sem = send_sem, recv_sem

    def columns(self, half, part):
        lo, mid, hi = self.cuts[half]
        return ((lo, hi), (lo, mid), (mid, hi))[part]

    def region(self, half, first, second, part):
        lo, hi = self.columns(half, part)
        return self.grad.at[rows_of(self.place.block(half, first, second), self.rows), lo:hi]

    def slot_ref(self, half, slot, part):
        base = self.cuts[half][0]
        lo, hi = self.columns(half, part)
        return self.landing.at[half, slot, :, lo - base : hi - base]

    def copy(self, half, sem, first, second, part, slot, ring=0, by=1):
        return remote(
            self.region(half, first, second, part), self.slot_ref(half, slot, part),
            self.send_sem.at[half, sem], self.recv_sem.at[half, sem],
            self.place.neighbour(half, ring, by),
        )

    def plan(self):
        found = {}
        for i, second in enumerate((2, 3, 1, 0)):
            found[4 * i] = ((2, second), 1, i, 0, 1)
            found[4 * i + 1] = ((2, second), 2, i, 0, 3)
            found[4 * i + 2] = ((1, second), 0, 4 + i, 0, 1)
            found[4 * i + 3] = ((3, second), 0, 8 + i, 0, 3)
        found[16] = ((0, 2), 1, 12, 1, 1)
        found[17] = ((0, 2), 2, 12, 1, 3)
        found[18] = ((0, 1), 0, 13, 1, 1)
        found[19] = ((0, 3), 0, 14, 1, 3)
        return found

    def send(self, half, *sems):
        for sem in sems:
            block, part, slot, ring, by = self.plan()[sem]
            self.copy(half, sem, *block, part, slot, ring, by).start()

    def wait(self, half, *sems):
        for sem in sems:
            block, part, slot, ring, by = self.plan()[sem]
            self.copy(half, sem, *block, part, slot, ring, by).wait_recv()

    def wait_sent(self):
        for half in range(2):
            for sem, (block, part, slot, ring, by) in self.plan().items():
                self.copy(half, sem, *block, part, slot, ring, by).wait_send()

    def add(self, half, first, second, part, *slots):
        ref = self.region(half, first, second, part)
        value = ref[...].astype(F32)
        for slot in slots:
            value += self.slot_ref(half, slot, part)[...].astype(F32)
        ref[...] = value.astype(BF16)

    def finish(self, half):
        self.add(half, 0, 0, 0, 13, 14)

        @pl.when(self.place.moved)
        def _():
            self.moved(half).start()

    def moved(self, half):
        lo, hi = self.columns(half, 0)
        return remote(
            self.region(half, 0, 0, 0), self.result.at[:, lo:hi],
            self.send_sem.at[half, 20], self.recv_sem.at[half, 20], self.place.partner,
        )

    def put(self, out_ref, sem):
        here = pltpu.make_async_copy(self.region_rows(), out_ref, sem)
        across = pltpu.make_async_copy(self.result, out_ref, sem)

        @pl.when(self.place.moved)
        def _():
            for half in range(2):
                self.moved(half).wait()
            across.start()

        @pl.when(jnp.logical_not(self.place.moved))
        def _():
            here.start()

        def wait():
            @pl.when(self.place.moved)
            def _():
                across.wait()

            @pl.when(jnp.logical_not(self.place.moved))
            def _():
                here.wait()

        return wait

    def region_rows(self):
        return self.grad.at[rows_of(self.place.block(0, 0, 0), self.rows), :]


def reduce(parts):
    pairs = [(part, half) for part in parts for half in range(2)]
    across = (2, 3, 1, 0)

    def offer(i):
        for part, half in pairs:
            part.send(half, 4 * i, 4 * i + 1)

    def pass_on(i):
        for part, half in pairs:
            part.wait(half, 4 * i)
            part.add(half, 1, across[i], 1, i)
            part.send(half, 4 * i + 2)
            part.wait(half, 4 * i + 1)
            part.add(half, 3, across[i], 2, i)
            part.send(half, 4 * i + 3)

    def take(part, half, i):
        part.wait(half, 4 * i + 2, 4 * i + 3)
        part.add(half, 0, across[i], 0, 4 + i, 8 + i)

    offer(0)
    offer(1)
    offer(2)
    pass_on(0)
    offer(3)
    pass_on(1)
    pass_on(2)
    for part, half in pairs:
        take(part, half, 0)
        part.send(half, 16, 17)
    pass_on(3)
    for part, half in pairs:
        take(part, half, 1)
        part.wait(half, 17)
        part.add(half, 0, 3, 2, 12)
        part.send(half, 19)
        take(part, half, 2)
        part.wait(half, 16)
        part.add(half, 0, 1, 1, 12)
        part.send(half, 18)
    for part, half in pairs:
        take(part, half, 3)
    for part, half in pairs:
        part.wait(half, 18, 19)
        part.finish(half)


def head_probs(proj, bias, head):
    lo = head * HEAD
    queries = proj[:, lo : lo + HEAD]
    keys = proj[:, HD + lo : HD + lo + HEAD]
    scores = dot(queries, keys, ((1,), (1,))) * SCALE + bias
    shifted = jnp.exp(scores - jnp.max(scores, -1, keepdims=True))
    return shifted / jnp.sum(shifted, -1, keepdims=True)


def section_kernel(
    start_ref, layout_ref, offset_ref, mask_ref, qkv_shard, out_shard, hint_shard,
    base_ref, cot_ref, update_ref, gain_ref,
    mine_out, sum_qkv, sum_out, sum_hint,
    landed, leaving, back_landed, back_leaving, after, acc, proj, att, gproj, probs, bias_ref,
    member, permitted, own_member, own_permitted, qkv, out, hint, normed_t, att_t,
    update, slots, gs, mine, mine_rows, base_rows, part_rows, row_sum, cot,
    land_qkv, land_out, land_hint, res_qkv, res_out, res_hint,
    hop_send, hop_recv, back_send, back_recv, small_send, small_recv, start_sem, local_sem, out_sem,
    qkv_send, qkv_recv, qkv_own, out_send, out_recv, out_own, hint_send, hint_recv, hint_own,
    rqkv_send, rqkv_recv, rout_send, rout_recv, rhint_send, rhint_recv,
    term_send, term_recv, part_send, part_recv, gs_send, gs_recv, mine_send, mine_recv,
    go_sem,
):
    place = Place()
    section, core = place.section, place.core
    kept = jnp.logical_not(place.moved)
    place.greet()
    drains = []

    def drained(condition):
        return lambda body: drains.append(lambda: pl.when(condition)(body))

    def member_copy():
        return remote(own_member, member, small_send.at[0], small_recv.at[0], place.sibling)

    def permitted_copy():
        return remote(own_permitted, permitted, small_send.at[1], small_recv.at[1], place.partner)

    def base_across():
        rows = base_ref.at[rows_of(place.z + 4 * (1 - core), 32), :]
        return remote(rows, base_rows, small_send.at[2], small_recv.at[2], place.sibling)

    def base_here():
        rows = base_ref.at[rows_of(section, 32), :]
        return pltpu.make_async_copy(rows, base_rows, local_sem.at[0])

    def cot_across():
        return remote(cot_ref, cot, small_send.at[3], small_recv.at[3], place.sibling)

    def cot_here():
        return pltpu.make_async_copy(cot_ref, cot, local_sem.at[1])

    def update_across():
        return remote(update_ref, update, small_send.at[4], small_recv.at[4], place.partner)

    def update_here():
        return pltpu.make_async_copy(update_ref, update, local_sem.at[2])

    def start_copy(k):
        return pltpu.make_async_copy(
            start_ref.at[:, k * CW : (k + 1) * CW], landed.at[k], start_sem.at[k]
        )

    def start_across(k):
        return remote(
            start_ref.at[:, k * CW : (k + 1) * CW], landed.at[k],
            hop_send.at[k], hop_recv.at[k], place.sibling,
        )

    def hop(k):
        return remote(leaving.at[k], landed.at[k], hop_send.at[k], hop_recv.at[k], place.later)

    first_here = (section == 0) & kept
    first_given = (section == 4) & kept

    qkv_gather = Gather(place, qkv_shard, qkv, QKV_CUT, qkv_send, qkv_recv, qkv_own)
    out_gather = Gather(place, out_shard, out, OUT_CUT, out_send, out_recv, out_own)
    hint_gather = Gather(place, hint_shard, hint, HINT_CUT, hint_send, hint_recv, hint_own)
    start_own([qkv_gather, out_gather])

    @drained(kept)
    def _():
        member_copy().wait_send()
        base_across().wait_send()

    @drained(place.moved)
    def _():
        permitted_copy().wait_send()

    own_member[...] = tile_members(layout_ref[...])
    own_permitted[...] = permitted_tiles(offset_ref, mask_ref)

    @pl.when(kept)
    def _():
        member_copy().start()
        base_across().start()
        base_here().start()
        update_here().start()
        member[...] = own_member[...]
        permitted[...] = own_permitted[...]

    @pl.when(place.moved)
    def _():
        permitted_copy().start()

    @pl.when((section == 3) & kept)
    def _():
        cot_across().start()

    @drained((section == 3) & kept)
    def _():
        cot_across().wait_send()

    @pl.when((section == 7) & kept)
    def _():
        cot_here().start()

    @pl.when(first_here)
    def _():
        for k in range(CH):
            start_copy(k).start()

    @pl.when(first_given)
    def _():
        for k in range(CH):
            start_across(k).start()

    @pl.when(core == 1)
    def _():
        pl.semaphore_wait(go_sem, 1)

    gather([qkv_gather, out_gather])

    @pl.when(core == 0)
    def _():
        pl.semaphore_signal(go_sem, inc=1, device_id=place.sibling, device_id_type=MESH)

    start_own([hint_gather])

    @pl.when(place.moved)
    def _():
        member_copy().wait_recv()
        permitted_copy().wait_recv()

    pairs = dot(dot(member[...], permitted[...]).astype(BF16), member[...], ((1,), (1,)))
    bias_ref[...] = jnp.where(pairs > 0.5, 0.0, -1e30)

    @pl.when(place.moved & (core == 1))
    def _():
        update_across().start()

    @drained(place.moved)
    def _():
        update_across().wait_send()

    @pl.when(section >= 6)
    def _():
        gather([hint_gather])

    @drained(section < 7)
    def _():
        for k in range(CH):
            hop(k).wait_send()

    squares = jnp.zeros((ROWS, 1), F32)
    for k in range(CH):
        @pl.when(first_here)
        def _():
            start_copy(k).wait()

        @pl.when(jnp.logical_not(first_here))
        def _():
            hop(k).wait_recv()

        x = landed[k]
        wide = x.astype(F32)
        squares += jnp.sum(wide * wide, -1, keepdims=True)
        for n in range(3):
            cols = slice(n * HD, (n + 1) * HD)
            part = dot(x, qkv[k * CW : (k + 1) * CW, cols])
            if k == 0:
                acc[:, cols] = part
            elif k < CH - 1:
                acc[:, cols] += part
            else:
                inverse = lax.rsqrt(squares * (1.0 / WIDTH) + 1e-06)
                proj[:, cols] = ((acc[:, cols] + part) * inverse).astype(BF16)
    bias = bias_ref[...]
    for h in range(HEADS):
        soft = head_probs(proj, bias, h)
        probs[h] = soft
        lo = 2 * HD + h * HEAD
        value = dot(soft.astype(BF16), proj[:, lo : lo + HEAD])
        att[:, h * HEAD : (h + 1) * HEAD] = value.astype(BF16)

    @pl.when(first_given)
    def _():
        for k in range(CH):
            start_across(k).wait_send()

    attended = att[...]
    for k in range(CH):
        value = landed[k].astype(F32) + dot(attended, out[:, k * CW : (k + 1) * CW])
        leaving[k] = value.astype(BF16)

        @pl.when(section < 7)
        def _():
            hop(k).start()

    @pl.when(place.moved & (core == 0))
    def _():
        update_across().start()

    @pl.when(section < 6)
    def _():
        gather([hint_gather])

    @pl.when(place.moved)
    def _():
        update_across().wait_recv()

    @pl.when(kept)
    def _():
        update_here().wait()

    def along_column(by):
        other = lax.rem(section + by, 8)
        return other, {"z": lax.rem(other, 4), "core": other // 4}

    def term_copy(by, half):
        other, to = along_column(by)
        cols = slice(half * 1280, (half + 1) * 1280)
        return remote(
            update.at[rows_of(other, 32), cols], slots.at[by, :, cols],
            term_send.at[by, half], term_recv.at[by, half], to,
        )

    def part_copy(owner):
        return remote(
            part_rows, gs.at[rows_of(owner, 32), :],
            part_send.at[0], part_recv.at[owner], {"z": 3, "core": 1},
        )

    def gs_copy(child, piece):
        rows = gs.at[piece * 64 : (piece + 1) * 64, :]
        to = (
            place.sibling,
            {"z": lax.rem(place.z + 1, 4)},
            {"z": lax.rem(place.z + 3, 4)},
        )[child]
        return remote(rows, rows, gs_send.at[child, piece], gs_recv.at[piece], to)

    has_child = (core == 1, (section == 7) | (section == 4), section == 7)

    def pass_down(piece):
        for child in (2, 1, 0):
            @pl.when(has_child[child])
            def _():
                gs_copy(child, piece).start()

    far_first = (4, 3, 5, 2, 6, 1, 7)

    @drained(section >= 0)
    def _():
        for by in far_first:
            for half in range(2):
                term_copy(by, half).wait_send()

    @drained(section < 7)
    def _():
        part_copy(section).wait_send()

    for child in range(3):
        @drained(has_child[child])
        def _(child=child):
            for piece in range(4):
                gs_copy(child, piece).wait_send()

    for half in range(2):
        for n in range(2):
            cols = slice(half * 1280 + n * 640, half * 1280 + (n + 1) * 640)
            value = update[:, cols].astype(F32)
            for k in range(CH):
                value += dot(leaving[k], hint[k * CW : (k + 1) * CW, cols])
            update[:, cols] = value.astype(BF16)

        @pl.when(section < 7)
        def _():
            for by in far_first:
                term_copy(by, half).start()

    @pl.when(kept)
    def _():
        base_here().wait()

    @pl.when(place.moved)
    def _():
        base_across().wait_recv()

    own_rows = rows_of(section, 32)
    row_sum[...] = base_rows[...].astype(F32)
    for by in (1, 2, 3, 4, 5, 6, 7):
        @pl.when(lax.rem(section + 8 - by, 8) < 7)
        def _():
            for half in range(2):
                term_copy(by, half).wait_recv()
            row_sum[...] += slots[by].astype(F32)

    @pl.when(section < 7)
    def _():
        row_sum[...] += update[own_rows, :].astype(F32)
        part_rows[...] = row_sum[...].astype(BF16)
        part_copy(section).start()
        for piece in range(4):
            gs_copy(0, piece).wait_recv()
            pass_down(piece)

    @pl.when(section == 7)
    def _():
        gs[7 * 32 :, :] = row_sum[...].astype(BF16)

        @pl.when(kept)
        def _():
            cot_here().wait()

        @pl.when(place.moved)
        def _():
            cot_across().wait_recv()

        gain = gain_ref[...]
        for piece in range(4):
            rows = slice(piece * 64, (piece + 1) * 64)
            for owner in (2 * piece, 2 * piece + 1):
                if owner < 7:
                    part_copy(owner).wait_recv()
            summed = gs[rows, :].astype(F32) + update[rows, :].astype(F32)
            inverse = lax.rsqrt(jnp.mean(summed * summed, -1, keepdims=True) + 1e-06)
            grad_normed = cot[rows, :].astype(F32) * gain
            slope = inverse * inverse * inverse * jnp.mean(grad_normed * summed, -1, keepdims=True)
            gs[rows, :] = (inverse * grad_normed - summed * slope).astype(BF16)
            pass_down(piece)
        row_sum[...] += update[7 * 32 :, :].astype(F32)

    def mine_copy(by, kind, owner):
        rows = mine.at[rows_of(owner, 32), :]
        to = {"z": lax.rem(place.z + by, 4), "core": place.xlo}
        return remote(mine_rows, rows, mine_send.at[by], mine_recv.at[by, kind], to)

    def mine_across():
        to = {"xlo": 1 - place.xlo}
        return remote(mine, mine, mine_send.at[4], mine_recv.at[4, 0], to)

    @drained(kept)
    def _():
        for by in (2, 1, 3):
            mine_copy(by, 0, section).wait_send()
        mine_across().wait_send()

    @drained(place.moved)
    def _():
        for by in (2, 1, 3, 0):
            mine_copy(by, 1, section).wait_send()

    def share_summed():
        @pl.when(section < 7)
        def _():
            last = lax.rem(section + 1, 8)
            for half in range(2):
                cols = slice(half * 1280, (half + 1) * 1280)
                remote(
                    update.at[own_rows, cols], slots.at[last, :, cols],
                    term_send.at[last, half], term_recv.at[last, half], place.sibling,
                ).wait_recv()
            row_sum[...] += slots[last].astype(F32)

        mine_rows[...] = row_sum[...].astype(BF16)

        @pl.when(kept)
        def _():
            mine[own_rows, :] = mine_rows[...]
            for by in (2, 1, 3):
                mine_copy(by, 0, section).start()

        @pl.when(place.moved)
        def _():
            for by in (2, 1, 3, 0):
                mine_copy(by, 1, section).start()

    def collect_summed():
        @pl.when(kept)
        def _():
            for by in range(4):
                for kind in range(2):
                    if (by, kind) != (0, 0):
                        owner = lax.rem(place.z + 4 - by, 4) + 4 * (core if kind == 0 else 1 - core)
                        mine_copy(by, kind, owner).wait_recv()
            mine_across().start()

    hint_gather.wait_sent()
    grad_sum = gs[...]
    for k in range(CH):
        acc[:, k * CW : (k + 1) * CW] = dot(grad_sum, hint[k * CW : (k + 1) * CW, :], ((1,), (1,)))

    red_qkv = Reduce(place, qkv, land_qkv, res_qkv, QKV_CUT, rqkv_send, rqkv_recv)
    red_out = Reduce(place, out, land_out, res_out, OUT_CUT, rout_send, rout_recv)
    red_hint = Reduce(place, hint, land_hint, res_hint, HINT_CUT, rhint_send, rhint_recv)

    mine_keep = pltpu.make_async_copy(mine, mine_out, out_sem.at[3])

    def hint_grads():
        for m in range(CH):
            for n in range(FEAT // 512):
                cols = slice(n * 512, (n + 1) * 512)
                rows = slice(m * CW, (m + 1) * CW)
                hint[rows, cols] = dot(leaving[m], gs[:, cols], ((0,), (0,))).astype(BF16)

    def transposes():
        squares = jnp.zeros((ROWS, 1), F32)
        for k in range(CH):
            wide = landed[k].astype(F32)
            squares += jnp.sum(wide * wide, -1, keepdims=True)
        inverse = lax.rsqrt(squares * (1.0 / WIDTH) + 1e-06)
        for k in range(CH):
            normed = (landed[k].astype(F32) * inverse).astype(BF16)
            normed_t[k * CW : (k + 1) * CW, :] = normed.T
        for k in range(HD // CW):
            att_t[k * CW : (k + 1) * CW, :] = att[:, k * CW : (k + 1) * CW].T

    hint_early = (section < 3) | (section == 4)

    @pl.when(section == 0)
    def _():
        pl.semaphore_wait(go_sem, 1)

    @pl.when(hint_early)
    def _():
        hint_grads()
        reduce([red_hint])

    @pl.when(section == 4)
    def _():
        pl.semaphore_signal(go_sem, inc=1, device_id=place.sibling, device_id_type=MESH)

    @pl.when(core == 0)
    def _():
        transposes()
        share_summed()

    @pl.when(section < 3)
    def _():
        collect_summed()

    @drained(section > 0)
    def _():
        for k in range(CH):
            back(k).wait_send()

    squares = jnp.zeros((ROWS, 1), F32)
    for k in range(CH):
        wide = landed[k].astype(F32)
        squares += jnp.sum(wide * wide, -1, keepdims=True)
    inverse = lax.rsqrt(squares * (1.0 / WIDTH) + 1e-06)

    def back(k):
        return remote(
            back_leaving.at[k], back_landed.at[k], back_send.at[k], back_recv.at[k], place.earlier
        )

    @pl.when(section == 7)
    def _():
        for k in range(CH):
            back_landed[k] = jnp.zeros((ROWS, CW), BF16)

    grad_att_cols = slice(WIDTH, WIDTH + HD)
    for k in range(CH):
        @pl.when(section < 7)
        def _():
            back(k).wait_recv()

        grad = (back_landed[k].astype(F32) + acc[:, k * CW : (k + 1) * CW]).astype(BF16)
        after[k] = grad
        part = dot(grad, out[:, k * CW : (k + 1) * CW], ((1,), (1,)))
        if k == 0:
            acc[:, grad_att_cols] = part
        else:
            acc[:, grad_att_cols] += part
    through = jnp.zeros((ROWS, 1), F32)
    for h in range(HEADS):
        lo = h * HEAD
        grad_att = acc[:, WIDTH + lo : WIDTH + lo + HEAD].astype(BF16)
        queries = proj[:, lo : lo + HEAD]
        keys = proj[:, HD + lo : HD + lo + HEAD]
        values = proj[:, 2 * HD + lo : 2 * HD + lo + HEAD]
        soft = probs[h]
        grad_probs = dot(grad_att, values, ((1,), (1,)))
        grad_values = dot(soft.astype(BF16), grad_att, ((0,), (0,))).astype(BF16)
        total = jnp.sum(grad_probs * soft, -1, keepdims=True)
        grad_scores = (soft * (grad_probs - total) * SCALE).astype(BF16)
        grad_queries = dot(grad_scores, keys).astype(BF16)
        grad_keys = dot(grad_scores, queries, ((0,), (0,))).astype(BF16)
        for n, (grad, value) in enumerate(
            ((grad_queries, queries), (grad_keys, keys), (grad_values, values))
        ):
            gproj[:, n * HD + lo : n * HD + lo + HEAD] = grad
            through += jnp.sum(grad.astype(F32) * value.astype(F32), -1, keepdims=True)
    slope = inverse * inverse * through * (1.0 / WIDTH)

    @pl.when(section > 0)
    def _():
        grad_proj = gproj[...]
        for k in range(CH):
            grad_normed = dot(grad_proj, qkv[k * CW : (k + 1) * CW, :], ((1,), (1,)))
            value = after[k].astype(F32) + inverse * grad_normed - landed[k].astype(F32) * slope
            back_leaving[k] = value.astype(BF16)
            back(k).start()

    @pl.when(section == 7)
    def _():
        for half in range(2):
            for by in far_first:
                term_copy(by, half).start()

    @pl.when(core == 1)
    def _():
        transposes()
        share_summed()

    @pl.when((section == 3) | (section == 4))
    def _():
        collect_summed()

    qkv_gather.wait_sent()
    out_gather.wait_sent()
    for m in range(CH):
        rows = slice(m * CW, (m + 1) * CW)
        for n in range(3):
            cols = slice(n * HD, (n + 1) * HD)
            qkv[rows, cols] = dot(normed_t[rows, :], gproj[:, cols]).astype(BF16)
    for m in range(HD // CW):
        rows = slice(m * CW, (m + 1) * CW)
        for n in range(CH):
            out[rows, n * CW : (n + 1) * CW] = dot(att_t[rows, :], after[n]).astype(BF16)
    @pl.when(hint_early)
    def _():
        reduce([red_qkv, red_out])

    @pl.when(jnp.logical_not(hint_early))
    def _():
        hint_grads()
        reduce([red_qkv, red_out, red_hint])

    @pl.when(section >= 5)
    def _():
        collect_summed()

    @pl.when(place.moved)
    def _():
        mine_across().wait_recv()

    mine_keep.start()
    keeps = [
        red.put(ref, out_sem.at[i])
        for i, (red, ref) in enumerate(((red_qkv, sum_qkv), (red_out, sum_out), (red_hint, sum_hint)))
    ]
    for red in (red_qkv, red_out, red_hint):
        red.wait_sent()
    mine_keep.wait()
    for keep in keeps:
        keep()
    for drain in drains:
        drain()


def scale_kernel(
    mine_ref, gain_ref, qkv_ref, out_ref, hint_ref, features_out, qkv_out, out_out, hint_out,
    mine, qkv, out, hint, features, grad_qkv, grad_out, grad_hint, in_sem, out_sem,
):
    ins = ((mine_ref, mine), (qkv_ref, qkv), (out_ref, out), (hint_ref, hint))
    outs = (
        (features, features_out), (grad_qkv, qkv_out), (grad_out, out_out), (grad_hint, hint_out)
    )
    reads = [pltpu.make_async_copy(*pair, in_sem.at[i]) for i, pair in enumerate(ins)]
    writes = [pltpu.make_async_copy(*pair, out_sem.at[i]) for i, pair in enumerate(outs)]
    for read in reads:
        read.start()
    gain = gain_ref[...]
    for i in range(4):
        reads[i].wait()
        if i == 0:
            wide = mine[...].astype(F32)
            inverse = lax.rsqrt(jnp.mean(wide * wide, -1, keepdims=True) + 1e-06)
            features[...] = wide * inverse * gain
        else:
            outs[i][0][...] = ins[i][1][...].astype(F32) * 4096.0 ** (-0.5)
        writes[i].start()
    for write in writes:
        write.wait()


def dma_sems(*shape):
    return pltpu.SemaphoreType.DMA(shape)


def kernel_call(kernel, ins, outs, scratch, collective_id, flops):
    spaces = {"v": pltpu.VMEM, "a": pl.ANY, "s": pltpu.SMEM}
    return pl.pallas_call(
        kernel,
        out_shape=[shape for shape, _ in outs],
        in_specs=[pl.BlockSpec(memory_space=spaces[kind]) for kind in ins],
        out_specs=[pl.BlockSpec(memory_space=spaces[kind]) for _, kind in outs],
        scratch_shapes=scratch,
        compiler_params=pltpu.CompilerParams(
            collective_id=collective_id, has_side_effects=True, vmem_limit_bytes=VMEM_LIMIT
        ),
        cost_estimate=pl.CostEstimate(flops=flops, bytes_accessed=12_000_000, transcendentals=0),
    )


def tile_members(layout):
    tokens = lax.broadcasted_iota(jnp.int32, (ROWS, ROWS), 0)
    positions = lax.broadcasted_iota(jnp.int32, (ROWS, ROWS), 1)
    tiles = jnp.where(layout == tokens, (positions // TILE).astype(F32), 0.0)
    tile_of = jnp.sum(tiles, -1, keepdims=True)
    columns = lax.broadcasted_iota(jnp.int32, (ROWS, 128), 1).astype(F32)
    return jnp.where(tile_of == columns, 1.0, 0.0).astype(BF16)


def permitted_tiles(offset, mask):
    row = lax.broadcasted_iota(jnp.int32, (128, 128), 0)
    col = lax.broadcasted_iota(jnp.int32, (128, 128), 1)
    found = jnp.where(row == col, 1, 0)
    for i in range(4):
        for j in range(4):
            if i != j:
                near = jnp.abs(j - i - offset[0, i]) <= 1
                value = jnp.where(near & (mask[0, i, j] == 1), 1, 0)
                found = jnp.where((row == i) & (col == j), value, found)
    return found.astype(F32).astype(BF16)


def shape_of(*dims, dtype=BF16):
    return jax.ShapeDtypeStruct(dims, dtype)


def shards(
    control_in, base_in, base_update, out_gain, cotangent,
    w_qkv, w_out, w_hint, window_offset, tile_mask, token_layout,
):
    chunks = (CH, ROWS, CW)
    gain = out_gain[None]
    mine, sum_qkv, sum_out, sum_hint = kernel_call(
        section_kernel,
        "avssaaaaaav",
        [
            (shape_of(ROWS, FEAT), "a"),
            (shape_of(96, QKV), "a"),
            (shape_of(48, WIDTH), "a"),
            (shape_of(96, FEAT), "a"),
        ],
        [
            *[pltpu.VMEM(chunks, BF16)] * 5,
            pltpu.VMEM((ROWS, QKV), F32),
            pltpu.VMEM((ROWS, QKV), BF16),
            pltpu.VMEM((ROWS, HD), BF16),
            pltpu.VMEM((ROWS, QKV), BF16),
            pltpu.VMEM((HEADS, ROWS, ROWS), F32),
            pltpu.VMEM((ROWS, ROWS), F32),
            *[pltpu.VMEM((ROWS, 128), BF16), pltpu.VMEM((128, 128), BF16)] * 2,
            pltpu.VMEM((WIDTH, QKV), BF16),
            pltpu.VMEM((HD, WIDTH), BF16),
            pltpu.VMEM((WIDTH, FEAT), BF16),
            pltpu.VMEM((WIDTH, ROWS), BF16),
            pltpu.VMEM((HD, ROWS), BF16),
            pltpu.VMEM((ROWS, FEAT), BF16),
            pltpu.VMEM((8, 32, FEAT), BF16),
            pltpu.VMEM((ROWS, FEAT), BF16),
            pltpu.VMEM((ROWS, FEAT), BF16),
            *[pltpu.VMEM((32, FEAT), BF16)] * 3,
            pltpu.VMEM((32, FEAT), F32),
            pltpu.VMEM((ROWS, FEAT), BF16),
            pltpu.VMEM((2, 15, 96, QKV // 2), BF16),
            pltpu.VMEM((2, 15, 48, WIDTH // 2), BF16),
            pltpu.VMEM((2, 15, 96, FEAT // 2), BF16),
            pltpu.VMEM((96, QKV), BF16),
            pltpu.VMEM((48, WIDTH), BF16),
            pltpu.VMEM((96, FEAT), BF16),
            *[dma_sems(CH)] * 4,
            dma_sems(5), dma_sems(5), dma_sems(CH), dma_sems(3), dma_sems(4),
            *[dma_sems(2, 21), dma_sems(2, 21), dma_sems(2)] * 3,
            *[dma_sems(2, 21)] * 6,
            dma_sems(8, 2), dma_sems(8, 2), dma_sems(1), dma_sems(7), dma_sems(3, 4), dma_sems(4),
            dma_sems(5), dma_sems(5, 2),
            pltpu.SemaphoreType.REGULAR,
        ],
        1,
        100_000_000_000,
    )(
        control_in, token_layout, window_offset, tile_mask, w_qkv[0], w_out[0], w_hint[0],
        base_in, cotangent, base_update[0], gain,
    )
    features, grad_qkv, grad_out, grad_hint = pl.pallas_call(
        scale_kernel,
        out_shape=[
            shape_of(ROWS, FEAT, dtype=F32),
            shape_of(96, QKV, dtype=F32),
            shape_of(48, WIDTH, dtype=F32),
            shape_of(96, FEAT, dtype=F32),
        ],
        in_specs=[
            pl.BlockSpec(memory_space=pltpu.VMEM if i == 1 else pl.ANY) for i in range(5)
        ],
        out_specs=[pl.BlockSpec(memory_space=pl.ANY)] * 4,
        scratch_shapes=[
            pltpu.VMEM(dims, dtype)
            for dtype in (BF16, F32)
            for dims in ((ROWS, FEAT), (96, QKV), (48, WIDTH), (96, FEAT))
        ]
        + [dma_sems(4), dma_sems(4)],
        compiler_params=pltpu.CompilerParams(vmem_limit_bytes=VMEM_LIMIT // 2),
    )(mine, gain, sum_qkv, sum_out, sum_hint)
    return features, grad_qkv[None], grad_out[None], grad_hint[None]


def solution(mesh):
    parts = jax.sharding.Mesh(
        mesh.devices.reshape(2, 4, 2, 4, 2), ("xlo", "z", "xhi", "y", "core")
    )
    segment = ("xlo", "z")
    dp = ("xhi", "y", "core")
    by_rows = P(dp, None)
    by_both = P(segment, dp, None)
    placed = (
        by_rows, by_rows, by_both, P(), by_rows, by_both, by_both, by_both,
        P(segment, None), P(segment, None, None), by_rows,
    )
    return jax.shard_map(
        shards,
        mesh=parts,
        in_specs=placed,
        out_specs=(by_rows, by_both, by_both, by_both),
        check_vma=False,
    )
```

```python
import functools

import jax
import jax.numpy as jnp
from jax import lax
from jax.experimental import pallas as pl
from jax.experimental.pallas import tpu as pltpu
from jax.sharding import PartitionSpec as P

HEADS = 6
HEAD = 128
TILE = 64
ROWS = 256
WIDTH = 1536
FEAT = 2560
HD = HEADS * HEAD
QKV = 3 * HD
CW = 256
CH = WIDTH // CW
SCALE = HEAD ** (-0.5)
MESH = pl.DeviceIdType.MESH
VMEM_LIMIT = 60 * 1024 * 1024
F32 = jnp.float32
BF16 = jnp.bfloat16
QKV_CUT = (96, ((0, 640, 1152), (1152, 1792, 2304)))
OUT_CUT = (48, ((0, 384, 768), (768, 1152, 1536)))
HINT_CUT = (96, ((0, 640, 1280), (1280, 1920, 2560)))


def dot(a, b, dims=((1,), (0,))):
    return lax.dot_general(a, b, (dims, ((), ())), preferred_element_type=F32)


def at_section(section):
    core = section // 4
    return {"z": section + core * (7 - 2 * section), "core": core}


def section_at(z, core):
    return z + core * (7 - 2 * z)


class Place:
    def __init__(self):
        self.xlo, self.z, self.xhi, self.y, self.core = (
            lax.axis_index(name) for name in ("xlo", "z", "xhi", "y", "core")
        )
        self.x = 2 * self.xhi + self.xlo
        self.section = section_at(self.z, self.core)
        self.later = at_section(lax.rem(self.section + 1, 8))
        self.earlier = at_section(lax.rem(self.section + 7, 8))
        self.sibling = {"core": 1 - self.core}
        self.kept = self.xlo == self.core
        self.home = (self.xlo == 0) & (self.core == 0)
        self.away = jnp.logical_not(self.home)
        self.worker = {
            "xlo": self.core,
            "z": self.z + self.xlo * (3 - 2 * self.z),
            "core": self.xlo,
        }
        self.owner = {
            "xlo": self.core,
            "z": self.z + self.core * (3 - 2 * self.z),
            "core": self.xlo,
        }

    def along_x(self, by):
        x = lax.rem(self.x + by, 4)
        return {"xhi": x // 2, "xlo": lax.rem(x, 2)}

    def along_y(self, by):
        return {"y": lax.rem(self.y + by, 4)}

    def neighbour(self, half, ring, by):
        return self.along_y(by) if half == ring else self.along_x(by)

    def block(self, half, first, second):
        dx, dy = (second, first) if half == 0 else (first, second)
        x = lax.rem(self.x + dx, 4)
        y = lax.rem(self.y + dy, 4)
        return (x // 2) * 8 + y * 2 + lax.rem(x, 2)

    def greet(self):
        others = [self.along_x(1), self.along_x(3), self.along_y(1), self.along_y(3)]
        others += [at_section(lax.rem(self.section + by, 8)) for by in range(1, 8)]
        barrier = pltpu.get_barrier_semaphore()
        for other in others:
            pl.semaphore_signal(barrier, inc=1, device_id=other, device_id_type=MESH)

        @pl.when(self.away)
        def _():
            for other in (self.worker, self.owner):
                pl.semaphore_signal(barrier, inc=1, device_id=other, device_id_type=MESH)
            pl.semaphore_wait(barrier, len(others) + 2)

        @pl.when(self.home)
        def _():
            pl.semaphore_wait(barrier, len(others))


def remote(src, dst, send_sem, recv_sem, to):
    return pltpu.make_async_remote_copy(
        src_ref=src, dst_ref=dst, send_sem=send_sem, recv_sem=recv_sem,
        device_id=to, device_id_type=MESH,
    )


def rows_of(index, rows):
    return pl.ds(pl.multiple_of(index * rows, rows), rows)


class Gather:
    def __init__(self, place, shard, full, cut, send_sem, recv_sem, own_sem):
        self.place, self.shard, self.full = place, shard, full
        self.rows, self.cuts = cut
        self.send_sem, self.recv_sem, self.own_sem = send_sem, recv_sem, own_sem

    def region(self, half, first, second, part):
        lo, mid, hi = self.cuts[half]
        lo, hi = ((lo, hi), (lo, mid), (mid, hi))[part]
        index = self.place.block(half, first, second)
        return self.full.at[rows_of(index, self.rows), lo:hi]

    def copy(self, half, slot, first, second, part, ring=0, by=1):
        ref = self.region(half, first, second, part)
        return remote(
            ref, ref, self.send_sem.at[half, slot], self.recv_sem.at[half, slot],
            self.place.neighbour(half, ring, by),
        )

    def own(self, half):
        lo, _, hi = self.cuts[half]
        return self.shard.at[:, lo:hi], self.region(half, 0, 0, 0)

    def moved_own(self, half, index=None):
        src, dst = self.own(half)
        if index is not None:
            lo, _, hi = self.cuts[half]
            dst = self.full.at[rows_of(index, self.rows), lo:hi]
        return remote(
            src, dst, self.send_sem.at[half, 20], self.recv_sem.at[half, 20], self.place.worker
        )

    def kept_own(self, half):
        src, dst = self.own(half)
        return pltpu.make_async_copy(src, dst, self.own_sem.at[half])

    def sends(self, half):
        yield 0, (0, 0), 0, 0, 1
        yield 1, (0, 0), 0, 0, 3
        yield 2, (3, 0), 1, 0, 1
        yield 3, (1, 0), 2, 0, 3
        for j, first in enumerate((0, 3, 1, 2)):
            yield 4 + 4 * j, (first, 0), 0, 1, 1
            yield 5 + 4 * j, (first, 0), 0, 1, 3
            yield 6 + 4 * j, (first, 3), 1, 1, 1
            yield 7 + 4 * j, (first, 1), 2, 1, 3

    def send(self, half, *slots):
        plan = {entry[0]: entry for entry in self.sends(half)}
        for slot in slots:
            _, block, part, ring, by = plan[slot]
            self.copy(half, slot, *block, part, ring, by).start()

    def wait(self, half, *slots):
        plan = {0: (3, 0, 0), 1: (1, 0, 0), 2: (2, 0, 1), 3: (2, 0, 2)}
        for j, first in enumerate((0, 3, 1, 2)):
            plan |= {
                4 + 4 * j: (first, 3, 0), 5 + 4 * j: (first, 1, 0),
                6 + 4 * j: (first, 2, 1), 7 + 4 * j: (first, 2, 2),
            }
        for slot in slots:
            self.copy(half, slot, *plan[slot]).wait_recv()

    def start_own(self, half):
        place = self.place

        @pl.when(place.away)
        def _():
            self.moved_own(half, place.xhi * 8 + place.y * 2 + place.core).start()

        @pl.when(place.home)
        def _():
            self.kept_own(half).start()

    def wait_own(self, half):
        @pl.when(self.place.away)
        def _():
            self.moved_own(half).wait_recv()

        @pl.when(self.place.home)
        def _():
            self.kept_own(half).wait()

    def wait_sent(self):
        for half in range(2):
            for slot, block, part, ring, by in self.sends(half):
                self.copy(half, slot, *block, part, ring, by).wait_send()

            @pl.when(self.place.away)
            def _():
                self.moved_own(half).wait_send()


def start_own(parts):
    for part in parts:
        for half in range(2):
            part.start_own(half)


def gather(parts):
    pairs = [(part, half) for part in parts for half in range(2)]
    for part, half in pairs:
        part.wait_own(half)
        part.send(half, 0, 1, 4, 5)
    for part, half in pairs:
        part.wait(half, 0)
        part.send(half, 2, 8, 9)
        part.wait(half, 1)
        part.send(half, 3, 12, 13)
    for part, half in pairs:
        part.wait(half, 4)
        part.send(half, 6)
        part.wait(half, 5)
        part.send(half, 7)
    for part, half in pairs:
        part.wait(half, 2, 3)
        part.send(half, 16, 17)
    for j in (1, 2, 3):
        for part, half in pairs:
            part.wait(half, 4 + 4 * j)
            part.send(half, 6 + 4 * j)
            part.wait(half, 5 + 4 * j)
            part.send(half, 7 + 4 * j)
    for part, half in pairs:
        for j in range(4):
            part.wait(half, 6 + 4 * j, 7 + 4 * j)


class Reduce:
    def __init__(self, place, grad, landing, result, cut, send_sem, recv_sem):
        self.place, self.grad, self.landing, self.result = place, grad, landing, result
        self.rows, self.cuts = cut
        self.send_sem, self.recv_sem = send_sem, recv_sem

    def columns(self, half, part):
        lo, mid, hi = self.cuts[half]
        return ((lo, hi), (lo, mid), (mid, hi))[part]

    def region(self, half, first, second, part):
        lo, hi = self.columns(half, part)
        return self.grad.at[rows_of(self.place.block(half, first, second), self.rows), lo:hi]

    def slot_ref(self, half, slot, part):
        base = self.cuts[half][0]
        lo, hi = self.columns(half, part)
        return self.landing.at[half, slot, :, lo - base : hi - base]

    def copy(self, half, sem, first, second, part, slot, ring=0, by=1):
        return remote(
            self.region(half, first, second, part), self.slot_ref(half, slot, part),
            self.send_sem.at[half, sem], self.recv_sem.at[half, sem],
            self.place.neighbour(half, ring, by),
        )

    def plan(self):
        found = {}
        for i, second in enumerate((2, 3, 1, 0)):
            found[4 * i] = ((2, second), 1, i, 0, 1)
            found[4 * i + 1] = ((2, second), 2, i, 0, 3)
            found[4 * i + 2] = ((1, second), 0, 4 + i, 0, 1)
            found[4 * i + 3] = ((3, second), 0, 8 + i, 0, 3)
        found[16] = ((0, 2), 1, 12, 1, 1)
        found[17] = ((0, 2), 2, 12, 1, 3)
        found[18] = ((0, 1), 0, 13, 1, 1)
        found[19] = ((0, 3), 0, 14, 1, 3)
        return found

    def send(self, half, *sems):
        for sem in sems:
            block, part, slot, ring, by = self.plan()[sem]
            self.copy(half, sem, *block, part, slot, ring, by).start()

    def wait(self, half, *sems):
        for sem in sems:
            block, part, slot, ring, by = self.plan()[sem]
            self.copy(half, sem, *block, part, slot, ring, by).wait_recv()

    def wait_sent(self):
        for half in range(2):
            for sem, (block, part, slot, ring, by) in self.plan().items():
                self.copy(half, sem, *block, part, slot, ring, by).wait_send()

    def add(self, half, first, second, part, *slots):
        ref = self.region(half, first, second, part)
        value = ref[...].astype(F32)
        for slot in slots:
            value += self.slot_ref(half, slot, part)[...].astype(F32)
        ref[...] = value.astype(BF16)

    def finish(self, half):
        self.add(half, 0, 0, 0, 13, 14)

        @pl.when(self.place.away)
        def _():
            self.moved(half).start()

    def moved(self, half):
        lo, hi = self.columns(half, 0)
        return remote(
            self.region(half, 0, 0, 0), self.result.at[:, lo:hi],
            self.send_sem.at[half, 20], self.recv_sem.at[half, 20], self.place.owner,
        )

    def put(self, out_ref, sem):
        here = pltpu.make_async_copy(self.region_rows(), out_ref, sem)
        across = pltpu.make_async_copy(self.result, out_ref, sem)

        @pl.when(self.place.away)
        def _():
            for half in range(2):
                self.moved(half).wait()
            across.start()

        @pl.when(self.place.home)
        def _():
            here.start()

        def wait():
            @pl.when(self.place.away)
            def _():
                across.wait()

            @pl.when(self.place.home)
            def _():
                here.wait()

        return wait

    def region_rows(self):
        return self.grad.at[rows_of(self.place.block(0, 0, 0), self.rows), :]


def reduce(parts, midway=lambda: None):
    pairs = [(part, half) for part in parts for half in range(2)]
    across = (2, 3, 1, 0)

    def offer(i):
        for part, half in pairs:
            part.send(half, 4 * i, 4 * i + 1)

    def pass_on(i):
        for part, half in pairs:
            part.wait(half, 4 * i)
            part.add(half, 1, across[i], 1, i)
            part.send(half, 4 * i + 2)
            part.wait(half, 4 * i + 1)
            part.add(half, 3, across[i], 2, i)
            part.send(half, 4 * i + 3)

    def take(part, half, i):
        part.wait(half, 4 * i + 2, 4 * i + 3)
        part.add(half, 0, across[i], 0, 4 + i, 8 + i)

    offer(0)
    offer(1)
    offer(2)
    pass_on(0)
    offer(3)
    pass_on(1)
    pass_on(2)
    midway()
    for part, half in pairs:
        take(part, half, 0)
        part.send(half, 16, 17)
    pass_on(3)
    for part, half in pairs:
        take(part, half, 1)
        part.wait(half, 17)
        part.add(half, 0, 3, 2, 12)
        part.send(half, 19)
        take(part, half, 2)
        part.wait(half, 16)
        part.add(half, 0, 1, 1, 12)
        part.send(half, 18)
    for part, half in pairs:
        take(part, half, 3)
    for part, half in pairs:
        part.wait(half, 18, 19)
        part.finish(half)


def head_probs(proj, bias, head):
    lo = head * HEAD
    queries = proj[:, lo : lo + HEAD]
    keys = proj[:, HD + lo : HD + lo + HEAD]
    scores = dot(queries, keys, ((1,), (1,))) * SCALE + bias
    shifted = jnp.exp(scores - jnp.max(scores, -1, keepdims=True))
    return shifted / jnp.sum(shifted, -1, keepdims=True)


def section_kernel(
    start_ref, layout_ref, offset_ref, mask_ref, qkv_shard, out_shard, hint_shard,
    base_ref, cot_ref, update_ref, gain_ref,
    mine_out, sum_qkv, sum_out, sum_hint,
    landed, leaving, back_landed, back_leaving, after, acc, proj, att, gproj, probs, bias_ref,
    member, permitted, own_member, own_permitted, qkv, out, hint, normed_t, att_t,
    update, slots, gs, mine, mine_rows, base_rows, part_rows, row_sum, cot,
    land_qkv, land_out, land_hint, res_qkv, res_out, res_hint,
    hop_send, hop_recv, back_send, back_recv, small_send, small_recv, start_sem, local_sem, out_sem,
    qkv_send, qkv_recv, qkv_own, out_send, out_recv, out_own, hint_send, hint_recv, hint_own,
    rqkv_send, rqkv_recv, rout_send, rout_recv, rhint_send, rhint_recv,
    term_send, term_recv, part_send, part_recv, gs_send, gs_recv, mine_send, mine_recv,
    go_sem,
):
    place = Place()
    section, core = place.section, place.core
    kept, away = place.kept, place.away
    lent = jnp.logical_not(kept)
    place.greet()
    drains = []

    def drained(condition):
        return lambda body: drains.append(lambda: pl.when(condition)(body))

    def member_copy():
        return remote(own_member, member, small_send.at[0], small_recv.at[0], place.sibling)

    def permitted_copy():
        return remote(own_permitted, permitted, small_send.at[1], small_recv.at[1], place.worker)

    def base_across():
        rows = base_ref.at[rows_of(7 - section, 32), :]
        return remote(rows, base_rows, small_send.at[2], small_recv.at[2], place.sibling)

    def base_here():
        rows = base_ref.at[rows_of(section, 32), :]
        return pltpu.make_async_copy(rows, base_rows, local_sem.at[0])

    def cot_across():
        return remote(cot_ref, cot, small_send.at[3], small_recv.at[3], place.sibling)

    def cot_here():
        return pltpu.make_async_copy(cot_ref, cot, local_sem.at[1])

    def update_across():
        return remote(update_ref, update, small_send.at[4], small_recv.at[4], place.worker)

    def update_here():
        return pltpu.make_async_copy(update_ref, update, local_sem.at[2])

    def start_copy(k):
        return pltpu.make_async_copy(
            start_ref.at[:, k * CW : (k + 1) * CW], landed.at[k], start_sem.at[k]
        )

    def start_across(k):
        return remote(
            start_ref.at[:, k * CW : (k + 1) * CW], landed.at[k],
            hop_send.at[k], hop_recv.at[k], place.sibling,
        )

    def hop(k):
        return remote(leaving.at[k], landed.at[k], hop_send.at[k], hop_recv.at[k], place.later)

    first_here = (section == 0) & kept
    first_given = (section == 7) & kept

    qkv_gather = Gather(place, qkv_shard, qkv, QKV_CUT, qkv_send, qkv_recv, qkv_own)
    out_gather = Gather(place, out_shard, out, OUT_CUT, out_send, out_recv, out_own)
    hint_gather = Gather(place, hint_shard, hint, HINT_CUT, hint_send, hint_recv, hint_own)
    start_own([qkv_gather, out_gather])

    @drained(kept)
    def _():
        member_copy().wait_send()
        base_across().wait_send()

    @drained(away)
    def _():
        permitted_copy().wait_send()

    own_member[...] = tile_members(layout_ref[...])
    own_permitted[...] = permitted_tiles(offset_ref, mask_ref)

    @pl.when(kept)
    def _():
        member_copy().start()
        base_across().start()
        base_here().start()
        member[...] = own_member[...]

    @pl.when(place.home)
    def _():
        update_here().start()
        permitted[...] = own_permitted[...]

    @pl.when(away)
    def _():
        permitted_copy().start()

    @pl.when((section == 0) & kept)
    def _():
        cot_across().start()

    @drained((section == 0) & kept)
    def _():
        cot_across().wait_send()

    @pl.when((section == 7) & kept)
    def _():
        cot_here().start()

    @pl.when(first_here)
    def _():
        for k in range(CH):
            start_copy(k).start()

    @pl.when(first_given)
    def _():
        for k in range(CH):
            start_across(k).start()

    @pl.when(core == 1)
    def _():
        pl.semaphore_wait(go_sem, 1)

    gather([qkv_gather, out_gather])

    @pl.when(core == 0)
    def _():
        pl.semaphore_signal(go_sem, inc=1, device_id=place.sibling, device_id_type=MESH)

    start_own([hint_gather])

    @pl.when(lent)
    def _():
        member_copy().wait_recv()

    @pl.when(away)
    def _():
        permitted_copy().wait_recv()

    pairs = dot(dot(member[...], permitted[...]).astype(BF16), member[...], ((1,), (1,)))
    bias_ref[...] = jnp.where(pairs > 0.5, 0.0, -1e30)

    @pl.when(core == 1)
    def _():
        update_across().start()

    @drained(away)
    def _():
        update_across().wait_send()

    @pl.when(section >= 6)
    def _():
        gather([hint_gather])

    @drained(section < 7)
    def _():
        for k in range(CH):
            hop(k).wait_send()

    squares = jnp.zeros((ROWS, 1), F32)
    for k in range(CH):
        @pl.when(first_here)
        def _():
            start_copy(k).wait()

        @pl.when(jnp.logical_not(first_here))
        def _():
            hop(k).wait_recv()

        x = landed[k]
        wide = x.astype(F32)
        squares += jnp.sum(wide * wide, -1, keepdims=True)
        for n in range(3):
            cols = slice(n * HD, (n + 1) * HD)
            part = dot(x, qkv[k * CW : (k + 1) * CW, cols])
            if k == 0:
                acc[:, cols] = part
            elif k < CH - 1:
                acc[:, cols] += part
            else:
                inverse = lax.rsqrt(squares * (1.0 / WIDTH) + 1e-06)
                proj[:, cols] = ((acc[:, cols] + part) * inverse).astype(BF16)
    bias = bias_ref[...]
    for h in range(HEADS):
        soft = head_probs(proj, bias, h)
        probs[h] = soft
        lo = 2 * HD + h * HEAD
        value = dot(soft.astype(BF16), proj[:, lo : lo + HEAD])
        att[:, h * HEAD : (h + 1) * HEAD] = value.astype(BF16)

    @pl.when(first_given)
    def _():
        for k in range(CH):
            start_across(k).wait_send()

    attended = att[...]
    for k in range(CH):
        value = landed[k].astype(F32) + dot(attended, out[:, k * CW : (k + 1) * CW])
        leaving[k] = value.astype(BF16)

        @pl.when(section < 7)
        def _():
            hop(k).start()

    @pl.when(away & (core == 0))
    def _():
        update_across().start()

    @pl.when(section < 6)
    def _():
        gather([hint_gather])

    @pl.when(away)
    def _():
        update_across().wait_recv()

    @pl.when(place.home)
    def _():
        update_here().wait()

    def along_column(by):
        other = lax.rem(section + by, 8)
        return other, at_section(other)

    def term_copy(by, half):
        other, to = along_column(by)
        cols = slice(half * 1280, (half + 1) * 1280)
        return remote(
            update.at[rows_of(other, 32), cols], slots.at[by, :, cols],
            term_send.at[by, half], term_recv.at[by, half], to,
        )

    def part_copy(owner):
        return remote(
            part_rows, gs.at[rows_of(owner, 32), :],
            part_send.at[0], part_recv.at[owner], {"z": 0, "core": 1},
        )

    def gs_copy(child, piece):
        rows = gs.at[piece * 64 : (piece + 1) * 64, :]
        to = (
            place.sibling,
            {"z": lax.rem(place.z + 3, 4)},
            {"z": lax.rem(place.z + 1, 4)},
        )[child]
        return remote(rows, rows, gs_send.at[child, piece], gs_recv.at[piece], to)

    has_child = (core == 1, (section == 7) | (section == 4), section == 7)

    def pass_down(piece):
        for child in (2, 1, 0):
            @pl.when(has_child[child])
            def _():
                gs_copy(child, piece).start()

    far_first = (4, 3, 5, 2, 6, 1, 7)

    @drained(section >= 0)
    def _():
        for by in far_first:
            for half in range(2):
                term_copy(by, half).wait_send()

    @drained(section < 7)
    def _():
        part_copy(section).wait_send()

    for child in range(3):
        @drained(has_child[child])
        def _(child=child):
            for piece in range(4):
                gs_copy(child, piece).wait_send()

    for half in range(2):
        for n in range(2):
            cols = slice(half * 1280 + n * 640, half * 1280 + (n + 1) * 640)
            value = update[:, cols].astype(F32)
            for k in range(CH):
                value += dot(leaving[k], hint[k * CW : (k + 1) * CW, cols])
            update[:, cols] = value.astype(BF16)

        @pl.when(section < 7)
        def _():
            for by in far_first:
                term_copy(by, half).start()

    @pl.when(kept)
    def _():
        base_here().wait()

    @pl.when(lent)
    def _():
        base_across().wait_recv()

    own_rows = rows_of(section, 32)
    row_sum[...] = base_rows[...].astype(F32)
    for by in (1, 2, 3, 4, 5, 6, 7):
        @pl.when(lax.rem(section + 8 - by, 8) < 7)
        def _():
            for half in range(2):
                term_copy(by, half).wait_recv()
            row_sum[...] += slots[by].astype(F32)

    @pl.when(section < 7)
    def _():
        row_sum[...] += update[own_rows, :].astype(F32)
        part_rows[...] = row_sum[...].astype(BF16)
        part_copy(section).start()
        for piece in range(4):
            gs_copy(0, piece).wait_recv()
            pass_down(piece)

    @pl.when(section == 7)
    def _():
        gs[7 * 32 :, :] = row_sum[...].astype(BF16)

        @pl.when(kept)
        def _():
            cot_here().wait()

        @pl.when(lent)
        def _():
            cot_across().wait_recv()

        gain = gain_ref[...]
        for piece in range(4):
            rows = slice(piece * 64, (piece + 1) * 64)
            for owner in (2 * piece, 2 * piece + 1):
                if owner < 7:
                    part_copy(owner).wait_recv()
            summed = gs[rows, :].astype(F32) + update[rows, :].astype(F32)
            inverse = lax.rsqrt(jnp.mean(summed * summed, -1, keepdims=True) + 1e-06)
            grad_normed = cot[rows, :].astype(F32) * gain
            slope = inverse * inverse * inverse * jnp.mean(grad_normed * summed, -1, keepdims=True)
            gs[rows, :] = (inverse * grad_normed - summed * slope).astype(BF16)
            pass_down(piece)
        row_sum[...] += update[7 * 32 :, :].astype(F32)

    def mine_copy(by, kind, owner):
        rows = mine.at[rows_of(owner, 32), :]
        to = {"z": lax.rem(place.z + by, 4), "core": place.xlo}
        return remote(mine_rows, rows, mine_send.at[by], mine_recv.at[by, kind], to)

    def mine_across():
        to = {"xlo": 1 - place.xlo}
        return remote(mine, mine, mine_send.at[4], mine_recv.at[4, 0], to)

    @drained(kept)
    def _():
        for by in (2, 1, 3):
            mine_copy(by, 0, section).wait_send()
        mine_across().wait_send()

    @drained(lent)
    def _():
        for by in (2, 1, 3, 0):
            mine_copy(by, 1, section).wait_send()

    def share_summed():
        @pl.when(section < 7)
        def _():
            last = lax.rem(section + 1, 8)
            for half in range(2):
                cols = slice(half * 1280, (half + 1) * 1280)
                remote(
                    update.at[own_rows, cols], slots.at[last, :, cols],
                    term_send.at[last, half], term_recv.at[last, half], place.sibling,
                ).wait_recv()
            row_sum[...] += slots[last].astype(F32)

        mine_rows[...] = row_sum[...].astype(BF16)

        @pl.when(kept)
        def _():
            mine[own_rows, :] = mine_rows[...]
            for by in (2, 1, 3):
                mine_copy(by, 0, section).start()

        @pl.when(lent)
        def _():
            for by in (2, 1, 3, 0):
                mine_copy(by, 1, section).start()

    def collect_summed():
        @pl.when(kept)
        def _():
            for by in range(4):
                for kind in range(2):
                    if (by, kind) != (0, 0):
                        z = lax.rem(place.z + 4 - by, 4)
                        owner = section_at(z, core if kind == 0 else 1 - core)
                        mine_copy(by, kind, owner).wait_recv()
            mine_across().start()

    hint_gather.wait_sent()
    grad_sum = gs[...]
    for k in range(CH):
        acc[:, k * CW : (k + 1) * CW] = dot(grad_sum, hint[k * CW : (k + 1) * CW, :], ((1,), (1,)))

    red_qkv = Reduce(place, qkv, land_qkv, res_qkv, QKV_CUT, rqkv_send, rqkv_recv)
    red_out = Reduce(place, out, land_out, res_out, OUT_CUT, rout_send, rout_recv)
    red_hint = Reduce(place, hint, land_hint, res_hint, HINT_CUT, rhint_send, rhint_recv)

    mine_keep = pltpu.make_async_copy(mine, mine_out, out_sem.at[3])

    def hint_grads():
        for m in range(CH):
            for n in range(FEAT // 512):
                cols = slice(n * 512, (n + 1) * 512)
                rows = slice(m * CW, (m + 1) * CW)
                hint[rows, cols] = dot(leaving[m], gs[:, cols], ((0,), (0,))).astype(BF16)

    def transposes():
        squares = jnp.zeros((ROWS, 1), F32)
        for k in range(CH):
            wide = landed[k].astype(F32)
            squares += jnp.sum(wide * wide, -1, keepdims=True)
        inverse = lax.rsqrt(squares * (1.0 / WIDTH) + 1e-06)
        for k in range(CH):
            normed = (landed[k].astype(F32) * inverse).astype(BF16)
            normed_t[k * CW : (k + 1) * CW, :] = normed.T
        for k in range(HD // CW):
            att_t[k * CW : (k + 1) * CW, :] = att[:, k * CW : (k + 1) * CW].T

    hint_early = section <= 4

    def let_sibling():
        @pl.when(section == 4)
        def _():
            pl.semaphore_signal(go_sem, inc=1, device_id=place.sibling, device_id_type=MESH)

    @pl.when(hint_early)
    def _():
        hint_grads()

        @pl.when(section == 3)
        def _():
            pl.semaphore_wait(go_sem, 1)

        reduce([red_hint], let_sibling)

    @pl.when(core == 0)
    def _():
        transposes()
        share_summed()

    @pl.when(section < 3)
    def _():
        collect_summed()

    @drained(section > 0)
    def _():
        for k in range(CH):
            back(k).wait_send()

    squares = jnp.zeros((ROWS, 1), F32)
    for k in range(CH):
        wide = landed[k].astype(F32)
        squares += jnp.sum(wide * wide, -1, keepdims=True)
    inverse = lax.rsqrt(squares * (1.0 / WIDTH) + 1e-06)

    def back(k):
        return remote(
            back_leaving.at[k], back_landed.at[k], back_send.at[k], back_recv.at[k], place.earlier
        )

    @pl.when(section == 7)
    def _():
        for k in range(CH):
            back_landed[k] = jnp.zeros((ROWS, CW), BF16)

    grad_att_cols = slice(WIDTH, WIDTH + HD)
    for k in range(CH):
        @pl.when(section < 7)
        def _():
            back(k).wait_recv()

        grad = (back_landed[k].astype(F32) + acc[:, k * CW : (k + 1) * CW]).astype(BF16)
        after[k] = grad
        part = dot(grad, out[:, k * CW : (k + 1) * CW], ((1,), (1,)))
        if k == 0:
            acc[:, grad_att_cols] = part
        else:
            acc[:, grad_att_cols] += part
    through = jnp.zeros((ROWS, 1), F32)
    for h in range(HEADS):
        lo = h * HEAD
        grad_att = acc[:, WIDTH + lo : WIDTH + lo + HEAD].astype(BF16)
        queries = proj[:, lo : lo + HEAD]
        keys = proj[:, HD + lo : HD + lo + HEAD]
        values = proj[:, 2 * HD + lo : 2 * HD + lo + HEAD]
        soft = probs[h]
        grad_probs = dot(grad_att, values, ((1,), (1,)))
        grad_values = dot(soft.astype(BF16), grad_att, ((0,), (0,))).astype(BF16)
        total = jnp.sum(grad_probs * soft, -1, keepdims=True)
        grad_scores = (soft * (grad_probs - total) * SCALE).astype(BF16)
        grad_queries = dot(grad_scores, keys).astype(BF16)
        grad_keys = dot(grad_scores, queries, ((0,), (0,))).astype(BF16)
        for n, (grad, value) in enumerate(
            ((grad_queries, queries), (grad_keys, keys), (grad_values, values))
        ):
            gproj[:, n * HD + lo : n * HD + lo + HEAD] = grad
            through += jnp.sum(grad.astype(F32) * value.astype(F32), -1, keepdims=True)
    slope = inverse * inverse * through * (1.0 / WIDTH)

    @pl.when(section > 0)
    def _():
        grad_proj = gproj[...]
        for k in range(CH):
            grad_normed = dot(grad_proj, qkv[k * CW : (k + 1) * CW, :], ((1,), (1,)))
            value = after[k].astype(F32) + inverse * grad_normed - landed[k].astype(F32) * slope
            back_leaving[k] = value.astype(BF16)
            back(k).start()

    @pl.when(section == 7)
    def _():
        for half in range(2):
            for by in far_first:
                term_copy(by, half).start()

    @pl.when(core == 1)
    def _():
        transposes()
        share_summed()

    @pl.when((section == 3) | (section == 4))
    def _():
        collect_summed()

    qkv_gather.wait_sent()
    out_gather.wait_sent()
    for m in range(CH):
        rows = slice(m * CW, (m + 1) * CW)
        for n in range(3):
            cols = slice(n * HD, (n + 1) * HD)
            qkv[rows, cols] = dot(normed_t[rows, :], gproj[:, cols]).astype(BF16)
    for m in range(HD // CW):
        rows = slice(m * CW, (m + 1) * CW)
        for n in range(CH):
            out[rows, n * CW : (n + 1) * CW] = dot(att_t[rows, :], after[n]).astype(BF16)
    @pl.when(hint_early)
    def _():
        reduce([red_qkv, red_out])

    @pl.when(jnp.logical_not(hint_early))
    def _():
        hint_grads()
        reduce([red_qkv, red_out, red_hint])

    @pl.when(section >= 5)
    def _():
        collect_summed()

    @pl.when(lent)
    def _():
        mine_across().wait_recv()

    mine_keep.start()
    keeps = [
        red.put(ref, out_sem.at[i])
        for i, (red, ref) in enumerate(((red_qkv, sum_qkv), (red_out, sum_out), (red_hint, sum_hint)))
    ]
    for red in (red_qkv, red_out, red_hint):
        red.wait_sent()
    mine_keep.wait()
    for keep in keeps:
        keep()
    for drain in drains:
        drain()


def scale_kernel(
    mine_ref, gain_ref, qkv_ref, out_ref, hint_ref, features_out, qkv_out, out_out, hint_out,
    mine, qkv, out, hint, features, grad_qkv, grad_out, grad_hint, in_sem, out_sem,
):
    ins = ((mine_ref, mine), (qkv_ref, qkv), (out_ref, out), (hint_ref, hint))
    outs = (
        (features, features_out), (grad_qkv, qkv_out), (grad_out, out_out), (grad_hint, hint_out)
    )
    reads = [pltpu.make_async_copy(*pair, in_sem.at[i]) for i, pair in enumerate(ins)]
    writes = [pltpu.make_async_copy(*pair, out_sem.at[i]) for i, pair in enumerate(outs)]
    for read in reads:
        read.start()
    gain = gain_ref[...]
    for i in range(4):
        reads[i].wait()
        if i == 0:
            wide = mine[...].astype(F32)
            inverse = lax.rsqrt(jnp.mean(wide * wide, -1, keepdims=True) + 1e-06)
            features[...] = wide * inverse * gain
        else:
            outs[i][0][...] = ins[i][1][...].astype(F32) * 4096.0 ** (-0.5)
        writes[i].start()
    for write in writes:
        write.wait()


def dma_sems(*shape):
    return pltpu.SemaphoreType.DMA(shape)


def kernel_call(kernel, ins, outs, scratch, collective_id, flops):
    spaces = {"v": pltpu.VMEM, "a": pl.ANY, "s": pltpu.SMEM}
    return pl.pallas_call(
        kernel,
        out_shape=[shape for shape, _ in outs],
        in_specs=[pl.BlockSpec(memory_space=spaces[kind]) for kind in ins],
        out_specs=[pl.BlockSpec(memory_space=spaces[kind]) for _, kind in outs],
        scratch_shapes=scratch,
        compiler_params=pltpu.CompilerParams(
            collective_id=collective_id, has_side_effects=True, vmem_limit_bytes=VMEM_LIMIT
        ),
        cost_estimate=pl.CostEstimate(flops=flops, bytes_accessed=12_000_000, transcendentals=0),
    )


def tile_members(layout):
    tokens = lax.broadcasted_iota(jnp.int32, (ROWS, ROWS), 0)
    positions = lax.broadcasted_iota(jnp.int32, (ROWS, ROWS), 1)
    tiles = jnp.where(layout == tokens, (positions // TILE).astype(F32), 0.0)
    tile_of = jnp.sum(tiles, -1, keepdims=True)
    columns = lax.broadcasted_iota(jnp.int32, (ROWS, 128), 1).astype(F32)
    return jnp.where(tile_of == columns, 1.0, 0.0).astype(BF16)


def permitted_tiles(offset, mask):
    row = lax.broadcasted_iota(jnp.int32, (128, 128), 0)
    col = lax.broadcasted_iota(jnp.int32, (128, 128), 1)
    found = jnp.where(row == col, 1, 0)
    for i in range(4):
        for j in range(4):
            if i != j:
                near = jnp.abs(j - i - offset[0, i]) <= 1
                value = jnp.where(near & (mask[0, i, j] == 1), 1, 0)
                found = jnp.where((row == i) & (col == j), value, found)
    return found.astype(F32).astype(BF16)


def shape_of(*dims, dtype=BF16):
    return jax.ShapeDtypeStruct(dims, dtype)


def shards(
    control_in, base_in, base_update, out_gain, cotangent,
    w_qkv, w_out, w_hint, window_offset, tile_mask, token_layout,
):
    chunks = (CH, ROWS, CW)
    gain = out_gain[None]
    mine, sum_qkv, sum_out, sum_hint = kernel_call(
        section_kernel,
        "avssaaaaaav",
        [
            (shape_of(ROWS, FEAT), "a"),
            (shape_of(96, QKV), "a"),
            (shape_of(48, WIDTH), "a"),
            (shape_of(96, FEAT), "a"),
        ],
        [
            *[pltpu.VMEM(chunks, BF16)] * 5,
            pltpu.VMEM((ROWS, QKV), F32),
            pltpu.VMEM((ROWS, QKV), BF16),
            pltpu.VMEM((ROWS, HD), BF16),
            pltpu.VMEM((ROWS, QKV), BF16),
            pltpu.VMEM((HEADS, ROWS, ROWS), F32),
            pltpu.VMEM((ROWS, ROWS), F32),
            *[pltpu.VMEM((ROWS, 128), BF16), pltpu.VMEM((128, 128), BF16)] * 2,
            pltpu.VMEM((WIDTH, QKV), BF16),
            pltpu.VMEM((HD, WIDTH), BF16),
            pltpu.VMEM((WIDTH, FEAT), BF16),
            pltpu.VMEM((WIDTH, ROWS), BF16),
            pltpu.VMEM((HD, ROWS), BF16),
            pltpu.VMEM((ROWS, FEAT), BF16),
            pltpu.VMEM((8, 32, FEAT), BF16),
            pltpu.VMEM((ROWS, FEAT), BF16),
            pltpu.VMEM((ROWS, FEAT), BF16),
            *[pltpu.VMEM((32, FEAT), BF16)] * 3,
            pltpu.VMEM((32, FEAT), F32),
            pltpu.VMEM((ROWS, FEAT), BF16),
            pltpu.VMEM((2, 15, 96, QKV // 2), BF16),
            pltpu.VMEM((2, 15, 48, WIDTH // 2), BF16),
            pltpu.VMEM((2, 15, 96, FEAT // 2), BF16),
            pltpu.VMEM((96, QKV), BF16),
            pltpu.VMEM((48, WIDTH), BF16),
            pltpu.VMEM((96, FEAT), BF16),
            *[dma_sems(CH)] * 4,
            dma_sems(5), dma_sems(5), dma_sems(CH), dma_sems(3), dma_sems(4),
            *[dma_sems(2, 21), dma_sems(2, 21), dma_sems(2)] * 3,
            *[dma_sems(2, 21)] * 6,
            dma_sems(8, 2), dma_sems(8, 2), dma_sems(1), dma_sems(7), dma_sems(3, 4), dma_sems(4),
            dma_sems(5), dma_sems(5, 2),
            pltpu.SemaphoreType.REGULAR,
        ],
        1,
        100_000_000_000,
    )(
        control_in, token_layout, window_offset, tile_mask, w_qkv[0], w_out[0], w_hint[0],
        base_in, cotangent, base_update[0], gain,
    )
    features, grad_qkv, grad_out, grad_hint = pl.pallas_call(
        scale_kernel,
        out_shape=[
            shape_of(ROWS, FEAT, dtype=F32),
            shape_of(96, QKV, dtype=F32),
            shape_of(48, WIDTH, dtype=F32),
            shape_of(96, FEAT, dtype=F32),
        ],
        in_specs=[
            pl.BlockSpec(memory_space=pltpu.VMEM if i == 1 else pl.ANY) for i in range(5)
        ],
        out_specs=[pl.BlockSpec(memory_space=pl.ANY)] * 4,
        scratch_shapes=[
            pltpu.VMEM(dims, dtype)
            for dtype in (BF16, F32)
            for dims in ((ROWS, FEAT), (96, QKV), (48, WIDTH), (96, FEAT))
        ]
        + [dma_sems(4), dma_sems(4)],
        compiler_params=pltpu.CompilerParams(vmem_limit_bytes=VMEM_LIMIT),
    )(mine, gain, sum_qkv, sum_out, sum_hint)
    return features, grad_qkv[None], grad_out[None], grad_hint[None]


def solution(mesh):
    parts = jax.sharding.Mesh(
        mesh.devices.reshape(2, 4, 2, 4, 2), ("xlo", "z", "xhi", "y", "core")
    )
    segment = ("xlo", "z")
    dp = ("xhi", "y", "core")
    by_rows = P(dp, None)
    by_both = P(segment, dp, None)
    placed = (
        by_rows, by_rows, by_both, P(), by_rows, by_both, by_both, by_both,
        P(segment, None), P(segment, None, None), by_rows,
    )
    return jax.shard_map(
        shards,
        mesh=parts,
        in_specs=placed,
        out_specs=(by_rows, by_both, by_both, by_both),
        check_vma=False,
    )
```

```python
import functools

import jax
import jax.numpy as jnp
from jax import lax
from jax.experimental import pallas as pl
from jax.experimental.pallas import tpu as pltpu
from jax.sharding import PartitionSpec as P

HEADS = 6
HEAD = 128
TILE = 64
ROWS = 256
WIDTH = 1536
FEAT = 2560
HD = HEADS * HEAD
QKV = 3 * HD
CW = 256
CH = WIDTH // CW
SCALE = HEAD ** (-0.5)
MESH = pl.DeviceIdType.MESH
VMEM_LIMIT = 60 * 1024 * 1024
F32 = jnp.float32
BF16 = jnp.bfloat16
QKV_CUT = (96, ((0, 640, 1152), (1152, 1792, 2304)))
OUT_CUT = (48, ((0, 384, 768), (768, 1152, 1536)))
HINT_CUT = (96, ((0, 640, 1280), (1280, 1920, 2560)))


def dot(a, b, dims=((1,), (0,))):
    return lax.dot_general(a, b, (dims, ((), ())), preferred_element_type=F32)


def at_section(section):
    core = section // 4
    return {"z": section + core * (7 - 2 * section), "core": core}


def section_at(z, core):
    return z + core * (7 - 2 * z)


class Place:
    def __init__(self):
        self.xlo, self.z, self.xhi, self.y, self.core = (
            lax.axis_index(name) for name in ("xlo", "z", "xhi", "y", "core")
        )
        self.x = 2 * self.xhi + self.xlo
        self.section = section_at(self.z, self.core)
        self.later = at_section(lax.rem(self.section + 1, 8))
        self.earlier = at_section(lax.rem(self.section + 7, 8))
        self.sibling = {"core": 1 - self.core}
        self.kept = self.xlo == self.core
        self.home = (self.xlo == 0) & (self.core == 0)
        self.away = jnp.logical_not(self.home)
        self.worker = {
            "xlo": self.core,
            "z": self.z + self.xlo * (3 - 2 * self.z),
            "core": self.xlo,
        }
        self.owner = {
            "xlo": self.core,
            "z": self.z + self.core * (3 - 2 * self.z),
            "core": self.xlo,
        }

    def along_x(self, by):
        x = lax.rem(self.x + by, 4)
        return {"xhi": x // 2, "xlo": lax.rem(x, 2)}

    def along_y(self, by):
        return {"y": lax.rem(self.y + by, 4)}

    def neighbour(self, half, ring, by):
        return self.along_y(by) if half == ring else self.along_x(by)

    def block(self, half, first, second):
        dx, dy = (second, first) if half == 0 else (first, second)
        x = lax.rem(self.x + dx, 4)
        y = lax.rem(self.y + dy, 4)
        return (x // 2) * 8 + y * 2 + lax.rem(x, 2)

    def greet(self):
        others = [self.along_x(1), self.along_x(3), self.along_y(1), self.along_y(3)]
        others += [at_section(lax.rem(self.section + by, 8)) for by in range(1, 8)]
        barrier = pltpu.get_barrier_semaphore()
        for other in others:
            pl.semaphore_signal(barrier, inc=1, device_id=other, device_id_type=MESH)

        @pl.when(self.away)
        def _():
            for other in (self.worker, self.owner):
                pl.semaphore_signal(barrier, inc=1, device_id=other, device_id_type=MESH)
            pl.semaphore_wait(barrier, len(others) + 2)

        @pl.when(self.home)
        def _():
            pl.semaphore_wait(barrier, len(others))


def remote(src, dst, send_sem, recv_sem, to):
    return pltpu.make_async_remote_copy(
        src_ref=src, dst_ref=dst, send_sem=send_sem, recv_sem=recv_sem,
        device_id=to, device_id_type=MESH,
    )


def rows_of(index, rows):
    return pl.ds(pl.multiple_of(index * rows, rows), rows)


class Gather:
    def __init__(self, place, shard, full, cut, send_sem, recv_sem, own_sem):
        self.place, self.shard, self.full = place, shard, full
        self.rows, self.cuts = cut
        self.send_sem, self.recv_sem, self.own_sem = send_sem, recv_sem, own_sem

    def region(self, half, first, second, part):
        lo, mid, hi = self.cuts[half]
        lo, hi = ((lo, hi), (lo, mid), (mid, hi))[part]
        index = self.place.block(half, first, second)
        return self.full.at[rows_of(index, self.rows), lo:hi]

    def copy(self, half, slot, first, second, part, ring=0, by=1):
        ref = self.region(half, first, second, part)
        return remote(
            ref, ref, self.send_sem.at[half, slot], self.recv_sem.at[half, slot],
            self.place.neighbour(half, ring, by),
        )

    def own(self, half):
        lo, _, hi = self.cuts[half]
        return self.shard.at[:, lo:hi], self.region(half, 0, 0, 0)

    def moved_own(self, half, index=None):
        src, dst = self.own(half)
        if index is not None:
            lo, _, hi = self.cuts[half]
            dst = self.full.at[rows_of(index, self.rows), lo:hi]
        return remote(
            src, dst, self.send_sem.at[half, 20], self.recv_sem.at[half, 20], self.place.worker
        )

    def kept_own(self, half):
        src, dst = self.own(half)
        return pltpu.make_async_copy(src, dst, self.own_sem.at[half])

    def sends(self, half):
        yield 0, (0, 0), 0, 0, 1
        yield 1, (0, 0), 0, 0, 3
        yield 2, (3, 0), 1, 0, 1
        yield 3, (1, 0), 2, 0, 3
        for j, first in enumerate((0, 3, 1, 2)):
            yield 4 + 4 * j, (first, 0), 0, 1, 1
            yield 5 + 4 * j, (first, 0), 0, 1, 3
            yield 6 + 4 * j, (first, 3), 1, 1, 1
            yield 7 + 4 * j, (first, 1), 2, 1, 3

    def send(self, half, *slots):
        plan = {entry[0]: entry for entry in self.sends(half)}
        for slot in slots:
            _, block, part, ring, by = plan[slot]
            self.copy(half, slot, *block, part, ring, by).start()

    def wait(self, half, *slots):
        plan = {0: (3, 0, 0), 1: (1, 0, 0), 2: (2, 0, 1), 3: (2, 0, 2)}
        for j, first in enumerate((0, 3, 1, 2)):
            plan |= {
                4 + 4 * j: (first, 3, 0), 5 + 4 * j: (first, 1, 0),
                6 + 4 * j: (first, 2, 1), 7 + 4 * j: (first, 2, 2),
            }
        for slot in slots:
            self.copy(half, slot, *plan[slot]).wait_recv()

    def start_own(self, half):
        place = self.place

        @pl.when(place.away)
        def _():
            self.moved_own(half, place.xhi * 8 + place.y * 2 + place.core).start()

        @pl.when(place.home)
        def _():
            self.kept_own(half).start()

    def wait_own(self, half):
        @pl.when(self.place.away)
        def _():
            self.moved_own(half).wait_recv()

        @pl.when(self.place.home)
        def _():
            self.kept_own(half).wait()

    def wait_sent(self):
        for half in range(2):
            for slot, block, part, ring, by in self.sends(half):
                self.copy(half, slot, *block, part, ring, by).wait_send()

            @pl.when(self.place.away)
            def _():
                self.moved_own(half).wait_send()


def start_own(parts):
    for part in parts:
        for half in range(2):
            part.start_own(half)


def gather(parts):
    pairs = [(part, half) for part in parts for half in range(2)]
    for part, half in pairs:
        part.wait_own(half)
        part.send(half, 0, 1, 4, 5)
    for part, half in pairs:
        part.wait(half, 0)
        part.send(half, 2, 8, 9)
        part.wait(half, 1)
        part.send(half, 3, 12, 13)
    for part, half in pairs:
        part.wait(half, 4)
        part.send(half, 6)
        part.wait(half, 5)
        part.send(half, 7)
    for part, half in pairs:
        part.wait(half, 2, 3)
        part.send(half, 16, 17)
    for j in (1, 2, 3):
        for part, half in pairs:
            part.wait(half, 4 + 4 * j)
            part.send(half, 6 + 4 * j)
            part.wait(half, 5 + 4 * j)
            part.send(half, 7 + 4 * j)
    for part, half in pairs:
        for j in range(4):
            part.wait(half, 6 + 4 * j, 7 + 4 * j)


class Reduce:
    def __init__(self, place, grad, landing, result, cut, send_sem, recv_sem):
        self.place, self.grad, self.landing, self.result = place, grad, landing, result
        self.rows, self.cuts = cut
        self.send_sem, self.recv_sem = send_sem, recv_sem

    def columns(self, half, part):
        lo, mid, hi = self.cuts[half]
        return ((lo, hi), (lo, mid), (mid, hi))[part]

    def region(self, half, first, second, part):
        lo, hi = self.columns(half, part)
        return self.grad.at[rows_of(self.place.block(half, first, second), self.rows), lo:hi]

    def slot_ref(self, half, slot, part):
        base = self.cuts[half][0]
        lo, hi = self.columns(half, part)
        return self.landing.at[half, slot, :, lo - base : hi - base]

    def copy(self, half, sem, first, second, part, slot, ring=0, by=1):
        return remote(
            self.region(half, first, second, part), self.slot_ref(half, slot, part),
            self.send_sem.at[half, sem], self.recv_sem.at[half, sem],
            self.place.neighbour(half, ring, by),
        )

    def plan(self):
        found = {}
        for i, second in enumerate((2, 3, 1, 0)):
            found[4 * i] = ((2, second), 1, i, 0, 1)
            found[4 * i + 1] = ((2, second), 2, i, 0, 3)
            found[4 * i + 2] = ((1, second), 0, 4 + i, 0, 1)
            found[4 * i + 3] = ((3, second), 0, 8 + i, 0, 3)
        found[16] = ((0, 2), 1, 12, 1, 1)
        found[17] = ((0, 2), 2, 12, 1, 3)
        found[18] = ((0, 1), 0, 13, 1, 1)
        found[19] = ((0, 3), 0, 14, 1, 3)
        return found

    def send(self, half, *sems):
        for sem in sems:
            block, part, slot, ring, by = self.plan()[sem]
            self.copy(half, sem, *block, part, slot, ring, by).start()

    def wait(self, half, *sems):
        for sem in sems:
            block, part, slot, ring, by = self.plan()[sem]
            self.copy(half, sem, *block, part, slot, ring, by).wait_recv()

    def wait_sent(self):
        for half in range(2):
            for sem, (block, part, slot, ring, by) in self.plan().items():
                self.copy(half, sem, *block, part, slot, ring, by).wait_send()

    def add(self, half, first, second, part, *slots):
        ref = self.region(half, first, second, part)
        value = ref[...].astype(F32)
        for slot in slots:
            value += self.slot_ref(half, slot, part)[...].astype(F32)
        ref[...] = value.astype(BF16)

    def finish(self, half):
        self.add(half, 0, 0, 0, 13, 14)

        @pl.when(self.place.away)
        def _():
            self.moved(half).start()

    def moved(self, half):
        lo, hi = self.columns(half, 0)
        return remote(
            self.region(half, 0, 0, 0), self.result.at[:, lo:hi],
            self.send_sem.at[half, 20], self.recv_sem.at[half, 20], self.place.owner,
        )

    def put(self, out_ref, sem):
        here = pltpu.make_async_copy(self.region_rows(), out_ref, sem)
        across = pltpu.make_async_copy(self.result, out_ref, sem)

        @pl.when(self.place.away)
        def _():
            for half in range(2):
                self.moved(half).wait()
            across.start()

        @pl.when(self.place.home)
        def _():
            here.start()

        def wait():
            @pl.when(self.place.away)
            def _():
                across.wait()

            @pl.when(self.place.home)
            def _():
                here.wait()

        return wait

    def region_rows(self):
        return self.grad.at[rows_of(self.place.block(0, 0, 0), self.rows), :]


def reduce(parts, midway=lambda: None):
    pairs = [(part, half) for part in parts for half in range(2)]
    across = (2, 3, 1, 0)

    def offer(i):
        for part, half in pairs:
            part.send(half, 4 * i, 4 * i + 1)

    def pass_on(i):
        for part, half in pairs:
            part.wait(half, 4 * i)
            part.add(half, 1, across[i], 1, i)
            part.send(half, 4 * i + 2)
            part.wait(half, 4 * i + 1)
            part.add(half, 3, across[i], 2, i)
            part.send(half, 4 * i + 3)

    def take(part, half, i):
        part.wait(half, 4 * i + 2, 4 * i + 3)
        part.add(half, 0, across[i], 0, 4 + i, 8 + i)

    offer(0)
    offer(1)
    offer(2)
    pass_on(0)
    offer(3)
    pass_on(1)
    pass_on(2)
    midway()
    for part, half in pairs:
        take(part, half, 0)
        part.send(half, 16, 17)
    pass_on(3)
    for part, half in pairs:
        take(part, half, 1)
        part.wait(half, 17)
        part.add(half, 0, 3, 2, 12)
        part.send(half, 19)
        take(part, half, 2)
        part.wait(half, 16)
        part.add(half, 0, 1, 1, 12)
        part.send(half, 18)
    for part, half in pairs:
        take(part, half, 3)
    for part, half in pairs:
        part.wait(half, 18, 19)
        part.finish(half)


def head_probs(proj, bias, head):
    lo = head * HEAD
    queries = proj[:, lo : lo + HEAD]
    keys = proj[:, HD + lo : HD + lo + HEAD]
    scores = dot(queries, keys, ((1,), (1,))) * SCALE + bias
    shifted = jnp.exp(scores - jnp.max(scores, -1, keepdims=True))
    return shifted / jnp.sum(shifted, -1, keepdims=True)


def section_kernel(
    start_ref, layout_ref, offset_ref, mask_ref, qkv_shard, out_shard, hint_shard,
    base_ref, cot_ref, update_ref, gain_ref,
    mine_out, sum_qkv, sum_out, sum_hint,
    landed, leaving, back_landed, back_leaving, after, acc, proj, att, gproj, probs, bias_ref,
    member, permitted, own_member, own_permitted, qkv, out, hint, normed_t, att_t,
    update, slots, gs, mine, mine_rows, base_rows, part_rows, row_sum, cot,
    land_qkv, land_out, land_hint, res_qkv, res_out, res_hint,
    hop_send, hop_recv, back_send, back_recv, small_send, small_recv, start_sem, local_sem, out_sem,
    qkv_send, qkv_recv, qkv_own, out_send, out_recv, out_own, hint_send, hint_recv, hint_own,
    rqkv_send, rqkv_recv, rout_send, rout_recv, rhint_send, rhint_recv,
    term_send, term_recv, part_send, part_recv, gs_send, gs_recv, mine_send, mine_recv,
    go_sem,
):
    place = Place()
    section, core = place.section, place.core
    kept, away = place.kept, place.away
    lent = jnp.logical_not(kept)
    place.greet()
    drains = []

    def drained(condition):
        return lambda body: drains.append(lambda: pl.when(condition)(body))

    def member_copy():
        return remote(own_member, member, small_send.at[0], small_recv.at[0], place.sibling)

    def permitted_copy():
        return remote(own_permitted, permitted, small_send.at[1], small_recv.at[1], place.worker)

    def base_across():
        rows = base_ref.at[rows_of(7 - section, 32), :]
        return remote(rows, base_rows, small_send.at[2], small_recv.at[2], place.sibling)

    def base_here():
        rows = base_ref.at[rows_of(section, 32), :]
        return pltpu.make_async_copy(rows, base_rows, local_sem.at[0])

    def cot_across():
        return remote(cot_ref, cot, small_send.at[3], small_recv.at[3], place.sibling)

    def cot_here():
        return pltpu.make_async_copy(cot_ref, cot, local_sem.at[1])

    def update_across():
        return remote(update_ref, update, small_send.at[4], small_recv.at[4], place.worker)

    def update_here():
        return pltpu.make_async_copy(update_ref, update, local_sem.at[2])

    def start_copy(k):
        return pltpu.make_async_copy(
            start_ref.at[:, k * CW : (k + 1) * CW], landed.at[k], start_sem.at[k]
        )

    def start_across(k):
        return remote(
            start_ref.at[:, k * CW : (k + 1) * CW], landed.at[k],
            hop_send.at[k], hop_recv.at[k], place.sibling,
        )

    def hop(k):
        return remote(leaving.at[k], landed.at[k], hop_send.at[k], hop_recv.at[k], place.later)

    first_here = (section == 0) & kept
    first_given = (section == 7) & kept

    qkv_gather = Gather(place, qkv_shard, qkv, QKV_CUT, qkv_send, qkv_recv, qkv_own)
    out_gather = Gather(place, out_shard, out, OUT_CUT, out_send, out_recv, out_own)
    hint_gather = Gather(place, hint_shard, hint, HINT_CUT, hint_send, hint_recv, hint_own)
    start_own([qkv_gather, out_gather])

    @drained(kept)
    def _():
        member_copy().wait_send()
        base_across().wait_send()

    @drained(away)
    def _():
        permitted_copy().wait_send()

    own_member[...] = tile_members(layout_ref[...])
    own_permitted[...] = permitted_tiles(offset_ref, mask_ref)

    @pl.when(kept)
    def _():
        member_copy().start()
        base_across().start()
        base_here().start()
        member[...] = own_member[...]

    @pl.when(place.home)
    def _():
        update_here().start()
        permitted[...] = own_permitted[...]

    @pl.when(away)
    def _():
        permitted_copy().start()

    @pl.when((section == 0) & kept)
    def _():
        cot_across().start()

    @drained((section == 0) & kept)
    def _():
        cot_across().wait_send()

    @pl.when((section == 7) & kept)
    def _():
        cot_here().start()

    @pl.when(first_here)
    def _():
        for k in range(CH):
            start_copy(k).start()

    @pl.when(first_given)
    def _():
        for k in range(CH):
            start_across(k).start()

    @pl.when(core == 1)
    def _():
        pl.semaphore_wait(go_sem, 1)

    gather([qkv_gather, out_gather])

    @pl.when(core == 0)
    def _():
        pl.semaphore_signal(go_sem, inc=1, device_id=place.sibling, device_id_type=MESH)

    start_own([hint_gather])

    @pl.when(lent)
    def _():
        member_copy().wait_recv()

    @pl.when(away)
    def _():
        permitted_copy().wait_recv()

    pairs = dot(dot(member[...], permitted[...]).astype(BF16), member[...], ((1,), (1,)))
    bias_ref[...] = jnp.where(pairs > 0.5, 0.0, -1e30)

    @pl.when(core == 1)
    def _():
        update_across().start()

    @drained(away)
    def _():
        update_across().wait_send()

    @pl.when(section >= 6)
    def _():
        gather([hint_gather])

    @drained(section < 7)
    def _():
        for k in range(CH):
            hop(k).wait_send()

    squares = jnp.zeros((ROWS, 1), F32)
    for k in range(CH):
        @pl.when(first_here)
        def _():
            start_copy(k).wait()

        @pl.when(jnp.logical_not(first_here))
        def _():
            hop(k).wait_recv()

        x = landed[k]
        wide = x.astype(F32)
        squares += jnp.sum(wide * wide, -1, keepdims=True)
        for n in range(3):
            cols = slice(n * HD, (n + 1) * HD)
            part = dot(x, qkv[k * CW : (k + 1) * CW, cols])
            if k == 0:
                acc[:, cols] = part
            elif k < CH - 1:
                acc[:, cols] += part
            else:
                inverse = lax.rsqrt(squares * (1.0 / WIDTH) + 1e-06)
                proj[:, cols] = ((acc[:, cols] + part) * inverse).astype(BF16)
    bias = bias_ref[...]
    for h in range(HEADS):
        soft = head_probs(proj, bias, h)
        probs[h] = soft
        lo = 2 * HD + h * HEAD
        value = dot(soft.astype(BF16), proj[:, lo : lo + HEAD])
        att[:, h * HEAD : (h + 1) * HEAD] = value.astype(BF16)

    @pl.when(first_given)
    def _():
        for k in range(CH):
            start_across(k).wait_send()

    attended = att[...]
    for k in range(CH):
        value = landed[k].astype(F32) + dot(attended, out[:, k * CW : (k + 1) * CW])
        leaving[k] = value.astype(BF16)

        @pl.when(section < 7)
        def _():
            hop(k).start()

    @pl.when(away & (core == 0))
    def _():
        update_across().start()

    @pl.when(section < 6)
    def _():
        gather([hint_gather])

    @pl.when(away)
    def _():
        update_across().wait_recv()

    @pl.when(place.home)
    def _():
        update_here().wait()

    def along_column(by):
        other = lax.rem(section + by, 8)
        return other, at_section(other)

    def term_copy(by, half):
        other, to = along_column(by)
        cols = slice(half * 1280, (half + 1) * 1280)
        return remote(
            update.at[rows_of(other, 32), cols], slots.at[by, :, cols],
            term_send.at[by, half], term_recv.at[by, half], to,
        )

    def part_copy(owner):
        return remote(
            part_rows, gs.at[rows_of(owner, 32), :],
            part_send.at[0], part_recv.at[owner], {"z": 0, "core": 1},
        )

    def gs_copy(child, piece):
        rows = gs.at[piece * 64 : (piece + 1) * 64, :]
        to = (
            place.sibling,
            {"z": lax.rem(place.z + 3, 4)},
            {"z": lax.rem(place.z + 1, 4)},
        )[child]
        return remote(rows, rows, gs_send.at[child, piece], gs_recv.at[piece], to)

    has_child = (core == 1, (section == 7) | (section == 4), section == 7)

    def pass_down(piece):
        for child in (2, 1, 0):
            @pl.when(has_child[child])
            def _():
                gs_copy(child, piece).start()

    far_first = (4, 3, 5, 2, 6, 1, 7)

    @drained(section >= 0)
    def _():
        for by in far_first:
            for half in range(2):
                term_copy(by, half).wait_send()

    @drained(section < 7)
    def _():
        part_copy(section).wait_send()

    for child in range(3):
        @drained(has_child[child])
        def _(child=child):
            for piece in range(4):
                gs_copy(child, piece).wait_send()

    for half in range(2):
        for n in range(2):
            cols = slice(half * 1280 + n * 640, half * 1280 + (n + 1) * 640)
            value = update[:, cols].astype(F32)
            for k in range(CH):
                value += dot(leaving[k], hint[k * CW : (k + 1) * CW, cols])
            update[:, cols] = value.astype(BF16)

        @pl.when(section < 7)
        def _():
            for by in far_first:
                term_copy(by, half).start()

    @pl.when(kept)
    def _():
        base_here().wait()

    @pl.when(lent)
    def _():
        base_across().wait_recv()

    own_rows = rows_of(section, 32)
    row_sum[...] = base_rows[...].astype(F32)
    for by in (1, 2, 3, 4, 5, 6, 7):
        @pl.when(lax.rem(section + 8 - by, 8) < 7)
        def _():
            for half in range(2):
                term_copy(by, half).wait_recv()
            row_sum[...] += slots[by].astype(F32)

    @pl.when(section < 7)
    def _():
        row_sum[...] += update[own_rows, :].astype(F32)
        part_rows[...] = row_sum[...].astype(BF16)
        part_copy(section).start()
        for piece in range(4):
            gs_copy(0, piece).wait_recv()
            pass_down(piece)

    @pl.when(section == 7)
    def _():
        gs[7 * 32 :, :] = row_sum[...].astype(BF16)

        @pl.when(kept)
        def _():
            cot_here().wait()

        @pl.when(lent)
        def _():
            cot_across().wait_recv()

        gain = gain_ref[...]
        for piece in range(4):
            rows = slice(piece * 64, (piece + 1) * 64)
            for owner in (2 * piece, 2 * piece + 1):
                if owner < 7:
                    part_copy(owner).wait_recv()
            summed = gs[rows, :].astype(F32) + update[rows, :].astype(F32)
            inverse = lax.rsqrt(jnp.mean(summed * summed, -1, keepdims=True) + 1e-06)
            grad_normed = cot[rows, :].astype(F32) * gain
            slope = inverse * inverse * inverse * jnp.mean(grad_normed * summed, -1, keepdims=True)
            gs[rows, :] = (inverse * grad_normed - summed * slope).astype(BF16)
            pass_down(piece)
        row_sum[...] += update[7 * 32 :, :].astype(F32)

    def mine_copy(by, kind, owner):
        rows = mine.at[rows_of(owner, 32), :]
        to = {"z": lax.rem(place.z + by, 4), "core": place.xlo}
        return remote(mine_rows, rows, mine_send.at[by], mine_recv.at[by, kind], to)

    def mine_across():
        to = {"xlo": 1 - place.xlo}
        return remote(mine, mine, mine_send.at[4], mine_recv.at[4, 0], to)

    @drained(kept)
    def _():
        for by in (2, 1, 3):
            mine_copy(by, 0, section).wait_send()
        mine_across().wait_send()

    @drained(lent)
    def _():
        for by in (2, 1, 3, 0):
            mine_copy(by, 1, section).wait_send()

    def share_summed():
        @pl.when(section < 7)
        def _():
            last = lax.rem(section + 1, 8)
            for half in range(2):
                cols = slice(half * 1280, (half + 1) * 1280)
                remote(
                    update.at[own_rows, cols], slots.at[last, :, cols],
                    term_send.at[last, half], term_recv.at[last, half], place.sibling,
                ).wait_recv()
            row_sum[...] += slots[last].astype(F32)

        mine_rows[...] = row_sum[...].astype(BF16)

        @pl.when(kept)
        def _():
            mine[own_rows, :] = mine_rows[...]
            for by in (2, 1, 3):
                mine_copy(by, 0, section).start()

        @pl.when(lent)
        def _():
            for by in (2, 1, 3, 0):
                mine_copy(by, 1, section).start()

    def collect_summed():
        @pl.when(kept)
        def _():
            for by in range(4):
                for kind in range(2):
                    if (by, kind) != (0, 0):
                        z = lax.rem(place.z + 4 - by, 4)
                        owner = section_at(z, core if kind == 0 else 1 - core)
                        mine_copy(by, kind, owner).wait_recv()
            mine_across().start()

    hint_gather.wait_sent()
    grad_sum = gs[...]
    for k in range(CH):
        acc[:, k * CW : (k + 1) * CW] = dot(grad_sum, hint[k * CW : (k + 1) * CW, :], ((1,), (1,)))

    red_qkv = Reduce(place, qkv, land_qkv, res_qkv, QKV_CUT, rqkv_send, rqkv_recv)
    red_out = Reduce(place, out, land_out, res_out, OUT_CUT, rout_send, rout_recv)
    red_hint = Reduce(place, hint, land_hint, res_hint, HINT_CUT, rhint_send, rhint_recv)

    mine_keep = pltpu.make_async_copy(mine, mine_out, out_sem.at[3])

    def hint_grads():
        for m in range(CH):
            for n in range(FEAT // 512):
                cols = slice(n * 512, (n + 1) * 512)
                rows = slice(m * CW, (m + 1) * CW)
                hint[rows, cols] = dot(leaving[m], gs[:, cols], ((0,), (0,))).astype(BF16)

    def transposes():
        squares = jnp.zeros((ROWS, 1), F32)
        for k in range(CH):
            wide = landed[k].astype(F32)
            squares += jnp.sum(wide * wide, -1, keepdims=True)
        inverse = lax.rsqrt(squares * (1.0 / WIDTH) + 1e-06)
        for k in range(CH):
            normed = (landed[k].astype(F32) * inverse).astype(BF16)
            normed_t[k * CW : (k + 1) * CW, :] = normed.T
        for k in range(HD // CW):
            att_t[k * CW : (k + 1) * CW, :] = att[:, k * CW : (k + 1) * CW].T

    hint_early = section <= 4

    def let_sibling():
        @pl.when(section == 4)
        def _():
            pl.semaphore_signal(go_sem, inc=1, device_id=place.sibling, device_id_type=MESH)

    @pl.when(hint_early)
    def _():
        hint_grads()

        @pl.when(section == 3)
        def _():
            pl.semaphore_wait(go_sem, 1)

        reduce([red_hint], let_sibling)

    @pl.when(section < 3)
    def _():
        transposes()

    @pl.when(core == 0)
    def _():
        share_summed()

    @pl.when(section < 3)
    def _():
        collect_summed()

    @drained(section > 0)
    def _():
        for k in range(CH):
            back(k).wait_send()

    squares = jnp.zeros((ROWS, 1), F32)
    for k in range(CH):
        wide = landed[k].astype(F32)
        squares += jnp.sum(wide * wide, -1, keepdims=True)
    inverse = lax.rsqrt(squares * (1.0 / WIDTH) + 1e-06)

    def back(k):
        return remote(
            back_leaving.at[k], back_landed.at[k], back_send.at[k], back_recv.at[k], place.earlier
        )

    @pl.when(section == 7)
    def _():
        for k in range(CH):
            back_landed[k] = jnp.zeros((ROWS, CW), BF16)

    grad_att_cols = slice(WIDTH, WIDTH + HD)
    for k in range(CH):
        @pl.when(section < 7)
        def _():
            back(k).wait_recv()

        grad = (back_landed[k].astype(F32) + acc[:, k * CW : (k + 1) * CW]).astype(BF16)
        after[k] = grad
        part = dot(grad, out[:, k * CW : (k + 1) * CW], ((1,), (1,)))
        if k == 0:
            acc[:, grad_att_cols] = part
        else:
            acc[:, grad_att_cols] += part
    through = jnp.zeros((ROWS, 1), F32)
    for h in range(HEADS):
        lo = h * HEAD
        grad_att = acc[:, WIDTH + lo : WIDTH + lo + HEAD].astype(BF16)
        queries = proj[:, lo : lo + HEAD]
        keys = proj[:, HD + lo : HD + lo + HEAD]
        values = proj[:, 2 * HD + lo : 2 * HD + lo + HEAD]
        soft = probs[h]
        grad_probs = dot(grad_att, values, ((1,), (1,)))
        grad_values = dot(soft.astype(BF16), grad_att, ((0,), (0,))).astype(BF16)
        total = jnp.sum(grad_probs * soft, -1, keepdims=True)
        grad_scores = (soft * (grad_probs - total) * SCALE).astype(BF16)
        grad_queries = dot(grad_scores, keys).astype(BF16)
        grad_keys = dot(grad_scores, queries, ((0,), (0,))).astype(BF16)
        for n, (grad, value) in enumerate(
            ((grad_queries, queries), (grad_keys, keys), (grad_values, values))
        ):
            gproj[:, n * HD + lo : n * HD + lo + HEAD] = grad
            through += jnp.sum(grad.astype(F32) * value.astype(F32), -1, keepdims=True)
    slope = inverse * inverse * through * (1.0 / WIDTH)

    @pl.when(section > 0)
    def _():
        grad_proj = gproj[...]
        for k in range(CH):
            grad_normed = dot(grad_proj, qkv[k * CW : (k + 1) * CW, :], ((1,), (1,)))
            value = after[k].astype(F32) + inverse * grad_normed - landed[k].astype(F32) * slope
            back_leaving[k] = value.astype(BF16)
            back(k).start()

    @pl.when(section == 7)
    def _():
        for half in range(2):
            for by in far_first:
                term_copy(by, half).start()

    @pl.when(section >= 3)
    def _():
        transposes()

    @pl.when(core == 1)
    def _():
        share_summed()

    @pl.when((section == 3) | (section == 4))
    def _():
        collect_summed()

    qkv_gather.wait_sent()
    out_gather.wait_sent()
    for m in range(CH):
        rows = slice(m * CW, (m + 1) * CW)
        for n in range(3):
            cols = slice(n * HD, (n + 1) * HD)
            qkv[rows, cols] = dot(normed_t[rows, :], gproj[:, cols]).astype(BF16)
    for m in range(HD // CW):
        rows = slice(m * CW, (m + 1) * CW)
        for n in range(CH):
            out[rows, n * CW : (n + 1) * CW] = dot(att_t[rows, :], after[n]).astype(BF16)
    @pl.when(hint_early)
    def _():
        reduce([red_qkv, red_out])

    @pl.when(jnp.logical_not(hint_early))
    def _():
        hint_grads()
        reduce([red_qkv, red_out, red_hint])

    @pl.when(section >= 5)
    def _():
        collect_summed()

    @pl.when(lent)
    def _():
        mine_across().wait_recv()

    mine_keep.start()
    keeps = [
        red.put(ref, out_sem.at[i])
        for i, (red, ref) in enumerate(((red_qkv, sum_qkv), (red_out, sum_out), (red_hint, sum_hint)))
    ]
    for red in (red_qkv, red_out, red_hint):
        red.wait_sent()
    mine_keep.wait()
    for keep in keeps:
        keep()
    for drain in drains:
        drain()


def scale_kernel(
    mine_ref, gain_ref, qkv_ref, out_ref, hint_ref, features_out, qkv_out, out_out, hint_out,
    mine, qkv, out, hint, features, grad_qkv, grad_out, grad_hint, in_sem, out_sem,
):
    ins = ((mine_ref, mine), (qkv_ref, qkv), (out_ref, out), (hint_ref, hint))
    outs = (
        (features, features_out), (grad_qkv, qkv_out), (grad_out, out_out), (grad_hint, hint_out)
    )
    reads = [pltpu.make_async_copy(*pair, in_sem.at[i]) for i, pair in enumerate(ins)]
    writes = [pltpu.make_async_copy(*pair, out_sem.at[i]) for i, pair in enumerate(outs)]
    for read in reads:
        read.start()
    gain = gain_ref[...]
    for i in range(4):
        reads[i].wait()
        if i == 0:
            wide = mine[...].astype(F32)
            inverse = lax.rsqrt(jnp.mean(wide * wide, -1, keepdims=True) + 1e-06)
            features[...] = wide * inverse * gain
        else:
            outs[i][0][...] = ins[i][1][...].astype(F32) * 4096.0 ** (-0.5)
        writes[i].start()
    for write in writes:
        write.wait()


def dma_sems(*shape):
    return pltpu.SemaphoreType.DMA(shape)


def kernel_call(kernel, ins, outs, scratch, collective_id, flops):
    spaces = {"v": pltpu.VMEM, "a": pl.ANY, "s": pltpu.SMEM}
    return pl.pallas_call(
        kernel,
        out_shape=[shape for shape, _ in outs],
        in_specs=[pl.BlockSpec(memory_space=spaces[kind]) for kind in ins],
        out_specs=[pl.BlockSpec(memory_space=spaces[kind]) for _, kind in outs],
        scratch_shapes=scratch,
        compiler_params=pltpu.CompilerParams(
            collective_id=collective_id, has_side_effects=True, vmem_limit_bytes=VMEM_LIMIT
        ),
        cost_estimate=pl.CostEstimate(flops=flops, bytes_accessed=12_000_000, transcendentals=0),
    )


def tile_members(layout):
    tokens = lax.broadcasted_iota(jnp.int32, (ROWS, ROWS), 0)
    positions = lax.broadcasted_iota(jnp.int32, (ROWS, ROWS), 1)
    tiles = jnp.where(layout == tokens, (positions // TILE).astype(F32), 0.0)
    tile_of = jnp.sum(tiles, -1, keepdims=True)
    columns = lax.broadcasted_iota(jnp.int32, (ROWS, 128), 1).astype(F32)
    return jnp.where(tile_of == columns, 1.0, 0.0).astype(BF16)


def permitted_tiles(offset, mask):
    row = lax.broadcasted_iota(jnp.int32, (128, 128), 0)
    col = lax.broadcasted_iota(jnp.int32, (128, 128), 1)
    found = jnp.where(row == col, 1, 0)
    for i in range(4):
        for j in range(4):
            if i != j:
                near = jnp.abs(j - i - offset[0, i]) <= 1
                value = jnp.where(near & (mask[0, i, j] == 1), 1, 0)
                found = jnp.where((row == i) & (col == j), value, found)
    return found.astype(F32).astype(BF16)


def shape_of(*dims, dtype=BF16):
    return jax.ShapeDtypeStruct(dims, dtype)


def shards(
    control_in, base_in, base_update, out_gain, cotangent,
    w_qkv, w_out, w_hint, window_offset, tile_mask, token_layout,
):
    chunks = (CH, ROWS, CW)
    gain = out_gain[None]
    mine, sum_qkv, sum_out, sum_hint = kernel_call(
        section_kernel,
        "avssaaaaaav",
        [
            (shape_of(ROWS, FEAT), "a"),
            (shape_of(96, QKV), "a"),
            (shape_of(48, WIDTH), "a"),
            (shape_of(96, FEAT), "a"),
        ],
        [
            *[pltpu.VMEM(chunks, BF16)] * 5,
            pltpu.VMEM((ROWS, QKV), F32),
            pltpu.VMEM((ROWS, QKV), BF16),
            pltpu.VMEM((ROWS, HD), BF16),
            pltpu.VMEM((ROWS, QKV), BF16),
            pltpu.VMEM((HEADS, ROWS, ROWS), F32),
            pltpu.VMEM((ROWS, ROWS), F32),
            *[pltpu.VMEM((ROWS, 128), BF16), pltpu.VMEM((128, 128), BF16)] * 2,
            pltpu.VMEM((WIDTH, QKV), BF16),
            pltpu.VMEM((HD, WIDTH), BF16),
            pltpu.VMEM((WIDTH, FEAT), BF16),
            pltpu.VMEM((WIDTH, ROWS), BF16),
            pltpu.VMEM((HD, ROWS), BF16),
            pltpu.VMEM((ROWS, FEAT), BF16),
            pltpu.VMEM((8, 32, FEAT), BF16),
            pltpu.VMEM((ROWS, FEAT), BF16),
            pltpu.VMEM((ROWS, FEAT), BF16),
            *[pltpu.VMEM((32, FEAT), BF16)] * 3,
            pltpu.VMEM((32, FEAT), F32),
            pltpu.VMEM((ROWS, FEAT), BF16),
            pltpu.VMEM((2, 15, 96, QKV // 2), BF16),
            pltpu.VMEM((2, 15, 48, WIDTH // 2), BF16),
            pltpu.VMEM((2, 15, 96, FEAT // 2), BF16),
            pltpu.VMEM((96, QKV), BF16),
            pltpu.VMEM((48, WIDTH), BF16),
            pltpu.VMEM((96, FEAT), BF16),
            *[dma_sems(CH)] * 4,
            dma_sems(5), dma_sems(5), dma_sems(CH), dma_sems(3), dma_sems(4),
            *[dma_sems(2, 21), dma_sems(2, 21), dma_sems(2)] * 3,
            *[dma_sems(2, 21)] * 6,
            dma_sems(8, 2), dma_sems(8, 2), dma_sems(1), dma_sems(7), dma_sems(3, 4), dma_sems(4),
            dma_sems(5), dma_sems(5, 2),
            pltpu.SemaphoreType.REGULAR,
        ],
        1,
        100_000_000_000,
    )(
        control_in, token_layout, window_offset, tile_mask, w_qkv[0], w_out[0], w_hint[0],
        base_in, cotangent, base_update[0], gain,
    )
    features, grad_qkv, grad_out, grad_hint = pl.pallas_call(
        scale_kernel,
        out_shape=[
            shape_of(ROWS, FEAT, dtype=F32),
            shape_of(96, QKV, dtype=F32),
            shape_of(48, WIDTH, dtype=F32),
            shape_of(96, FEAT, dtype=F32),
        ],
        in_specs=[
            pl.BlockSpec(memory_space=pltpu.VMEM if i == 1 else pl.ANY) for i in range(5)
        ],
        out_specs=[pl.BlockSpec(memory_space=pl.ANY)] * 4,
        scratch_shapes=[
            pltpu.VMEM(dims, dtype)
            for dtype in (BF16, F32)
            for dims in ((ROWS, FEAT), (96, QKV), (48, WIDTH), (96, FEAT))
        ]
        + [dma_sems(4), dma_sems(4)],
        compiler_params=pltpu.CompilerParams(vmem_limit_bytes=VMEM_LIMIT),
    )(mine, gain, sum_qkv, sum_out, sum_hint)
    return features, grad_qkv[None], grad_out[None], grad_hint[None]


def solution(mesh):
    parts = jax.sharding.Mesh(
        mesh.devices.reshape(2, 4, 2, 4, 2), ("xlo", "z", "xhi", "y", "core")
    )
    segment = ("xlo", "z")
    dp = ("xhi", "y", "core")
    by_rows = P(dp, None)
    by_both = P(segment, dp, None)
    placed = (
        by_rows, by_rows, by_both, P(), by_rows, by_both, by_both, by_both,
        P(segment, None), P(segment, None, None), by_rows,
    )
    return jax.shard_map(
        shards,
        mesh=parts,
        in_specs=placed,
        out_specs=(by_rows, by_both, by_both, by_both),
        check_vma=False,
    )
```
